32 devices in a mesh: parts: 2 (over x), seq: 16 (over z, y, core).
Axes of the slice: x: 2, y: 2, z: 4, core: 2. Of those that a mesh axis runs over, the one named last changes fastest.
Arguments:
- fresh_qkv: bfloat16 [2432, 3, 2048], P(('parts', 'seq')), parts along dimension 0, may hold values from -6 to 6
- slot_rows: int32 [2432], P(('parts', 'seq')), parts along dimension 0, may hold values from 0 to 128, as said below
- k_cache: bfloat16 [4096, 2048], P(('parts', 'seq')), parts along dimension 0, may hold values from -6 to 6
- v_cache: bfloat16 [4096, 2048], P(('parts', 'seq')), parts along dimension 0, may hold values from -6 to 6
- attn_cache: bfloat16 [4096, 2048], P(('parts', 'seq')), parts along dimension 0, may hold values from -6 to 6
- text_k: bfloat16 [512, 2048], P('parts'), parts along dimension 0, may hold values from -6 to 6
- text_v: bfloat16 [512, 2048], P('parts'), parts along dimension 0, may hold values from -6 to 6
- q_gain: float32 [128], replicated, may hold values from 1 to 2.2
- k_gain: float32 [128], replicated, may hold values from 1 to 2.2
Outputs:
- attn_out: bfloat16 [4096, 2048], P(('parts', 'seq')), parts along dimension 0
The draws below stay inside these ranges and needn't reach their ends.
There are 2 independent parts, one for each index of `parts`. The reference program is written for one: setup_inputs(seed, part) draws one part's arguments, and reference() takes and returns one part's arrays. A program takes and returns all parts, laid end to end along the dimension named above; an argument that names none is the same for every part. Nothing has to cross between parts.
Inputs may be any that keep to these rules, and one draw needn't show every extreme that they name: `slot_rows`: entries s * 76 to s * 76 + 75 belong to sequence shard s: the local indices of that shard's fresh tokens in increasing order, then 128 in every slot left empty. A shard holds at most 76 fresh tokens and some shard exactly 76; the shards of a sample hold exactly 608 fresh tokens together.
All inputs are finite; a program needn't handle non-finite values.
Results may differ from the reference program's by a relative error of at most 0.0025.
Values may be sent and summed in bfloat16 or wider, within the bound.
No kernel may reach another device: no remote copies, remote signals or barrier semaphores. Data moves between devices by JAX's collectives and lax.ppermute only.
A program may use at most 64 MiB of HBM per device.

```python
import math
import jax
import jax.numpy as jnp
from jax import lax

HEADS = 16
HD = 128
TOK_DEV = 128
TEXT = 256
FRESH_DEV = 38
CAP = 76
TOKENS = 2048
SLOTS = 1216
N_SEQ = 16


def draw_slot_rows(key, part):
    key = jax.random.fold_in(key, 7)
    halves = N_SEQ // 2
    offsets = jax.random.randint(jax.random.fold_in(key, 1), (halves,), 0, FRESH_DEV + 1)
    offsets = offsets.at[0].set(FRESH_DEV)
    fresh_counts = jnp.concatenate([FRESH_DEV + offsets, FRESH_DEV - offsets])
    fresh_counts = fresh_counts[jax.random.permutation(jax.random.fold_in(key, 2), N_SEQ)]
    shard_key = jax.random.fold_in(key, 3)

    def one_shard(shard_id, fresh_count):
        shuffled = jax.random.permutation(jax.random.fold_in(shard_key, shard_id), TOK_DEV)[:CAP]
        chosen = jnp.where(jnp.arange(CAP, dtype=jnp.int32) < fresh_count, shuffled, TOK_DEV)
        return jnp.sort(chosen)
    rows_all = jax.vmap(one_shard)(jnp.arange(N_SEQ, dtype=jnp.int32), fresh_counts)
    return rows_all.reshape(N_SEQ * CAP).astype(jnp.int32)


def level_of(own_key, extent, shards, low, high):
    loudness = 1.0
    for dim, shards_of in shards:
        heights = jax.random.uniform(jax.random.fold_in(jax.random.fold_in(own_key, 6), dim), (shards_of,), jnp.float32, low / len(shards), high / len(shards))
        loudness = loudness * jnp.repeat(jnp.exp(heights), extent[dim] // shards_of).reshape((-1,) + (1,) * (len(extent) - 1 - dim))
    return loudness


def noise(rng, shape, scale, limit, split=(), held_as=jnp.bfloat16):
    values = jax.random.normal(rng, shape, jnp.float32) * scale
    if len(split) > 0:
        values = level_of(rng, shape, split, -0.22, 0.18) * values
    return jnp.clip(values, min=-limit, max=limit).astype(held_as)


def setup_inputs(seed: int = 0, part: int = 0) -> dict:
    arg_keys = jax.random.split(jax.random.key(seed), 10)
    own_keys = jax.random.split(jax.random.fold_in(arg_keys[9], part), 10)
    return {
        "fresh_qkv": noise(own_keys[0], (SLOTS, 3, HEADS * HD), 1.0, 6.0, ((0, 16),)),
        "slot_rows": draw_slot_rows(jax.random.fold_in(jax.random.fold_in(arg_keys[9], part), 71), part),
        "k_cache": noise(own_keys[2], (TOKENS, HEADS * HD), 1.0, 6.0, ((0, 16),)),
        "v_cache": noise(own_keys[3], (TOKENS, HEADS * HD), 1.0, 6.0, ((0, 16),)),
        "attn_cache": noise(own_keys[4], (TOKENS, HEADS * HD), 1.0, 6.0, ((0, 16),)),
        "text_k": noise(own_keys[5], (TEXT, HEADS * HD), 1.0, 6.0),
        "text_v": noise(own_keys[6], (TEXT, HEADS * HD), 1.0, 6.0),
        "q_gain": jnp.clip(jnp.exp(jax.random.uniform(arg_keys[7], (HD,), jnp.float32, math.log(1.0), math.log(2.2))), 1.0, 2.2),
        "k_gain": jnp.clip(jnp.exp(jax.random.uniform(arg_keys[8], (HD,), jnp.float32, math.log(1.0), math.log(2.2))), 1.0, 2.2),
    }


def normalize(entries, scales):
    mean_square = lax.optimization_barrier(jnp.mean(entries * entries, axis=-1, keepdims=True))
    return entries * lax.rsqrt(mean_square + 1e-06) * scales

def one_head(operands):
    head_queries, head_keys, head_values = operands
    scores = jnp.dot(head_queries, head_keys.T, preferred_element_type=jnp.float32) * HD ** (-0.5)
    expd = jnp.exp(scores)
    denominator = lax.optimization_barrier(jnp.sum(expd, axis=1))
    numerator = jnp.dot(expd.astype(jnp.bfloat16), head_values, preferred_element_type=jnp.float32)
    return (numerator / denominator[:, None]).astype(jnp.bfloat16)

def reference(fresh_qkv, slot_rows, k_cache, v_cache, attn_cache, text_k, text_v, q_gain, k_gain):
    row_width = HEADS * HD
    shard_ids = jnp.repeat(jnp.arange(N_SEQ, dtype=jnp.int32), CAP)
    target = jnp.where(slot_rows < TOK_DEV, shard_ids * TOK_DEV + slot_rows, TOKENS).astype(jnp.int32)
    raw_queries = fresh_qkv[:, 0].astype(jnp.float32).reshape(SLOTS, HEADS, HD)
    queries = normalize(raw_queries, q_gain).astype(jnp.bfloat16)
    keys_raw = k_cache.at[target].set(fresh_qkv[:, 1], mode='drop')
    values = v_cache.at[target].set(fresh_qkv[:, 2], mode='drop')
    keys = normalize(keys_raw.astype(jnp.float32).reshape(TOKENS, HEADS, HD), k_gain).astype(jnp.bfloat16)
    text_keys = normalize(text_k.astype(jnp.float32).reshape(TEXT, HEADS, HD), k_gain).astype(jnp.bfloat16)
    all_keys = jnp.concatenate([keys, text_keys], axis=0)
    all_values = jnp.concatenate([values.reshape(TOKENS, HEADS, HD), text_v.reshape(TEXT, HEADS, HD)], axis=0)
    head_outs = lax.map(one_head, (jnp.transpose(queries, (1, 0, 2)), jnp.transpose(all_keys, (1, 0, 2)), jnp.transpose(all_values, (1, 0, 2))))
    slot_out = jnp.transpose(head_outs, (1, 0, 2)).reshape(SLOTS, row_width)
    return attn_cache.at[target].set(slot_out, mode='drop')
```

```python
import math

import jax
import jax.numpy as jnp
from jax import lax
from jax.experimental import pallas as pl
from jax.experimental.pallas import tpu as pltpu
from jax.sharding import PartitionSpec as P

LOG2E = math.log2(math.e)


def round_up(count, step):
    return (count + step - 1) // step * step


def normalize(entries, scales):
    mean_square = jnp.mean(entries * entries, axis=-1, keepdims=True)
    return entries * lax.rsqrt(mean_square + 1e-06) * scales


def place(slots, tokens):
    owner = lax.broadcasted_iota(jnp.int32, (tokens, slots.shape[1]), 0)
    return owner == slots


def prepare_kernel(
    per_group, padded, slots_ref, qkv_ref, k_ref, v_ref, q_gain_ref, k_gain_ref, out_ref
):
    tokens = k_ref.shape[0]
    head_size = q_gain_ref.shape[1]
    groups = qkv_ref.shape[1] // per_group
    heads = k_ref.shape[1] // head_size
    mine = place(slots_ref[...], tokens)
    is_fresh = jnp.max(mine.astype(jnp.float32), axis=1, keepdims=True) > 0.5
    one_hot = mine.astype(jnp.bfloat16)
    q_gain = q_gain_ref[...]
    k_gain = k_gain_ref[...]

    def merged(part, cache_ref):
        spread = jnp.dot(one_hot, qkv_ref[part], preferred_element_type=jnp.float32)
        return jnp.where(is_fresh, spread, cache_ref[...].astype(jnp.float32))

    keys_raw = merged(1, k_ref)
    values = merged(2, v_ref).astype(jnp.bfloat16)
    raw_queries = qkv_ref[0].astype(jnp.float32)
    for head in range(heads):
        columns = slice(head * head_size, (head + 1) * head_size)
        keys = normalize(keys_raw[:, columns], k_gain).astype(jnp.bfloat16)
        queries = normalize(raw_queries[:, columns], q_gain)
        for group in range(groups):
            at = head * groups + group
            out_ref[at, :tokens] = keys
            out_ref[at, tokens : 2 * tokens] = values[:, columns]
            share = queries[group * per_group : (group + 1) * per_group]
            if padded > per_group:
                empty = jnp.zeros((padded - per_group, head_size), jnp.float32)
                share = jnp.concatenate([share, empty], axis=0)
            out_ref[at, 2 * tokens :] = share.astype(jnp.bfloat16)


def attend_kernel(
    tokens,
    query_sources,
    key_sources,
    head_ref,
    arrived_ref,
    text_k_ref,
    text_v_ref,
    k_gain_ref,
    out_ref,
    text_keys,
    weights,
):
    del head_ref
    sources, rows, head_size = arrived_ref.shape
    padded = rows - 2 * tokens
    factor = head_size ** (-0.5) * LOG2E
    text_keys[...] = normalize(text_k_ref[...].astype(jnp.float32), k_gain_ref[...]).astype(
        jnp.bfloat16
    )
    text = text_keys.shape[0]
    query_rows = query_sources * padded
    key_rows = key_sources * tokens

    def keys_of(turn):
        if turn == 0:
            return text_keys[...]
        first = (turn - 1) * key_sources
        return arrived_ref[first : first + key_sources, :tokens].reshape(key_rows, head_size)

    def values_of(turn):
        if turn == 0:
            rows_of = text_v_ref[...]
        else:
            first = (turn - 1) * key_sources
            rows_of = arrived_ref[first : first + key_sources, tokens : 2 * tokens].reshape(
                key_rows, head_size
            )
        return jnp.concatenate([rows_of, jnp.ones_like(rows_of)], axis=1)

    turns = 1 + sources // key_sources

    def columns_of(turn):
        if turn == 0:
            return slice(0, text)
        return slice(text + (turn - 1) * key_rows, text + turn * key_rows)

    def add_queries(step, carry):
        first = step * query_sources
        queries = arrived_ref[pl.ds(first, query_sources), 2 * tokens :].reshape(
            query_rows, head_size
        )
        for turn in range(turns):
            scores = lax.dot_general(
                queries,
                keys_of(turn),
                (((1,), (1,)), ((), ())),
                preferred_element_type=jnp.float32,
            )
            weights[:, columns_of(turn)] = jnp.exp2(scores * factor).astype(jnp.bfloat16)
        sums = jnp.zeros((query_rows, 2 * head_size), jnp.float32)
        for turn in range(turns):
            sums = sums + jnp.dot(
                weights[:, columns_of(turn)],
                values_of(turn),
                preferred_element_type=jnp.float32,
            )
        result = (sums[:, :head_size] / sums[:, head_size:]).astype(jnp.bfloat16)
        out_ref[pl.ds(first, query_sources)] = result.reshape(query_sources, padded, head_size)
        return carry

    lax.fori_loop(0, sources // query_sources, add_queries, 0)


def finish_kernel(per_group, slots_ref, returned_ref, cache_ref, out_ref):
    tokens = cache_ref.shape[0]
    head_size = returned_ref.shape[2]
    groups = slots_ref.shape[0]
    heads = cache_ref.shape[1] // head_size
    mine = [place(slots_ref[group : group + 1], tokens) for group in range(groups)]
    count = sum(jnp.sum(m.astype(jnp.float32), axis=1, keepdims=True) for m in mine)
    is_fresh = count > 0.5
    one_hot = [m.astype(jnp.bfloat16) for m in mine]
    for head in range(heads):
        columns = slice(head * head_size, (head + 1) * head_size)
        placed = sum(
            jnp.dot(
                one_hot[group],
                returned_ref[head * groups + group],
                preferred_element_type=jnp.float32,
            )
            for group in range(groups)
        )
        out_ref[:, columns] = jnp.where(
            is_fresh, placed, cache_ref[:, columns].astype(jnp.float32)
        ).astype(out_ref.dtype)


def shards(fresh_qkv, slot_rows, k_cache, v_cache, attn_cache, text_k, text_v, q_gain, k_gain):
    seq_count = lax.axis_size("seq")
    my_index = lax.axis_index("seq")
    slot_count = slot_rows.shape[0]
    tokens, row_width = k_cache.shape
    text = text_k.shape[0]
    head_size = q_gain.shape[0]
    head_count = row_width // head_size
    groups = seq_count // head_count
    per_group = slot_count // groups
    padded = round_up(per_group, 16)
    rows = 2 * tokens + padded
    my_head = my_index // groups
    q_gain = q_gain.reshape(1, head_size)
    k_gain = k_gain.reshape(1, head_size)
    qkv = jnp.transpose(fresh_qkv, (1, 0, 2))
    slots = slot_rows.reshape(1, slot_count)
    padded_slots = jnp.pad(
        slot_rows.reshape(groups, per_group),
        ((0, 0), (0, padded - per_group)),
        constant_values=tokens,
    )

    steps = 4
    width = row_width // steps
    step_heads = head_count // steps
    outgoing = pl.pallas_call(
        lambda *refs: prepare_kernel(per_group, padded, *refs),
        out_shape=jax.ShapeDtypeStruct((seq_count, rows, head_size), jnp.bfloat16),
        grid=(steps,),
        in_specs=[
            pl.BlockSpec((1, slot_count), lambda i: (0, 0)),
            pl.BlockSpec((3, slot_count, width), lambda i: (0, 0, i)),
            pl.BlockSpec((tokens, width), lambda i: (0, i)),
            pl.BlockSpec((tokens, width), lambda i: (0, i)),
            pl.BlockSpec((1, head_size), lambda i: (0, 0)),
            pl.BlockSpec((1, head_size), lambda i: (0, 0)),
        ],
        out_specs=pl.BlockSpec((step_heads * groups, rows, head_size), lambda i: (i, 0, 0)),
        compiler_params=pltpu.CompilerParams(vmem_limit_bytes=32 * 2**20),
        name="prepare",
    )(slots, qkv, k_cache, v_cache, q_gain, k_gain)

    arrived = lax.all_to_all(outgoing, "seq", split_axis=0, concat_axis=0, tiled=True)

    query_sources = 4
    result = pl.pallas_call(
        lambda *refs: attend_kernel(tokens, query_sources, 4, *refs),
        out_shape=jax.ShapeDtypeStruct((seq_count, padded, head_size), jnp.bfloat16),
        grid_spec=pltpu.PrefetchScalarGridSpec(
            num_scalar_prefetch=1,
            grid=(1,),
            in_specs=[
                pl.BlockSpec((seq_count, rows, head_size), lambda i, head: (0, 0, 0)),
                pl.BlockSpec((text, head_size), lambda i, head: (0, head[0])),
                pl.BlockSpec((text, head_size), lambda i, head: (0, head[0])),
                pl.BlockSpec((1, head_size), lambda i, head: (0, 0)),
            ],
            out_specs=pl.BlockSpec((seq_count, padded, head_size), lambda i, head: (0, 0, 0)),
            scratch_shapes=[
                pltpu.VMEM((text, head_size), jnp.bfloat16),
                pltpu.VMEM((query_sources * padded, text + seq_count * tokens), jnp.bfloat16),
            ],
        ),
        compiler_params=pltpu.CompilerParams(vmem_limit_bytes=40 * 2**20),
        name="attend",
    )(my_head.reshape(1), arrived, text_k, text_v, k_gain)

    returned = lax.all_to_all(result, "seq", split_axis=0, concat_axis=0, tiled=True)

    return pl.pallas_call(
        lambda *refs: finish_kernel(per_group, *refs),
        out_shape=jax.ShapeDtypeStruct((tokens, row_width), attn_cache.dtype),
        grid=(steps,),
        in_specs=[
            pl.BlockSpec((groups, padded), lambda i: (0, 0)),
            pl.BlockSpec((step_heads * groups, padded, head_size), lambda i: (i, 0, 0)),
            pl.BlockSpec((tokens, width), lambda i: (0, i)),
        ],
        out_specs=pl.BlockSpec((tokens, width), lambda i: (0, i)),
        compiler_params=pltpu.CompilerParams(vmem_limit_bytes=32 * 2**20),
        name="finish",
    )(padded_slots, returned, attn_cache)


def solution(mesh):
    return jax.shard_map(
        shards,
        mesh=mesh,
        in_specs=(
            P(("parts", "seq"), None, None),
            P(("parts", "seq")),
            P(("parts", "seq"), None),
            P(("parts", "seq"), None),
            P(("parts", "seq"), None),
            P("parts", None),
            P("parts", None),
            P(),
            P(),
        ),
        out_specs=P(("parts", "seq"), None),
        check_vma=False,
    )
```

```python
import math

import jax
import jax.numpy as jnp
from jax import lax
from jax.experimental import pallas as pl
from jax.experimental.pallas import tpu as pltpu
from jax.sharding import PartitionSpec as P

LOG2E = math.log2(math.e)


def round_up(count, step):
    return (count + step - 1) // step * step


def normalize(entries, scales):
    mean_square = jnp.mean(entries * entries, axis=-1, keepdims=True)
    return entries * lax.rsqrt(mean_square + 1e-06) * scales


def place(slots, tokens):
    owner = lax.broadcasted_iota(jnp.int32, (tokens, slots.shape[1]), 0)
    return owner == slots


def prepare_kernel(
    per_group, padded, me_ref, slots_ref, qkv_ref, k_ref, v_ref, q_gain_ref, k_gain_ref, *rest
):
    outs, queries_ref = rest[:-1], rest[-1]
    tokens = k_ref.shape[0]
    head_size = q_gain_ref.shape[1]
    groups = qkv_ref.shape[1] // per_group
    mine = place(slots_ref[...], tokens)
    is_fresh = jnp.max(mine.astype(jnp.float32), axis=1, keepdims=True) > 0.5
    one_hot = mine.astype(jnp.bfloat16)
    q_gain = q_gain_ref[...]
    k_gain = k_gain_ref[...]
    me = me_ref[0]

    for high in range(len(outs) // groups):
        head = lax.bitwise_xor(me // groups, high)
        columns = pl.ds(pl.multiple_of(head * head_size, head_size), head_size)

        def merged(part, cache_ref):
            spread = jnp.dot(
                one_hot, qkv_ref[part, :, columns], preferred_element_type=jnp.float32
            )
            return jnp.where(is_fresh, spread, cache_ref[:, columns].astype(jnp.float32))

        keys = normalize(merged(1, k_ref), k_gain).astype(jnp.bfloat16)
        values = merged(2, v_ref).astype(jnp.bfloat16)
        queries = normalize(qkv_ref[0, :, columns].astype(jnp.float32), q_gain)
        empty = jnp.zeros((padded - per_group, head_size), jnp.float32)
        for group in range(groups):
            share = queries[group * per_group : (group + 1) * per_group]
            if padded > per_group:
                share = jnp.concatenate([share, empty], axis=0)
            queries_ref[group] = share.astype(jnp.bfloat16)
        for low in range(groups):
            out_ref = outs[high * groups + low]
            group = lax.bitwise_xor(me % groups, low)
            out_ref[:tokens] = keys
            out_ref[tokens : 2 * tokens] = values
            out_ref[2 * tokens :] = queries_ref[group]


def attend_kernel(tokens, query_rows, key_rows, count, me_ref, *rest):
    del me_ref
    arrived = rest[:count]
    text_k_ref, text_v_ref, k_gain_ref = rest[count : count + 3]
    outs = rest[count + 3 : 2 * count + 3]
    queries_ref, keys_ref, values_ref, weights_ref, result_ref = rest[2 * count + 3 :]
    head_size = text_k_ref.shape[1]
    padded = arrived[0].shape[0] - 2 * tokens
    factor = head_size ** (-0.5) * LOG2E
    text = text_k_ref.shape[0]
    text_keys = normalize(text_k_ref[...].astype(jnp.float32), k_gain_ref[...])
    keys_ref[:text] = text_keys.astype(jnp.bfloat16)
    values_ref[:text, :head_size] = text_v_ref[...]
    values_ref[:, head_size:] = jnp.ones((values_ref.shape[0], head_size), jnp.bfloat16)
    for step in range(count):
        first = text + step * tokens
        keys_ref[first : first + tokens] = arrived[step][:tokens]
        values_ref[first : first + tokens, :head_size] = arrived[step][tokens : 2 * tokens]
        queries_ref[step * padded : (step + 1) * padded] = arrived[step][2 * tokens :]

    def add_queries(step, carry):
        mine = pl.ds(pl.multiple_of(step * query_rows, 16), query_rows)
        queries = queries_ref[mine]
        for first in range(0, keys_ref.shape[0], key_rows):
            scores = lax.dot_general(
                queries,
                keys_ref[first : first + key_rows],
                (((1,), (1,)), ((), ())),
                preferred_element_type=jnp.float32,
            )
            weights_ref[:, first : first + key_rows] = jnp.exp2(scores * factor).astype(
                jnp.bfloat16
            )
        sums = jnp.dot(weights_ref[...], values_ref[...], preferred_element_type=jnp.float32)
        result_ref[mine] = (sums[:, :head_size] / sums[:, head_size:]).astype(jnp.bfloat16)
        return carry

    lax.fori_loop(0, queries_ref.shape[0] // query_rows, add_queries, 0)
    for step in range(count):
        outs[step][...] = result_ref[step * padded : (step + 1) * padded]


def finish_kernel(count, me_ref, slots_ref, cache_ref, *rest):
    returned, out_ref = rest[:count], rest[count]
    tokens = cache_ref.shape[0]
    head_size = returned[0].shape[1]
    groups = slots_ref.shape[0]
    me = me_ref[0]
    one_hot = []
    owned = jnp.zeros((tokens, 1), jnp.float32)
    for low in range(groups):
        group = lax.bitwise_xor(me % groups, low)
        mine = place(slots_ref[pl.ds(group, 1)], tokens).astype(jnp.float32)
        owned = owned + jnp.sum(mine, axis=1, keepdims=True)
        one_hot.append(mine.astype(jnp.bfloat16))
    is_fresh = owned > 0.5
    for high in range(count // groups):
        head = lax.bitwise_xor(me // groups, high)
        columns = pl.ds(pl.multiple_of(head * head_size, head_size), head_size)
        placed = jnp.zeros((tokens, head_size), jnp.float32)
        for low in range(groups):
            placed = placed + jnp.dot(
                one_hot[low], returned[high * groups + low][...], preferred_element_type=jnp.float32
            )
        out_ref[:, columns] = jnp.where(
            is_fresh, placed, cache_ref[:, columns].astype(jnp.float32)
        ).astype(out_ref.dtype)


def whole(shape):
    return pl.BlockSpec(shape, lambda i, me: (0,) * len(shape))


def exchange(blocks):
    count = len(blocks)
    arrived = list(blocks)
    for step in reversed(range(1, count)):
        arrived[step] = lax.ppermute(blocks[step], "seq", [(a, a ^ step) for a in range(count)])
    return arrived


def shards(fresh_qkv, slot_rows, k_cache, v_cache, attn_cache, text_k, text_v, q_gain, k_gain):
    seq_count = lax.axis_size("seq")
    me = lax.axis_index("seq").reshape(1)
    slot_count = slot_rows.shape[0]
    tokens, row_width = k_cache.shape
    text = text_k.shape[0]
    head_size = q_gain.shape[0]
    head_count = row_width // head_size
    groups = seq_count // head_count
    per_group = slot_count // groups
    padded = round_up(per_group, 16)
    rows = 2 * tokens + padded
    q_gain = q_gain.reshape(1, head_size)
    k_gain = k_gain.reshape(1, head_size)
    qkv = jnp.transpose(fresh_qkv, (1, 0, 2))
    slots = slot_rows.reshape(1, slot_count)
    padded_slots = jnp.pad(
        slot_rows.reshape(groups, per_group),
        ((0, 0), (0, padded - per_group)),
        constant_values=tokens,
    )

    outgoing = pl.pallas_call(
        lambda *refs: prepare_kernel(per_group, padded, *refs),
        out_shape=[jax.ShapeDtypeStruct((rows, head_size), jnp.bfloat16)] * seq_count,
        grid_spec=pltpu.PrefetchScalarGridSpec(
            num_scalar_prefetch=1,
            grid=(1,),
            in_specs=[
                whole((1, slot_count)),
                whole((3, slot_count, row_width)),
                whole((tokens, row_width)),
                whole((tokens, row_width)),
                whole((1, head_size)),
                whole((1, head_size)),
            ],
            out_specs=[whole((rows, head_size))] * seq_count,
            scratch_shapes=[pltpu.VMEM((groups, padded, head_size), jnp.bfloat16)],
        ),
        name="prepare",
    )(me, slots, qkv, k_cache, v_cache, q_gain, k_gain)

    arrived = exchange(outgoing)

    query_rows = 4 * padded
    all_keys = text + seq_count * tokens
    result = pl.pallas_call(
        lambda *refs: attend_kernel(tokens, query_rows, 256, seq_count, *refs),
        out_shape=[jax.ShapeDtypeStruct((padded, head_size), jnp.bfloat16)] * seq_count,
        grid_spec=pltpu.PrefetchScalarGridSpec(
            num_scalar_prefetch=1,
            grid=(1,),
            in_specs=[whole((rows, head_size))] * seq_count
            + [pl.BlockSpec((text, head_size), lambda i, me: (0, me[0] // groups))] * 2
            + [whole((1, head_size))],
            out_specs=[whole((padded, head_size))] * seq_count,
            scratch_shapes=[
                pltpu.VMEM((seq_count * padded, head_size), jnp.bfloat16),
                pltpu.VMEM((all_keys, head_size), jnp.bfloat16),
                pltpu.VMEM((all_keys, 2 * head_size), jnp.bfloat16),
                pltpu.VMEM((query_rows, all_keys), jnp.bfloat16),
                pltpu.VMEM((seq_count * padded, head_size), jnp.bfloat16),
            ],
        ),
        compiler_params=pltpu.CompilerParams(vmem_limit_bytes=40 * 2**20),
        name="attend",
    )(me, *arrived, text_k, text_v, k_gain)

    returned = exchange(result)

    return pl.pallas_call(
        lambda *refs: finish_kernel(seq_count, *refs),
        out_shape=jax.ShapeDtypeStruct((tokens, row_width), attn_cache.dtype),
        grid_spec=pltpu.PrefetchScalarGridSpec(
            num_scalar_prefetch=1,
            grid=(1,),
            in_specs=[whole((groups, padded)), whole((tokens, row_width))]
            + [whole((padded, head_size))] * seq_count,
            out_specs=whole((tokens, row_width)),
        ),
        compiler_params=pltpu.CompilerParams(vmem_limit_bytes=32 * 2**20),
        name="finish",
    )(me, padded_slots, attn_cache, *returned)


def solution(mesh):
    return jax.shard_map(
        shards,
        mesh=mesh,
        in_specs=(
            P(("parts", "seq"), None, None),
            P(("parts", "seq")),
            P(("parts", "seq"), None),
            P(("parts", "seq"), None),
            P(("parts", "seq"), None),
            P("parts", None),
            P("parts", None),
            P(),
            P(),
        ),
        out_specs=P(("parts", "seq"), None),
        check_vma=False,
    )
```

```python
import math

import jax
import jax.numpy as jnp
from jax import lax
from jax.experimental import pallas as pl
from jax.experimental.pallas import tpu as pltpu
from jax.sharding import PartitionSpec as P

LOG2E = math.log2(math.e)


def round_up(count, step):
    return (count + step - 1) // step * step


def normalize(entries, scales):
    mean_square = jnp.mean(entries * entries, axis=-1, keepdims=True)
    return entries * lax.rsqrt(mean_square + 1e-06) * scales


def place(slots, tokens):
    owner = lax.broadcasted_iota(jnp.int32, (tokens, slots.shape[1]), 0)
    return owner == slots


def prepare_kernel(
    per_group, padded, slots_ref, qkv_ref, k_ref, v_ref, q_gain_ref, k_gain_ref, out_ref
):
    tokens = k_ref.shape[0]
    head_size = q_gain_ref.shape[1]
    groups = qkv_ref.shape[1] // per_group
    heads = k_ref.shape[1] // head_size
    mine = place(slots_ref[...], tokens)
    is_fresh = jnp.max(mine.astype(jnp.float32), axis=1, keepdims=True) > 0.5
    one_hot = mine.astype(jnp.bfloat16)
    q_gain = q_gain_ref[...]
    k_gain = k_gain_ref[...]

    def merged(part, cache_ref):
        spread = jnp.dot(one_hot, qkv_ref[part], preferred_element_type=jnp.float32)
        return jnp.where(is_fresh, spread, cache_ref[...].astype(jnp.float32))

    keys_raw = merged(1, k_ref)
    values = merged(2, v_ref).astype(jnp.bfloat16)
    raw_queries = qkv_ref[0].astype(jnp.float32)
    for head in range(heads):
        columns = slice(head * head_size, (head + 1) * head_size)
        keys = normalize(keys_raw[:, columns], k_gain).astype(jnp.bfloat16)
        queries = normalize(raw_queries[:, columns], q_gain)
        for group in range(groups):
            at = head * groups + group
            out_ref[at, :tokens] = keys
            out_ref[at, tokens : 2 * tokens] = values[:, columns]
            share = queries[group * per_group : (group + 1) * per_group]
            if padded > per_group:
                empty = jnp.zeros((padded - per_group, head_size), jnp.float32)
                share = jnp.concatenate([share, empty], axis=0)
            out_ref[at, 2 * tokens :] = share.astype(jnp.bfloat16)


def attend_kernel(
    tokens,
    query_rows,
    key_rows,
    head_ref,
    arrived_ref,
    text_k_ref,
    text_v_ref,
    k_gain_ref,
    out_ref,
    queries_ref,
    keys_ref,
    values_ref,
    weights_ref,
    result_ref,
):
    del head_ref
    count, rows, head_size = arrived_ref.shape
    padded = rows - 2 * tokens
    factor = head_size ** (-0.5) * LOG2E
    text = text_k_ref.shape[0]
    text_keys = normalize(text_k_ref[...].astype(jnp.float32), k_gain_ref[...])
    keys_ref[:text] = text_keys.astype(jnp.bfloat16)
    values_ref[:text, :head_size] = text_v_ref[...]
    values_ref[:, head_size:] = jnp.ones((values_ref.shape[0], head_size), jnp.bfloat16)
    for step in range(count):
        first = text + step * tokens
        keys_ref[first : first + tokens] = arrived_ref[step, :tokens]
        values_ref[first : first + tokens, :head_size] = arrived_ref[step, tokens : 2 * tokens]
        queries_ref[step * padded : (step + 1) * padded] = arrived_ref[step, 2 * tokens :]

    def add_queries(step, carry):
        mine = pl.ds(pl.multiple_of(step * query_rows, 16), query_rows)
        queries = queries_ref[mine]
        for first in range(0, keys_ref.shape[0], key_rows):
            scores = lax.dot_general(
                queries,
                keys_ref[first : first + key_rows],
                (((1,), (1,)), ((), ())),
                preferred_element_type=jnp.float32,
            )
            weights_ref[:, first : first + key_rows] = jnp.exp2(scores * factor).astype(
                jnp.bfloat16
            )
        sums = jnp.dot(weights_ref[...], values_ref[...], preferred_element_type=jnp.float32)
        result_ref[mine] = (sums[:, :head_size] / sums[:, head_size:]).astype(jnp.bfloat16)
        return carry

    lax.fori_loop(0, queries_ref.shape[0] // query_rows, add_queries, 0)
    for step in range(count):
        out_ref[step] = result_ref[step * padded : (step + 1) * padded]


def finish_kernel(per_group, slots_ref, returned_ref, cache_ref, out_ref):
    tokens = cache_ref.shape[0]
    head_size = returned_ref.shape[2]
    groups = slots_ref.shape[0]
    heads = cache_ref.shape[1] // head_size
    mine = [place(slots_ref[group : group + 1], tokens) for group in range(groups)]
    count = sum(jnp.sum(m.astype(jnp.float32), axis=1, keepdims=True) for m in mine)
    is_fresh = count > 0.5
    one_hot = [m.astype(jnp.bfloat16) for m in mine]
    for head in range(heads):
        columns = slice(head * head_size, (head + 1) * head_size)
        placed = sum(
            jnp.dot(
                one_hot[group],
                returned_ref[head * groups + group],
                preferred_element_type=jnp.float32,
            )
            for group in range(groups)
        )
        out_ref[:, columns] = jnp.where(
            is_fresh, placed, cache_ref[:, columns].astype(jnp.float32)
        ).astype(out_ref.dtype)


def shards(fresh_qkv, slot_rows, k_cache, v_cache, attn_cache, text_k, text_v, q_gain, k_gain):
    seq_count = lax.axis_size("seq")
    my_index = lax.axis_index("seq")
    slot_count = slot_rows.shape[0]
    tokens, row_width = k_cache.shape
    text = text_k.shape[0]
    head_size = q_gain.shape[0]
    head_count = row_width // head_size
    groups = seq_count // head_count
    per_group = slot_count // groups
    padded = round_up(per_group, 16)
    rows = 2 * tokens + padded
    my_head = my_index // groups
    q_gain = q_gain.reshape(1, head_size)
    k_gain = k_gain.reshape(1, head_size)
    qkv = jnp.transpose(fresh_qkv, (1, 0, 2))
    slots = slot_rows.reshape(1, slot_count)
    padded_slots = jnp.pad(
        slot_rows.reshape(groups, per_group),
        ((0, 0), (0, padded - per_group)),
        constant_values=tokens,
    )

    steps = 4
    width = row_width // steps
    step_heads = head_count // steps
    outgoing = pl.pallas_call(
        lambda *refs: prepare_kernel(per_group, padded, *refs),
        out_shape=jax.ShapeDtypeStruct((seq_count, rows, head_size), jnp.bfloat16),
        grid=(steps,),
        in_specs=[
            pl.BlockSpec((1, slot_count), lambda i: (0, 0)),
            pl.BlockSpec((3, slot_count, width), lambda i: (0, 0, i)),
            pl.BlockSpec((tokens, width), lambda i: (0, i)),
            pl.BlockSpec((tokens, width), lambda i: (0, i)),
            pl.BlockSpec((1, head_size), lambda i: (0, 0)),
            pl.BlockSpec((1, head_size), lambda i: (0, 0)),
        ],
        out_specs=pl.BlockSpec((step_heads * groups, rows, head_size), lambda i: (i, 0, 0)),
        name="prepare",
    )(slots, qkv, k_cache, v_cache, q_gain, k_gain)

    arrived = lax.all_to_all(outgoing, "seq", split_axis=0, concat_axis=0, tiled=True)

    query_rows = 4 * padded
    all_keys = text + seq_count * tokens
    result = pl.pallas_call(
        lambda *refs: attend_kernel(tokens, query_rows, 256, *refs),
        out_shape=jax.ShapeDtypeStruct((seq_count, padded, head_size), jnp.bfloat16),
        grid_spec=pltpu.PrefetchScalarGridSpec(
            num_scalar_prefetch=1,
            grid=(1,),
            in_specs=[
                pl.BlockSpec((seq_count, rows, head_size), lambda i, head: (0, 0, 0)),
                pl.BlockSpec((text, head_size), lambda i, head: (0, head[0])),
                pl.BlockSpec((text, head_size), lambda i, head: (0, head[0])),
                pl.BlockSpec((1, head_size), lambda i, head: (0, 0)),
            ],
            out_specs=pl.BlockSpec((seq_count, padded, head_size), lambda i, head: (0, 0, 0)),
            scratch_shapes=[
                pltpu.VMEM((seq_count * padded, head_size), jnp.bfloat16),
                pltpu.VMEM((all_keys, head_size), jnp.bfloat16),
                pltpu.VMEM((all_keys, 2 * head_size), jnp.bfloat16),
                pltpu.VMEM((query_rows, all_keys), jnp.bfloat16),
                pltpu.VMEM((seq_count * padded, head_size), jnp.bfloat16),
            ],
        ),
        compiler_params=pltpu.CompilerParams(vmem_limit_bytes=40 * 2**20),
        name="attend",
    )(my_head.reshape(1), arrived, text_k, text_v, k_gain)

    returned = lax.all_to_all(result, "seq", split_axis=0, concat_axis=0, tiled=True)

    finish_steps = 2
    return pl.pallas_call(
        lambda *refs: finish_kernel(per_group, *refs),
        out_shape=jax.ShapeDtypeStruct((tokens, row_width), attn_cache.dtype),
        grid=(finish_steps,),
        in_specs=[
            pl.BlockSpec((groups, padded), lambda i: (0, 0)),
            pl.BlockSpec((seq_count // finish_steps, padded, head_size), lambda i: (i, 0, 0)),
            pl.BlockSpec((tokens, row_width // finish_steps), lambda i: (0, i)),
        ],
        out_specs=pl.BlockSpec((tokens, row_width // finish_steps), lambda i: (0, i)),
        compiler_params=pltpu.CompilerParams(vmem_limit_bytes=32 * 2**20),
        name="finish",
    )(padded_slots, returned, attn_cache)


def solution(mesh):
    return jax.shard_map(
        shards,
        mesh=mesh,
        in_specs=(
            P(("parts", "seq"), None, None),
            P(("parts", "seq")),
            P(("parts", "seq"), None),
            P(("parts", "seq"), None),
            P(("parts", "seq"), None),
            P("parts", None),
            P("parts", None),
            P(),
            P(),
        ),
        out_specs=P(("parts", "seq"), None),
        check_vma=False,
    )
```

```python
import math

import jax
import jax.numpy as jnp
from jax import lax
from jax.experimental import pallas as pl
from jax.experimental.pallas import tpu as pltpu
from jax.sharding import PartitionSpec as P

LOG2E = math.log2(math.e)


def round_up(count, step):
    return (count + step - 1) // step * step


def normalize(entries, scales):
    mean_square = jnp.mean(entries * entries, axis=-1, keepdims=True)
    return entries * lax.rsqrt(mean_square + 1e-06) * scales


def place(slots, tokens):
    owner = lax.broadcasted_iota(jnp.int32, (tokens, slots.shape[1]), 0)
    return owner == slots


def prepare_kernel(
    per_group, padded, me_ref, slots_ref, qkv_ref, k_ref, v_ref, q_gain_ref, k_gain_ref, *rest
):
    outs, queries_ref = rest[:-1], rest[-1]
    tokens = k_ref.shape[0]
    head_size = q_gain_ref.shape[1]
    groups = qkv_ref.shape[1] // per_group
    mine = place(slots_ref[...], tokens)
    is_fresh = jnp.max(mine.astype(jnp.float32), axis=1, keepdims=True) > 0.5
    one_hot = mine.astype(jnp.bfloat16)
    q_gain = q_gain_ref[...]
    k_gain = k_gain_ref[...]
    me = me_ref[0]

    for high in range(len(outs) // groups):
        head = lax.bitwise_xor(me // groups, high)
        columns = pl.ds(pl.multiple_of(head * head_size, head_size), head_size)

        def merged(part, cache_ref):
            spread = jnp.dot(
                one_hot, qkv_ref[part, :, columns], preferred_element_type=jnp.float32
            )
            return jnp.where(is_fresh, spread, cache_ref[:, columns].astype(jnp.float32))

        keys = normalize(merged(1, k_ref), k_gain).astype(jnp.bfloat16)
        values = merged(2, v_ref).astype(jnp.bfloat16)
        queries = normalize(qkv_ref[0, :, columns].astype(jnp.float32), q_gain)
        empty = jnp.zeros((padded - per_group, head_size), jnp.float32)
        for group in range(groups):
            share = queries[group * per_group : (group + 1) * per_group]
            if padded > per_group:
                share = jnp.concatenate([share, empty], axis=0)
            queries_ref[group] = share.astype(jnp.bfloat16)
        for low in range(groups):
            out_ref = outs[high * groups + low]
            group = lax.bitwise_xor(me % groups, low)
            out_ref[:tokens] = keys
            out_ref[tokens : 2 * tokens] = values
            out_ref[2 * tokens :] = queries_ref[group]


def attend_kernel(tokens, query_rows, key_rows, steps, me_ref, *rest):
    me = me_ref[0]
    count = len(steps)
    arrived = rest[:count]
    text_k_ref, text_v_ref, k_gain_ref = rest[count : count + 3]
    out_ref, queries_ref, keys_ref, values_ref, weights_ref, result_ref = rest[count + 3 :]
    head_size = text_k_ref.shape[1]
    padded = arrived[0].shape[0] - 2 * tokens
    factor = head_size ** (-0.5) * LOG2E
    text = text_k_ref.shape[0]
    text_keys = normalize(text_k_ref[...].astype(jnp.float32), k_gain_ref[...])
    keys_ref[:text] = text_keys.astype(jnp.bfloat16)
    values_ref[:text, :head_size] = text_v_ref[...]
    values_ref[:, head_size:] = jnp.ones((values_ref.shape[0], head_size), jnp.bfloat16)
    for step in range(count):
        first = text + step * tokens
        keys_ref[first : first + tokens] = arrived[step][:tokens]
        values_ref[first : first + tokens, :head_size] = arrived[step][tokens : 2 * tokens]
        queries_ref[step * padded : (step + 1) * padded] = arrived[step][2 * tokens :]

    def add_queries(step, carry):
        mine = pl.ds(pl.multiple_of(step * query_rows, 16), query_rows)
        queries = queries_ref[mine]
        for first in range(0, keys_ref.shape[0], key_rows):
            scores = lax.dot_general(
                queries,
                keys_ref[first : first + key_rows],
                (((1,), (1,)), ((), ())),
                preferred_element_type=jnp.float32,
            )
            weights_ref[:, first : first + key_rows] = jnp.exp2(scores * factor).astype(
                jnp.bfloat16
            )
        sums = jnp.dot(weights_ref[...], values_ref[...], preferred_element_type=jnp.float32)
        result_ref[mine] = (sums[:, :head_size] / sums[:, head_size:]).astype(jnp.bfloat16)
        return carry

    lax.fori_loop(0, queries_ref.shape[0] // query_rows, add_queries, 0)
    for step in range(count):
        owner = lax.bitwise_xor(me, steps[step])
        out_ref[owner] = result_ref[step * padded : (step + 1) * padded]


def finish_kernel(per_group, slots_ref, returned_ref, cache_ref, out_ref):
    tokens = cache_ref.shape[0]
    head_size = returned_ref.shape[2]
    groups = slots_ref.shape[0]
    heads = cache_ref.shape[1] // head_size
    mine = [place(slots_ref[group : group + 1], tokens) for group in range(groups)]
    count = sum(jnp.sum(m.astype(jnp.float32), axis=1, keepdims=True) for m in mine)
    is_fresh = count > 0.5
    one_hot = [m.astype(jnp.bfloat16) for m in mine]
    for head in range(heads):
        columns = slice(head * head_size, (head + 1) * head_size)
        placed = sum(
            jnp.dot(
                one_hot[group],
                returned_ref[head * groups + group],
                preferred_element_type=jnp.float32,
            )
            for group in range(groups)
        )
        out_ref[:, columns] = jnp.where(
            is_fresh, placed, cache_ref[:, columns].astype(jnp.float32)
        ).astype(out_ref.dtype)


def whole(shape):
    return pl.BlockSpec(shape, lambda i, me: (0,) * len(shape))


def partners(count):
    half = count // 2
    order = []
    for near in reversed(range(half)):
        order.append(half + near)
        if near > 0:
            order.append(near)
    order[1], order[2] = order[2], order[1]
    names = sorted(range(count - 1), key=lambda number: str(number) if number else "")
    return [0] + [order[names.index(number)] for number in range(count - 1)]


def exchange(blocks, steps):
    count = len(blocks)
    arrived = []
    for step in steps:
        pairs = [(a, a ^ step) for a in range(count)]
        arrived.append(lax.ppermute(blocks[step], "seq", pairs) if step else blocks[0])
    return arrived


def shards(fresh_qkv, slot_rows, k_cache, v_cache, attn_cache, text_k, text_v, q_gain, k_gain):
    seq_count = lax.axis_size("seq")
    me = lax.axis_index("seq").reshape(1)
    slot_count = slot_rows.shape[0]
    tokens, row_width = k_cache.shape
    text = text_k.shape[0]
    head_size = q_gain.shape[0]
    head_count = row_width // head_size
    groups = seq_count // head_count
    per_group = slot_count // groups
    padded = round_up(per_group, 16)
    rows = 2 * tokens + padded
    q_gain = q_gain.reshape(1, head_size)
    k_gain = k_gain.reshape(1, head_size)
    qkv = jnp.transpose(fresh_qkv, (1, 0, 2))
    slots = slot_rows.reshape(1, slot_count)
    padded_slots = jnp.pad(
        slot_rows.reshape(groups, per_group),
        ((0, 0), (0, padded - per_group)),
        constant_values=tokens,
    )

    outgoing = pl.pallas_call(
        lambda *refs: prepare_kernel(per_group, padded, *refs),
        out_shape=[jax.ShapeDtypeStruct((rows, head_size), jnp.bfloat16)] * seq_count,
        grid_spec=pltpu.PrefetchScalarGridSpec(
            num_scalar_prefetch=1,
            grid=(1,),
            in_specs=[
                whole((1, slot_count)),
                whole((3, slot_count, row_width)),
                whole((tokens, row_width)),
                whole((tokens, row_width)),
                whole((1, head_size)),
                whole((1, head_size)),
            ],
            out_specs=[whole((rows, head_size))] * seq_count,
            scratch_shapes=[pltpu.VMEM((groups, padded, head_size), jnp.bfloat16)],
        ),
        name="prepare",
    )(me, slots, qkv, k_cache, v_cache, q_gain, k_gain)

    steps = partners(seq_count)
    arrived = exchange(outgoing, steps)

    query_rows = 4 * padded
    all_keys = text + seq_count * tokens
    result = pl.pallas_call(
        lambda *refs: attend_kernel(tokens, query_rows, 256, steps, *refs),
        out_shape=jax.ShapeDtypeStruct((seq_count, padded, head_size), jnp.bfloat16),
        grid_spec=pltpu.PrefetchScalarGridSpec(
            num_scalar_prefetch=1,
            grid=(1,),
            in_specs=[whole((rows, head_size))] * seq_count
            + [pl.BlockSpec((text, head_size), lambda i, me: (0, me[0] // groups))] * 2
            + [whole((1, head_size))],
            out_specs=whole((seq_count, padded, head_size)),
            scratch_shapes=[
                pltpu.VMEM((seq_count * padded, head_size), jnp.bfloat16),
                pltpu.VMEM((all_keys, head_size), jnp.bfloat16),
                pltpu.VMEM((all_keys, 2 * head_size), jnp.bfloat16),
                pltpu.VMEM((query_rows, all_keys), jnp.bfloat16),
                pltpu.VMEM((seq_count * padded, head_size), jnp.bfloat16),
            ],
        ),
        compiler_params=pltpu.CompilerParams(vmem_limit_bytes=40 * 2**20),
        name="attend",
    )(me, *arrived, text_k, text_v, k_gain)

    returned = lax.all_to_all(result, "seq", split_axis=0, concat_axis=0, tiled=True)

    finish_steps = 1
    return pl.pallas_call(
        lambda *refs: finish_kernel(per_group, *refs),
        out_shape=jax.ShapeDtypeStruct((tokens, row_width), attn_cache.dtype),
        grid=(finish_steps,),
        in_specs=[
            pl.BlockSpec((groups, padded), lambda i: (0, 0)),
            pl.BlockSpec((seq_count // finish_steps, padded, head_size), lambda i: (i, 0, 0)),
            pl.BlockSpec((tokens, row_width // finish_steps), lambda i: (0, i)),
        ],
        out_specs=pl.BlockSpec((tokens, row_width // finish_steps), lambda i: (0, i)),
        compiler_params=pltpu.CompilerParams(vmem_limit_bytes=32 * 2**20),
        name="finish",
    )(padded_slots, returned, attn_cache)


def solution(mesh):
    return jax.shard_map(
        shards,
        mesh=mesh,
        in_specs=(
            P(("parts", "seq"), None, None),
            P(("parts", "seq")),
            P(("parts", "seq"), None),
            P(("parts", "seq"), None),
            P(("parts", "seq"), None),
            P("parts", None),
            P("parts", None),
            P(),
            P(),
        ),
        out_specs=P(("parts", "seq"), None),
        check_vma=False,
    )
```

```python
import math

import jax
import jax.numpy as jnp
from jax import lax
from jax.experimental import pallas as pl
from jax.experimental.pallas import tpu as pltpu
from jax.sharding import PartitionSpec as P

LOG2E = math.log2(math.e)
FIRST_HEADS = [15, 14, 13, 1]


def round_up(count, step):
    return (count + step - 1) // step * step


def normalize(entries, scales):
    mean_square = jnp.mean(entries * entries, axis=-1, keepdims=True)
    return entries * lax.rsqrt(mean_square + 1e-06) * scales


def place(slots, tokens):
    owner = lax.broadcasted_iota(jnp.int32, (tokens, slots.shape[1]), 0)
    return owner == slots


def prepare_kernel(per_group, padded, highs, by_head, me_ref, slots_ref, q_gain_ref, k_gain_ref, *rest):
    tokens = 0
    if by_head:
        groups = slots_ref.shape[1] // per_group
        loads = [rest[3 * turn : 3 * turn + 3] for turn in range(len(highs))]
        outs = rest[3 * len(highs) : 3 * len(highs) + groups * len(highs)]
        queries_ref = rest[-1]
        tokens = loads[0][1].shape[0]
    else:
        groups = slots_ref.shape[1] // per_group
        qkv_ref, k_ref, v_ref, text_k_ref, text_v_ref = rest[:5]
        rest = rest[6:]
        outs = rest[: groups * len(highs)]
        text_keys_ref, text_values_ref, queries_ref = rest[groups * len(highs) :]
        tokens = k_ref.shape[0]
    head_size = q_gain_ref.shape[1]
    me = me_ref[0]
    mine = place(slots_ref[...], tokens)
    is_fresh = jnp.max(mine.astype(jnp.float32), axis=1, keepdims=True) > 0.5
    one_hot = mine.astype(jnp.bfloat16)
    q_gain = q_gain_ref[...]
    k_gain = k_gain_ref[...]

    def merged(fresh, cache):
        spread = jnp.dot(one_hot, fresh, preferred_element_type=jnp.float32)
        return jnp.where(is_fresh, spread, cache.astype(jnp.float32))

    for turn, high in enumerate(highs):
        if by_head:
            fresh_ref, cache_k_ref, cache_v_ref = loads[turn]
            fresh = [fresh_ref[part] for part in range(3)]
            cache_k, cache_v = cache_k_ref[...], cache_v_ref[...]
        else:
            head = lax.bitwise_xor(me // groups, high)
            columns = pl.ds(pl.multiple_of(head * head_size, head_size), head_size)
            fresh = [qkv_ref[part, :, columns] for part in range(3)]
            cache_k, cache_v = k_ref[:, columns], v_ref[:, columns]
        keys = normalize(merged(fresh[1], cache_k), k_gain).astype(jnp.bfloat16)
        values = merged(fresh[2], cache_v).astype(jnp.bfloat16)
        queries = normalize(fresh[0].astype(jnp.float32), q_gain)
        empty = jnp.zeros((padded - per_group, head_size), jnp.float32)
        for group in range(groups):
            share = queries[group * per_group : (group + 1) * per_group]
            if padded > per_group:
                share = jnp.concatenate([share, empty], axis=0)
            queries_ref[group] = share.astype(jnp.bfloat16)
        for low in range(groups):
            out_ref = outs[turn * groups + low]
            group = lax.bitwise_xor(me % groups, low)
            out_ref[:tokens] = keys
            out_ref[tokens : 2 * tokens] = values
            out_ref[2 * tokens :] = queries_ref[group]
    if not by_head:
        text_keys = normalize(text_k_ref[...].astype(jnp.float32), k_gain)
        text_keys_ref[...] = text_keys.astype(jnp.bfloat16)
        text_values_ref[...] = text_v_ref[...]


def attend_kernel(tokens, query_rows, key_rows, steps, me_ref, *rest):
    me = me_ref[0]
    count = len(steps)
    arrived = rest[:count]
    text_keys_ref, text_values_ref = rest[count : count + 2]
    out_ref, queries_ref, keys_ref, values_ref, weights_ref, result_ref = rest[count + 2 :]
    head_size = text_keys_ref.shape[1]
    padded = arrived[0].shape[0] - 2 * tokens
    factor = head_size ** (-0.5) * LOG2E
    text = text_keys_ref.shape[0]
    keys_ref[:text] = text_keys_ref[...]
    values_ref[:text, :head_size] = text_values_ref[...]
    values_ref[:, head_size:] = jnp.ones((values_ref.shape[0], head_size), jnp.bfloat16)
    for step in range(count):
        first = text + step * tokens
        keys_ref[first : first + tokens] = arrived[step][:tokens]
        values_ref[first : first + tokens, :head_size] = arrived[step][tokens : 2 * tokens]
        queries_ref[step * padded : (step + 1) * padded] = arrived[step][2 * tokens :]

    def add_queries(step, carry):
        mine = pl.ds(pl.multiple_of(step * query_rows, 16), query_rows)
        queries = queries_ref[mine]
        for first in range(0, keys_ref.shape[0], key_rows):
            scores = lax.dot_general(
                queries,
                keys_ref[first : first + key_rows],
                (((1,), (1,)), ((), ())),
                preferred_element_type=jnp.float32,
            )
            weights_ref[:, first : first + key_rows] = jnp.exp2(scores * factor).astype(
                jnp.bfloat16
            )
        sums = jnp.dot(weights_ref[...], values_ref[...], preferred_element_type=jnp.float32)
        result_ref[mine] = (sums[:, :head_size] / sums[:, head_size:]).astype(jnp.bfloat16)
        return carry

    lax.fori_loop(0, queries_ref.shape[0] // query_rows, add_queries, 0)
    for step in range(count):
        owner = lax.bitwise_xor(me, steps[step])
        out_ref[owner] = result_ref[step * padded : (step + 1) * padded]


def finish_kernel(per_group, slots_ref, returned_ref, cache_ref, out_ref):
    tokens = cache_ref.shape[0]
    head_size = returned_ref.shape[2]
    groups = slots_ref.shape[0]
    heads = cache_ref.shape[1] // head_size
    mine = [place(slots_ref[group : group + 1], tokens) for group in range(groups)]
    count = sum(jnp.sum(m.astype(jnp.float32), axis=1, keepdims=True) for m in mine)
    is_fresh = count > 0.5
    one_hot = [m.astype(jnp.bfloat16) for m in mine]
    for head in range(heads):
        columns = slice(head * head_size, (head + 1) * head_size)
        placed = sum(
            jnp.dot(
                one_hot[group],
                returned_ref[head * groups + group],
                preferred_element_type=jnp.float32,
            )
            for group in range(groups)
        )
        out_ref[:, columns] = jnp.where(
            is_fresh, placed, cache_ref[:, columns].astype(jnp.float32)
        ).astype(out_ref.dtype)


def whole(shape):
    return pl.BlockSpec(shape, lambda i, me: (0,) * len(shape))


def partners(count):
    half = count // 2
    far = list(reversed(range(half, count)))
    near = list(reversed(range(1, half)))
    order = far[:3]
    for turn in range(max(len(far) - 3, len(near))):
        order += near[turn : turn + 1] + far[turn + 3 : turn + 4]
    names = sorted(range(count - 1), key=lambda number: str(number) if number else "")
    return [0] + [order[names.index(number)] for number in range(count - 1)]


def trade(block, step):
    if step == 0:
        return block
    count = lax.axis_size("seq")
    return lax.ppermute(block, "seq", [(a, a ^ step) for a in range(count)])


def shards(fresh_qkv, slot_rows, k_cache, v_cache, attn_cache, text_k, text_v, q_gain, k_gain):
    seq_count = lax.axis_size("seq")
    me = lax.axis_index("seq").reshape(1)
    slot_count = slot_rows.shape[0]
    tokens, row_width = k_cache.shape
    text = text_k.shape[0]
    head_size = q_gain.shape[0]
    head_count = row_width // head_size
    groups = seq_count // head_count
    per_group = slot_count // groups
    padded = round_up(per_group, 16)
    rows = 2 * tokens + padded
    q_gain = q_gain.reshape(1, head_size)
    k_gain = k_gain.reshape(1, head_size)
    qkv = jnp.transpose(fresh_qkv, (1, 0, 2))
    slots = slot_rows.reshape(1, slot_count)
    padded_slots = jnp.pad(
        slot_rows.reshape(groups, per_group),
        ((0, 0), (0, padded - per_group)),
        constant_values=tokens,
    )

    steps = partners(seq_count)
    block = jax.ShapeDtypeStruct((rows, head_size), jnp.bfloat16)
    text_block = jax.ShapeDtypeStruct((text, head_size), jnp.bfloat16)
    scratch = [pltpu.VMEM((groups, padded, head_size), jnp.bfloat16)]
    common = [whole((1, slot_count)), whole((1, head_size)), whole((1, head_size))]
    early = FIRST_HEADS
    late = [high for high in reversed(range(head_count)) if high not in early]

    def head_specs(high):
        def column(me):
            return lax.bitwise_xor(me[0] // groups, high)

        return [
            pl.BlockSpec((3, slot_count, head_size), lambda i, me: (0, 0, column(me))),
            pl.BlockSpec((tokens, head_size), lambda i, me: (0, column(me))),
            pl.BlockSpec((tokens, head_size), lambda i, me: (0, column(me))),
        ]

    first = pl.pallas_call(
        lambda *refs: prepare_kernel(per_group, padded, early, True, *refs),
        out_shape=[block] * (groups * len(early)),
        grid_spec=pltpu.PrefetchScalarGridSpec(
            num_scalar_prefetch=1,
            grid=(1,),
            in_specs=common + [spec for high in early for spec in head_specs(high)],
            out_specs=[whole((rows, head_size))] * (groups * len(early)),
            scratch_shapes=scratch,
        ),
        name="prepare_first",
    )(me, slots, q_gain, k_gain, *([qkv, k_cache, v_cache] * len(early)))
    met = {}
    for turn, made in enumerate(first):
        step = early[turn // groups] * groups + turn % groups
        met[step] = trade(made, step)
    text_spec = pl.BlockSpec((text, head_size), lambda i, me: (0, me[0] // groups))
    *second, text_keys, text_values = pl.pallas_call(
        lambda *refs: prepare_kernel(per_group, padded, late, False, *refs),
        out_shape=[block] * (groups * len(late)) + [text_block] * 2,
        grid_spec=pltpu.PrefetchScalarGridSpec(
            num_scalar_prefetch=1,
            grid=(1,),
            in_specs=common
            + [
                whole((3, slot_count, row_width)),
                whole((tokens, row_width)),
                whole((tokens, row_width)),
                text_spec,
                text_spec,
                pl.BlockSpec(memory_space=pl.ANY),
            ],
            out_specs=[whole((rows, head_size))] * (groups * len(late))
            + [whole((text, head_size))] * 2,
            scratch_shapes=scratch,
        ),
        name="prepare_rest",
    )(me, slots, q_gain, k_gain, qkv, k_cache, v_cache, text_k, text_v, met[groups])
    arrived = dict(met)
    for turn, made in enumerate(second):
        step = late[turn // groups] * groups + turn % groups
        arrived[step] = trade(made, step)
    arrived = [arrived[step] for step in steps]

    query_rows = 4 * padded
    all_keys = text + seq_count * tokens
    result = pl.pallas_call(
        lambda *refs: attend_kernel(tokens, query_rows, 256, steps, *refs),
        out_shape=jax.ShapeDtypeStruct((seq_count, padded, head_size), jnp.bfloat16),
        grid_spec=pltpu.PrefetchScalarGridSpec(
            num_scalar_prefetch=1,
            grid=(1,),
            in_specs=[whole((rows, head_size))] * seq_count
            + [whole((text, head_size))] * 2,
            out_specs=whole((seq_count, padded, head_size)),
            scratch_shapes=[
                pltpu.VMEM((seq_count * padded, head_size), jnp.bfloat16),
                pltpu.VMEM((all_keys, head_size), jnp.bfloat16),
                pltpu.VMEM((all_keys, 2 * head_size), jnp.bfloat16),
                pltpu.VMEM((query_rows, all_keys), jnp.bfloat16),
                pltpu.VMEM((seq_count * padded, head_size), jnp.bfloat16),
            ],
        ),
        compiler_params=pltpu.CompilerParams(vmem_limit_bytes=40 * 2**20),
        name="attend",
    )(me, *arrived, text_keys, text_values)

    returned = lax.all_to_all(result, "seq", split_axis=0, concat_axis=0, tiled=True)

    finish_steps = 1
    return pl.pallas_call(
        lambda *refs: finish_kernel(per_group, *refs),
        out_shape=jax.ShapeDtypeStruct((tokens, row_width), attn_cache.dtype),
        grid=(finish_steps,),
        in_specs=[
            pl.BlockSpec((groups, padded), lambda i: (0, 0)),
            pl.BlockSpec((seq_count // finish_steps, padded, head_size), lambda i: (i, 0, 0)),
            pl.BlockSpec((tokens, row_width // finish_steps), lambda i: (0, i)),
        ],
        out_specs=pl.BlockSpec((tokens, row_width // finish_steps), lambda i: (0, i)),
        compiler_params=pltpu.CompilerParams(vmem_limit_bytes=32 * 2**20),
        name="finish",
    )(padded_slots, returned, attn_cache)


def solution(mesh):
    return jax.shard_map(
        shards,
        mesh=mesh,
        in_specs=(
            P(("parts", "seq"), None, None),
            P(("parts", "seq")),
            P(("parts", "seq"), None),
            P(("parts", "seq"), None),
            P(("parts", "seq"), None),
            P("parts", None),
            P("parts", None),
            P(),
            P(),
        ),
        out_specs=P(("parts", "seq"), None),
        check_vma=False,
    )
```

```python
import math

import jax
import jax.numpy as jnp
from jax import lax
from jax.experimental import pallas as pl
from jax.experimental.pallas import tpu as pltpu
from jax.sharding import PartitionSpec as P

LOG2E = math.log2(math.e)
INNER = 2
MIB = 2**20


def round_up(count, step):
    return (count + step - 1) // step * step


def normalize(entries, scales):
    mean_square = jnp.mean(entries * entries, axis=-1, keepdims=True)
    return entries * lax.rsqrt(mean_square + 1e-06) * scales


def place(slots, tokens):
    owner = lax.broadcasted_iota(jnp.int32, (tokens, slots.shape[1]), 0)
    return owner == slots


def prepare_kernel(plan, groups, per_group, padded, with_text, me_ref, *refs):
    slots_hbm, q_gain_hbm, k_gain_hbm, qkv_hbm, k_hbm, v_hbm = refs[:6]
    rest = refs[6:]
    if with_text:
        text_k_hbm, text_v_hbm = rest[:2]
        rest = rest[3:]
    outs = []
    for _, apart in plan:
        taken = 2 if apart else 1
        outs.append(rest[:taken])
        rest = rest[taken:]
    if with_text:
        text_keys_ref, text_values_ref = rest[:2]
        rest = rest[2:]
    slots_ref, q_gain_ref, k_gain_ref, fresh_ref, k_ref, v_ref, text_ref, share_ref = rest[:8]
    small_sems, sems, text_sems = rest[8:]
    tokens, width = k_ref.shape[1:]
    head_size = q_gain_ref.shape[1]
    outer = me_ref[0] // INNER

    def columns(step):
        block = lax.bitwise_xor(outer // groups, step // groups)
        return pl.ds(pl.multiple_of(block * width, width), width)

    small = [
        pltpu.make_async_copy(slots_hbm, slots_ref, small_sems.at[0]),
        pltpu.make_async_copy(q_gain_hbm, q_gain_ref, small_sems.at[1]),
        pltpu.make_async_copy(k_gain_hbm, k_gain_ref, small_sems.at[2]),
    ]
    for copy in small:
        copy.start()
    loads = []
    for turn, (step, _) in enumerate(plan):
        mine = columns(step)
        loads.append(
            [
                pltpu.make_async_copy(
                    qkv_hbm.at[:, :, mine], fresh_ref.at[turn], sems.at[turn, 0]
                ),
                pltpu.make_async_copy(k_hbm.at[:, mine], k_ref.at[turn], sems.at[turn, 1]),
                pltpu.make_async_copy(v_hbm.at[:, mine], v_ref.at[turn], sems.at[turn, 2]),
            ]
        )
        for copy in loads[-1]:
            copy.start()
    if with_text:
        mine = columns(0)
        text_loads = [
            pltpu.make_async_copy(text_k_hbm.at[:, mine], text_ref.at[0], text_sems.at[0]),
            pltpu.make_async_copy(text_v_hbm.at[:, mine], text_ref.at[1], text_sems.at[1]),
        ]
        for copy in text_loads:
            copy.start()
    for copy in small:
        copy.wait()
    belongs = place(slots_ref[...], tokens)
    is_fresh = jnp.max(belongs.astype(jnp.float32), axis=1, keepdims=True) > 0.5
    one_hot = belongs.astype(jnp.bfloat16)
    q_gain = q_gain_ref[...]
    k_gain = k_gain_ref[...]

    def merged(fresh, cache):
        spread = jnp.dot(one_hot, fresh, preferred_element_type=jnp.float32)
        return jnp.where(is_fresh, spread, cache.astype(jnp.float32))

    for turn, (step, apart) in enumerate(plan):
        for copy in loads[turn]:
            copy.wait()
        group = lax.bitwise_xor(outer % groups, step % groups)
        for head in range(width // head_size):
            lanes = slice(head * head_size, (head + 1) * head_size)
            keys = normalize(merged(fresh_ref[turn, 1, :, lanes], k_ref[turn, :, lanes]), k_gain)
            values = merged(fresh_ref[turn, 2, :, lanes], v_ref[turn, :, lanes])
            queries = normalize(fresh_ref[turn, 0, :, lanes].astype(jnp.float32), q_gain)
            for part in range(groups):
                share = queries[part * per_group : (part + 1) * per_group]
                if padded > per_group:
                    empty = jnp.zeros((padded - per_group, head_size), jnp.float32)
                    share = jnp.concatenate([share, empty], axis=0)
                share_ref[part] = share.astype(jnp.bfloat16)
            outs[turn][0][head, :tokens] = keys.astype(jnp.bfloat16)
            outs[turn][0][head, tokens : 2 * tokens] = values.astype(jnp.bfloat16)
            if apart:
                outs[turn][1][head] = share_ref[group]
            else:
                outs[turn][0][head, 2 * tokens :] = share_ref[group]
    if with_text:
        for copy in text_loads:
            copy.wait()
        for head in range(width // head_size):
            lanes = slice(head * head_size, (head + 1) * head_size)
            text_keys = normalize(text_ref[0, :, lanes].astype(jnp.float32), k_gain)
            text_keys_ref[head] = text_keys.astype(jnp.bfloat16)
            text_values_ref[head] = text_ref[1, :, lanes]


def gather_kernel(tokens, extra, count, *refs):
    blocks, refs = refs[:count], refs[count:]
    if extra:
        own, other, text_keys, text_values, own_queries = refs[:5]
        refs = refs[5:]
        kept_ref = refs[2]
        text = text_keys.shape[1]
        for number, block in enumerate([own, other]):
            rows = slice(text + number * tokens, text + (number + 1) * tokens)
            kept_ref[:, 0, rows] = block[:, :tokens]
            kept_ref[:, 1, rows] = block[:, tokens:]
        kept_ref[:, 0, :text] = text_keys[...]
        kept_ref[:, 1, :text] = text_values[...]
        parts = [own_queries[...]]
    else:
        parts = []
    out_ref, queries_ref = refs[:2]
    for number, block in enumerate(blocks):
        rows = slice(number * tokens, (number + 1) * tokens)
        out_ref[:, 0, rows] = block[:, :tokens]
        out_ref[:, 1, rows] = block[:, tokens : 2 * tokens]
        parts.append(block[:, 2 * tokens :])
    padded = parts[0].shape[1]
    for number, part in enumerate(parts):
        queries_ref[:, number * padded : (number + 1) * padded] = part


def add_keys(sums, queries, keys, values):
    factor = queries.shape[1] ** (-0.5) * LOG2E
    scores = lax.dot_general(
        queries, keys, (((1,), (1,)), ((), ())), preferred_element_type=jnp.float32
    )
    weights = jnp.exp2(scores * factor).astype(jnp.bfloat16)
    beside = jnp.concatenate([values, jnp.ones_like(values)], axis=1)
    added = jnp.dot(weights, beside, preferred_element_type=jnp.float32)
    return added if sums is None else sums + added


def add_shared(sums, queries, shared, head, tokens):
    for ref in shared:
        rows = ref.shape[2]
        chunk = next(c * tokens for c in (4, 3, 2, 1) if rows % (c * tokens) == 0)
        for first in range(0, rows, chunk):
            at = slice(first, first + chunk)
            sums = add_keys(sums, queries, ref[head, 0, at], ref[head, 1, at])
    return sums


def row_blocks(ref, padded):
    rows = ref.shape[1]
    return [slice(first, min(first + 5 * padded, rows)) for first in range(0, rows, 5 * padded)]


def attend_early_kernel(tokens, padded, *refs):
    shared, queries_ref, sums_ref = refs[:-2], refs[-2], refs[-1]
    for head in range(queries_ref.shape[0]):
        for rows in row_blocks(queries_ref, padded):
            sums_ref[head, rows] = add_shared(None, queries_ref[head, rows], shared, head, tokens)


def attend_late_kernel(tokens, padded, *refs):
    shared = refs[:-5]
    early_ref, early_sums_ref, late_ref, early_out_ref, late_out_ref = refs[-5:]
    for head in range(early_ref.shape[0]):
        for rows in row_blocks(early_ref, padded):
            early_out_ref[head, rows] = add_shared(
                early_sums_ref[head, rows], early_ref[head, rows], shared[-1:], head, tokens
            )
        for rows in row_blocks(late_ref, padded):
            late_out_ref[head, rows] = add_shared(
                None, late_ref[head, rows], shared, head, tokens
            )


def complete_kernel(tokens, steps, me_ref, shared_ref, *refs):
    outer = me_ref[0] // INNER
    out_ref = refs[-1]
    heads, padded, head_size = out_ref.shape[1:]
    for head in range(heads):
        number = 0
        for queries_ref, sums_ref in (refs[0:2], refs[2:4]):
            for rows in row_blocks(queries_ref, padded):
                sums = add_shared(
                    sums_ref[head, rows], queries_ref[head, rows], [shared_ref], head, tokens
                )
                result = (sums[:, :head_size] / sums[:, head_size:]).astype(jnp.bfloat16)
                for first in range(0, rows.stop - rows.start, padded):
                    owner = lax.bitwise_xor(outer, steps[number])
                    out_ref[owner, head] = result[first : first + padded]
                    number += 1


def finish_kernel(per_group, slots_ref, returned_ref, cache_ref, out_ref):
    tokens = cache_ref.shape[0]
    heads, _, head_size = returned_ref.shape[1:]
    groups = slots_ref.shape[0]
    mine = [place(slots_ref[group : group + 1], tokens) for group in range(groups)]
    count = sum(jnp.sum(m.astype(jnp.float32), axis=1, keepdims=True) for m in mine)
    is_fresh = count > 0.5
    one_hot = [m.astype(jnp.bfloat16) for m in mine]
    for number in range(cache_ref.shape[1] // head_size):
        columns = slice(number * head_size, (number + 1) * head_size)
        placed = sum(
            jnp.dot(
                one_hot[group],
                returned_ref[number // heads * groups + group, number % heads],
                preferred_element_type=jnp.float32,
            )
            for group in range(groups)
        )
        out_ref[:, columns] = jnp.where(
            is_fresh, placed, cache_ref[:, columns].astype(jnp.float32)
        ).astype(out_ref.dtype)


def work(micros):
    return pl.CostEstimate(
        flops=int(micros * 1e9), bytes_accessed=int(micros * 3e6), transcendentals=0
    )


def trade(block, distance):
    count = lax.axis_size("seq")
    return lax.ppermute(block, "seq", [(a, a ^ distance) for a in range(count)])


def shards(fresh_qkv, slot_rows, k_cache, v_cache, attn_cache, text_k, text_v, q_gain, k_gain):
    seq_count = lax.axis_size("seq")
    me = lax.axis_index("seq").reshape(1)
    slot_count = slot_rows.shape[0]
    tokens, row_width = k_cache.shape
    text = text_k.shape[0]
    head_size = q_gain.shape[0]
    outers = seq_count // INNER
    all_heads = row_width // head_size
    heads = max(1, all_heads // outers)
    groups = outers * heads // all_heads
    per_group = slot_count // groups
    padded = round_up(per_group, 16)
    width = heads * head_size
    qkv = jnp.transpose(fresh_qkv, (1, 0, 2))
    q_gain = q_gain.reshape(1, head_size)
    k_gain = k_gain.reshape(1, head_size)
    slots = slot_rows.reshape(1, slot_count)
    padded_slots = jnp.pad(
        slot_rows.reshape(groups, per_group),
        ((0, 0), (0, padded - per_group)),
        constant_values=tokens,
    )

    def shaped(*shape, dtype=jnp.bfloat16):
        return jax.ShapeDtypeStruct(shape, dtype)

    in_hbm = pl.BlockSpec(memory_space=pltpu.HBM)
    in_vmem = pl.BlockSpec(memory_space=pltpu.VMEM)
    in_smem = pl.BlockSpec(memory_space=pltpu.SMEM)

    def prepare(plan, with_text, name, *extra):
        shapes = []
        for _, apart in plan:
            if apart:
                shapes += [shaped(heads, 2 * tokens, head_size), shaped(heads, padded, head_size)]
            else:
                shapes += [shaped(heads, 2 * tokens + padded, head_size)]
        if with_text:
            shapes += [shaped(heads, text, head_size)] * 2
        made = pl.pallas_call(
            lambda *refs: prepare_kernel(plan, groups, per_group, padded, with_text, *refs),
            out_shape=shapes,
            in_specs=[in_smem] + [in_hbm] * 6 + [in_hbm] * (2 * with_text)
            + [pl.BlockSpec(memory_space=pl.ANY)] * with_text,
            out_specs=[in_vmem] * len(shapes),
            scratch_shapes=[
                pltpu.VMEM((1, slot_count), jnp.int32),
                pltpu.VMEM((1, head_size), jnp.float32),
                pltpu.VMEM((1, head_size), jnp.float32),
                pltpu.VMEM((len(plan), 3, slot_count, width), jnp.bfloat16),
                pltpu.VMEM((len(plan), tokens, width), jnp.bfloat16),
                pltpu.VMEM((len(plan), tokens, width), jnp.bfloat16),
                pltpu.VMEM((2, text, width), jnp.bfloat16),
                pltpu.VMEM((groups, padded, head_size), jnp.bfloat16),
                pltpu.SemaphoreType.DMA((3,)),
                pltpu.SemaphoreType.DMA((len(plan), 3)),
                pltpu.SemaphoreType.DMA((2,)),
            ],
            cost_estimate=work(20),
            name=name,
        )(me, slots, q_gain, k_gain, qkv, k_cache, v_cache, *extra)
        return list(made)

    half = outers // 2
    far = list(reversed(range(half, outers)))
    early = far[:1] + list(range(1, half))
    late = far[1:]
    block, own, own_queries = prepare([(far[0], False), (0, True)], False, "prepare_first")
    arrived = {far[0]: trade(block, far[0] * INNER)}
    other = trade(own, 1)

    order = late[:1] + early[1:] + late[1:]
    *made, text_keys, text_values = prepare(
        [(step, False) for step in order], True, "prepare_rest", text_k, text_v, other
    )
    for step, block in zip(order, made):
        arrived[step] = trade(block, step * INNER)

    def gather(steps, name, *extra, after=()):
        count = len(steps) + (1 if extra else 0)
        shapes = [
            shaped(heads, 2, len(steps) * tokens, head_size),
            shaped(heads, count * padded, head_size),
        ]
        if extra:
            shapes.append(shaped(heads, 2, text + 2 * tokens, head_size))
        return pl.pallas_call(
            lambda *refs: gather_kernel(
                tokens, bool(extra), len(steps), *refs[len(after) :]
            ),
            out_shape=shapes,
            in_specs=[pl.BlockSpec(memory_space=pl.ANY)] * len(after)
            + [in_vmem] * (len(steps) + len(extra)),
            out_specs=[in_vmem] * len(shapes),
            compiler_params=pltpu.CompilerParams(vmem_limit_bytes=24 * MIB),
            cost_estimate=work(10),
            name=name,
        )(*after, *[arrived[step] for step in steps], *extra)

    early_keys, early_queries, kept = gather(
        early, "gather_early", own, other, text_keys, text_values, own_queries
    )
    early_other = trade(early_keys, 1)
    sums_shape = shaped(heads, early_queries.shape[1], 2 * head_size, dtype=jnp.float32)
    early_sums = pl.pallas_call(
        lambda *refs: attend_early_kernel(tokens, padded, *refs),
        out_shape=sums_shape,
        in_specs=[in_vmem] * 4,
        out_specs=in_vmem,
        compiler_params=pltpu.CompilerParams(vmem_limit_bytes=24 * MIB),
        cost_estimate=work(10),
        name="attend_early",
    )(kept, early_keys, early_other, early_queries)

    late_keys, late_queries = gather(late, "gather_late", after=(early_sums,))
    late_other = trade(late_keys, 1)
    early_sums, late_sums = pl.pallas_call(
        lambda *refs: attend_late_kernel(tokens, padded, *refs),
        out_shape=[
            sums_shape,
            shaped(heads, late_queries.shape[1], 2 * head_size, dtype=jnp.float32),
        ],
        in_specs=[in_vmem] * 7,
        out_specs=[in_vmem] * 2,
        compiler_params=pltpu.CompilerParams(vmem_limit_bytes=24 * MIB),
        cost_estimate=work(10),
        name="attend_late",
    )(kept, early_keys, early_other, late_keys, early_queries, early_sums, late_queries)
    result = pl.pallas_call(
        lambda *refs: complete_kernel(tokens, [0] + early + late, *refs),
        out_shape=shaped(outers, heads, padded, head_size),
        in_specs=[in_smem] + [in_vmem] * 5,
        out_specs=in_vmem,
        compiler_params=pltpu.CompilerParams(vmem_limit_bytes=24 * MIB),
        name="complete",
    )(me, late_other, early_queries, early_sums, late_queries, late_sums)

    returned = lax.all_to_all(
        result,
        "seq",
        split_axis=0,
        concat_axis=0,
        tiled=True,
        axis_index_groups=[list(range(core, seq_count, INNER)) for core in range(INNER)],
    )

    return pl.pallas_call(
        lambda *refs: finish_kernel(per_group, *refs),
        out_shape=jax.ShapeDtypeStruct((tokens, row_width), attn_cache.dtype),
        in_specs=[in_vmem] * 3,
        out_specs=in_vmem,
        compiler_params=pltpu.CompilerParams(vmem_limit_bytes=24 * MIB),
        name="finish",
    )(padded_slots, returned, attn_cache)


def solution(mesh):
    return jax.shard_map(
        shards,
        mesh=mesh,
        in_specs=(
            P(("parts", "seq"), None, None),
            P(("parts", "seq")),
            P(("parts", "seq"), None),
            P(("parts", "seq"), None),
            P(("parts", "seq"), None),
            P("parts", None),
            P("parts", None),
            P(),
            P(),
        ),
        out_specs=P(("parts", "seq"), None),
        check_vma=False,
    )
```

```python
import math

import jax
import jax.numpy as jnp
from jax import lax
from jax.experimental import pallas as pl
from jax.experimental.pallas import tpu as pltpu
from jax.sharding import PartitionSpec as P

LOG2E = math.log2(math.e)
FIRST_HEADS = [15, 14, 13, 1]


def round_up(count, step):
    return (count + step - 1) // step * step


def normalize(entries, scales):
    mean_square = jnp.mean(entries * entries, axis=-1, keepdims=True)
    return entries * lax.rsqrt(mean_square + 1e-06) * scales


def place(slots, tokens):
    owner = lax.broadcasted_iota(jnp.int32, (tokens, slots.shape[1]), 0)
    return owner == slots


def prepare_kernel(per_group, padded, highs, by_head, me_ref, slots_ref, q_gain_ref, k_gain_ref, *rest):
    tokens = 0
    if by_head:
        groups = slots_ref.shape[1] // per_group
        loads = [rest[3 * turn : 3 * turn + 3] for turn in range(len(highs))]
        outs = rest[3 * len(highs) : 3 * len(highs) + groups * len(highs)]
        queries_ref = rest[-1]
        tokens = loads[0][1].shape[0]
    else:
        groups = slots_ref.shape[1] // per_group
        qkv_ref, k_ref, v_ref, text_k_ref, text_v_ref = rest[:5]
        rest = rest[6:]
        outs = rest[: groups * len(highs)]
        text_keys_ref, text_values_ref, queries_ref = rest[groups * len(highs) :]
        tokens = k_ref.shape[0]
    head_size = q_gain_ref.shape[1]
    me = me_ref[0]
    mine = place(slots_ref[...], tokens)
    is_fresh = jnp.max(mine.astype(jnp.float32), axis=1, keepdims=True) > 0.5
    one_hot = mine.astype(jnp.bfloat16)
    q_gain = q_gain_ref[...]
    k_gain = k_gain_ref[...]

    def merged(fresh, cache):
        spread = jnp.dot(one_hot, fresh, preferred_element_type=jnp.float32)
        return jnp.where(is_fresh, spread, cache.astype(jnp.float32))

    for turn, high in enumerate(highs):
        if by_head:
            fresh_ref, cache_k_ref, cache_v_ref = loads[turn]
            fresh = [fresh_ref[part] for part in range(3)]
            cache_k, cache_v = cache_k_ref[...], cache_v_ref[...]
        else:
            head = lax.bitwise_xor(me // groups, high)
            columns = pl.ds(pl.multiple_of(head * head_size, head_size), head_size)
            fresh = [qkv_ref[part, :, columns] for part in range(3)]
            cache_k, cache_v = k_ref[:, columns], v_ref[:, columns]
        keys = normalize(merged(fresh[1], cache_k), k_gain).astype(jnp.bfloat16)
        values = merged(fresh[2], cache_v).astype(jnp.bfloat16)
        queries = normalize(fresh[0].astype(jnp.float32), q_gain)
        empty = jnp.zeros((padded - per_group, head_size), jnp.float32)
        for group in range(groups):
            share = queries[group * per_group : (group + 1) * per_group]
            if padded > per_group:
                share = jnp.concatenate([share, empty], axis=0)
            queries_ref[group] = share.astype(jnp.bfloat16)
        for low in range(groups):
            out_ref = outs[turn * groups + low]
            group = lax.bitwise_xor(me % groups, low)
            out_ref[:tokens] = keys
            out_ref[tokens : 2 * tokens] = values
            out_ref[2 * tokens :] = queries_ref[group]
    if not by_head:
        text_keys = normalize(text_k_ref[...].astype(jnp.float32), k_gain)
        text_keys_ref[...] = text_keys.astype(jnp.bfloat16)
        text_values_ref[...] = text_v_ref[...]


def attend_kernel(tokens, query_rows, key_rows, steps, me_ref, *rest):
    me = me_ref[0]
    count = len(steps)
    arrived = rest[:count]
    text_keys_ref, text_values_ref = rest[count : count + 2]
    out_ref, queries_ref, keys_ref, values_ref, weights_ref, result_ref = rest[count + 2 :]
    head_size = text_keys_ref.shape[1]
    padded = arrived[0].shape[0] - 2 * tokens
    factor = head_size ** (-0.5) * LOG2E
    text = text_keys_ref.shape[0]
    keys_ref[:text] = text_keys_ref[...]
    values_ref[:text, :head_size] = text_values_ref[...]
    values_ref[:, head_size:] = jnp.ones((values_ref.shape[0], head_size), jnp.bfloat16)
    for step in range(count):
        first = text + step * tokens
        keys_ref[first : first + tokens] = arrived[step][:tokens]
        values_ref[first : first + tokens, :head_size] = arrived[step][tokens : 2 * tokens]
        queries_ref[step * padded : (step + 1) * padded] = arrived[step][2 * tokens :]

    def add_queries(step, carry):
        mine = pl.ds(pl.multiple_of(step * query_rows, 16), query_rows)
        queries = queries_ref[mine]
        for first in range(0, keys_ref.shape[0], key_rows):
            scores = lax.dot_general(
                queries,
                keys_ref[first : first + key_rows],
                (((1,), (1,)), ((), ())),
                preferred_element_type=jnp.float32,
            )
            weights_ref[:, first : first + key_rows] = jnp.exp2(scores * factor).astype(
                jnp.bfloat16
            )
        sums = jnp.dot(weights_ref[...], values_ref[...], preferred_element_type=jnp.float32)
        result_ref[mine] = (sums[:, :head_size] / sums[:, head_size:]).astype(jnp.bfloat16)
        return carry

    lax.fori_loop(0, queries_ref.shape[0] // query_rows, add_queries, 0)
    for step in range(count):
        owner = lax.bitwise_xor(me, steps[step])
        out_ref[owner] = result_ref[step * padded : (step + 1) * padded]


def finish_kernel(per_group, slots_ref, returned_ref, cache_ref, out_ref):
    tokens = cache_ref.shape[0]
    head_size = returned_ref.shape[2]
    groups = slots_ref.shape[0]
    heads = cache_ref.shape[1] // head_size
    mine = [place(slots_ref[group : group + 1], tokens) for group in range(groups)]
    count = sum(jnp.sum(m.astype(jnp.float32), axis=1, keepdims=True) for m in mine)
    is_fresh = count > 0.5
    one_hot = [m.astype(jnp.bfloat16) for m in mine]
    for head in range(heads):
        columns = slice(head * head_size, (head + 1) * head_size)
        placed = sum(
            jnp.dot(
                one_hot[group],
                returned_ref[head * groups + group],
                preferred_element_type=jnp.float32,
            )
            for group in range(groups)
        )
        out_ref[:, columns] = jnp.where(
            is_fresh, placed, cache_ref[:, columns].astype(jnp.float32)
        ).astype(out_ref.dtype)


def whole(shape):
    return pl.BlockSpec(shape, lambda i, me: (0,) * len(shape))


def partners(count):
    half = count // 2
    far = list(reversed(range(half, count)))
    near = list(reversed(range(1, half)))
    order = far[:3]
    for turn in range(max(len(far) - 3, len(near))):
        order += near[turn : turn + 1] + far[turn + 3 : turn + 4]
    names = sorted(range(count - 1), key=lambda number: str(number) if number else "")
    return [0] + [order[names.index(number)] for number in range(count - 1)]


def trade(block, step):
    if step == 0:
        return block
    count = lax.axis_size("seq")
    return lax.ppermute(block, "seq", [(a, a ^ step) for a in range(count)])


def shards(fresh_qkv, slot_rows, k_cache, v_cache, attn_cache, text_k, text_v, q_gain, k_gain):
    seq_count = lax.axis_size("seq")
    me = lax.axis_index("seq").reshape(1)
    slot_count = slot_rows.shape[0]
    tokens, row_width = k_cache.shape
    text = text_k.shape[0]
    head_size = q_gain.shape[0]
    head_count = row_width // head_size
    groups = seq_count // head_count
    per_group = slot_count // groups
    padded = round_up(per_group, 16)
    rows = 2 * tokens + padded
    q_gain = q_gain.reshape(1, head_size)
    k_gain = k_gain.reshape(1, head_size)
    qkv = jnp.transpose(fresh_qkv, (1, 0, 2))
    slots = slot_rows.reshape(1, slot_count)
    padded_slots = jnp.pad(
        slot_rows.reshape(groups, per_group),
        ((0, 0), (0, padded - per_group)),
        constant_values=tokens,
    )

    steps = partners(seq_count)
    block = jax.ShapeDtypeStruct((rows, head_size), jnp.bfloat16)
    text_block = jax.ShapeDtypeStruct((text, head_size), jnp.bfloat16)
    scratch = [pltpu.VMEM((groups, padded, head_size), jnp.bfloat16)]
    common = [whole((1, slot_count)), whole((1, head_size)), whole((1, head_size))]
    early = FIRST_HEADS
    late = [high for high in reversed(range(head_count)) if high not in early]

    def head_specs(high):
        def column(me):
            return lax.bitwise_xor(me[0] // groups, high)

        return [
            pl.BlockSpec((3, slot_count, head_size), lambda i, me: (0, 0, column(me))),
            pl.BlockSpec((tokens, head_size), lambda i, me: (0, column(me))),
            pl.BlockSpec((tokens, head_size), lambda i, me: (0, column(me))),
        ]

    first = pl.pallas_call(
        lambda *refs: prepare_kernel(per_group, padded, early, True, *refs),
        out_shape=[block] * (groups * len(early)),
        grid_spec=pltpu.PrefetchScalarGridSpec(
            num_scalar_prefetch=1,
            grid=(1,),
            in_specs=common + [spec for high in early for spec in head_specs(high)],
            out_specs=[whole((rows, head_size))] * (groups * len(early)),
            scratch_shapes=scratch,
        ),
        name="prepare_first",
    )(me, slots, q_gain, k_gain, *([qkv, k_cache, v_cache] * len(early)))
    met = {}
    for turn, made in enumerate(first):
        step = early[turn // groups] * groups + turn % groups
        met[step] = trade(made, step)
    text_spec = pl.BlockSpec((text, head_size), lambda i, me: (0, me[0] // groups))
    *second, text_keys, text_values = pl.pallas_call(
        lambda *refs: prepare_kernel(per_group, padded, late, False, *refs),
        out_shape=[block] * (groups * len(late)) + [text_block] * 2,
        grid_spec=pltpu.PrefetchScalarGridSpec(
            num_scalar_prefetch=1,
            grid=(1,),
            in_specs=common
            + [
                whole((3, slot_count, row_width)),
                whole((tokens, row_width)),
                whole((tokens, row_width)),
                text_spec,
                text_spec,
                pl.BlockSpec(memory_space=pl.ANY),
            ],
            out_specs=[whole((rows, head_size))] * (groups * len(late))
            + [whole((text, head_size))] * 2,
            scratch_shapes=scratch,
        ),
        compiler_params=pltpu.CompilerParams(vmem_limit_bytes=24 * 2**20),
        name="prepare_rest",
    )(me, slots, q_gain, k_gain, qkv, k_cache, v_cache, text_k, text_v, met[groups])
    arrived = dict(met)
    for turn, made in enumerate(second):
        step = late[turn // groups] * groups + turn % groups
        arrived[step] = trade(made, step)
    arrived = [arrived[step] for step in steps]

    query_rows = 4 * padded
    all_keys = text + seq_count * tokens
    result = pl.pallas_call(
        lambda *refs: attend_kernel(tokens, query_rows, 256, steps, *refs),
        out_shape=jax.ShapeDtypeStruct((seq_count, padded, head_size), jnp.bfloat16),
        grid_spec=pltpu.PrefetchScalarGridSpec(
            num_scalar_prefetch=1,
            grid=(1,),
            in_specs=[whole((rows, head_size))] * seq_count
            + [whole((text, head_size))] * 2,
            out_specs=whole((seq_count, padded, head_size)),
            scratch_shapes=[
                pltpu.VMEM((seq_count * padded, head_size), jnp.bfloat16),
                pltpu.VMEM((all_keys, head_size), jnp.bfloat16),
                pltpu.VMEM((all_keys, 2 * head_size), jnp.bfloat16),
                pltpu.VMEM((query_rows, all_keys), jnp.bfloat16),
                pltpu.VMEM((seq_count * padded, head_size), jnp.bfloat16),
            ],
        ),
        compiler_params=pltpu.CompilerParams(vmem_limit_bytes=40 * 2**20),
        name="attend",
    )(me, *arrived, text_keys, text_values)

    returned = lax.all_to_all(result, "seq", split_axis=0, concat_axis=0, tiled=True)

    finish_steps = 1
    return pl.pallas_call(
        lambda *refs: finish_kernel(per_group, *refs),
        out_shape=jax.ShapeDtypeStruct((tokens, row_width), attn_cache.dtype),
        grid=(finish_steps,),
        in_specs=[
            pl.BlockSpec((groups, padded), lambda i: (0, 0)),
            pl.BlockSpec((seq_count // finish_steps, padded, head_size), lambda i: (i, 0, 0)),
            pl.BlockSpec((tokens, row_width // finish_steps), lambda i: (0, i)),
        ],
        out_specs=pl.BlockSpec((tokens, row_width // finish_steps), lambda i: (0, i)),
        compiler_params=pltpu.CompilerParams(vmem_limit_bytes=32 * 2**20),
        name="finish",
    )(padded_slots, returned, attn_cache)


def solution(mesh):
    return jax.shard_map(
        shards,
        mesh=mesh,
        in_specs=(
            P(("parts", "seq"), None, None),
            P(("parts", "seq")),
            P(("parts", "seq"), None),
            P(("parts", "seq"), None),
            P(("parts", "seq"), None),
            P("parts", None),
            P("parts", None),
            P(),
            P(),
        ),
        out_specs=P(("parts", "seq"), None),
        check_vma=False,
    )
```

```python
import math

import jax
import jax.numpy as jnp
from jax import lax
from jax.experimental import pallas as pl
from jax.experimental.pallas import tpu as pltpu
from jax.sharding import PartitionSpec as P

LOG2E = math.log2(math.e)
INNER = 2
MIB = 2**20


def round_up(count, step):
    return (count + step - 1) // step * step


def normalize(entries, scales):
    mean_square = jnp.mean(entries * entries, axis=-1, keepdims=True)
    return entries * lax.rsqrt(mean_square + 1e-06) * scales


def place(slots, tokens):
    owner = lax.broadcasted_iota(jnp.int32, (tokens, slots.shape[1]), 0)
    return owner == slots


def prepare_kernel(plan, groups, per_group, padded, with_text, me_ref, *refs):
    slots_hbm, q_gain_hbm, k_gain_hbm, qkv_hbm, k_hbm, v_hbm = refs[:6]
    rest = refs[6:]
    if with_text:
        text_k_hbm, text_v_hbm = rest[:2]
        rest = rest[3:]
    outs = []
    for _, apart in plan:
        taken = 2 if apart else 1
        outs.append(rest[:taken])
        rest = rest[taken:]
    if with_text:
        text_keys_ref, text_values_ref = rest[:2]
        rest = rest[2:]
    slots_ref, q_gain_ref, k_gain_ref, fresh_ref, k_ref, v_ref, text_ref, share_ref = rest[:8]
    small_sems, sems, text_sems = rest[8:]
    tokens, width = k_ref.shape[1:]
    head_size = q_gain_ref.shape[1]
    outer = me_ref[0] // INNER

    def columns(step):
        block = lax.bitwise_xor(outer // groups, step // groups)
        return pl.ds(pl.multiple_of(block * width, width), width)

    small = [
        pltpu.make_async_copy(slots_hbm, slots_ref, small_sems.at[0]),
        pltpu.make_async_copy(q_gain_hbm, q_gain_ref, small_sems.at[1]),
        pltpu.make_async_copy(k_gain_hbm, k_gain_ref, small_sems.at[2]),
    ]
    for copy in small:
        copy.start()
    loads = []
    for turn, (step, _) in enumerate(plan):
        mine = columns(step)
        loads.append(
            [
                pltpu.make_async_copy(
                    qkv_hbm.at[:, :, mine], fresh_ref.at[turn], sems.at[turn, 0]
                ),
                pltpu.make_async_copy(k_hbm.at[:, mine], k_ref.at[turn], sems.at[turn, 1]),
                pltpu.make_async_copy(v_hbm.at[:, mine], v_ref.at[turn], sems.at[turn, 2]),
            ]
        )
        for copy in loads[-1]:
            copy.start()
    if with_text:
        mine = columns(0)
        text_loads = [
            pltpu.make_async_copy(text_k_hbm.at[:, mine], text_ref.at[0], text_sems.at[0]),
            pltpu.make_async_copy(text_v_hbm.at[:, mine], text_ref.at[1], text_sems.at[1]),
        ]
        for copy in text_loads:
            copy.start()
    for copy in small:
        copy.wait()
    belongs = place(slots_ref[...], tokens)
    is_fresh = jnp.max(belongs.astype(jnp.float32), axis=1, keepdims=True) > 0.5
    one_hot = belongs.astype(jnp.bfloat16)
    q_gain = q_gain_ref[...]
    k_gain = k_gain_ref[...]

    def merged(fresh, cache):
        spread = jnp.dot(one_hot, fresh, preferred_element_type=jnp.float32)
        return jnp.where(is_fresh, spread, cache.astype(jnp.float32))

    for turn, (step, apart) in enumerate(plan):
        for copy in loads[turn]:
            copy.wait()
        group = lax.bitwise_xor(outer % groups, step % groups)
        for head in range(width // head_size):
            lanes = slice(head * head_size, (head + 1) * head_size)
            keys = normalize(merged(fresh_ref[turn, 1, :, lanes], k_ref[turn, :, lanes]), k_gain)
            values = merged(fresh_ref[turn, 2, :, lanes], v_ref[turn, :, lanes])
            queries = normalize(fresh_ref[turn, 0, :, lanes].astype(jnp.float32), q_gain)
            for part in range(groups):
                share = queries[part * per_group : (part + 1) * per_group]
                if padded > per_group:
                    empty = jnp.zeros((padded - per_group, head_size), jnp.float32)
                    share = jnp.concatenate([share, empty], axis=0)
                share_ref[part] = share.astype(jnp.bfloat16)
            outs[turn][0][head, :tokens] = keys.astype(jnp.bfloat16)
            outs[turn][0][head, tokens : 2 * tokens] = values.astype(jnp.bfloat16)
            if apart:
                outs[turn][1][head] = share_ref[group]
            else:
                outs[turn][0][head, 2 * tokens :] = share_ref[group]
    if with_text:
        for copy in text_loads:
            copy.wait()
        for head in range(width // head_size):
            lanes = slice(head * head_size, (head + 1) * head_size)
            text_keys = normalize(text_ref[0, :, lanes].astype(jnp.float32), k_gain)
            text_keys_ref[head] = text_keys.astype(jnp.bfloat16)
            text_values_ref[head] = text_ref[1, :, lanes]


def gather_kernel(tokens, extra, count, *refs):
    blocks, refs = refs[:count], refs[count:]
    if extra:
        own, other, text_keys, text_values, own_queries = refs[:5]
        refs = refs[5:]
        kept_ref = refs[2]
        text = text_keys.shape[1]
        for number, block in enumerate([own, other]):
            rows = slice(text + number * tokens, text + (number + 1) * tokens)
            kept_ref[:, 0, rows] = block[:, :tokens]
            kept_ref[:, 1, rows] = block[:, tokens:]
        kept_ref[:, 0, :text] = text_keys[...]
        kept_ref[:, 1, :text] = text_values[...]
        parts = [own_queries[...]]
    else:
        parts = []
    out_ref, queries_ref = refs[:2]
    for number, block in enumerate(blocks):
        rows = slice(number * tokens, (number + 1) * tokens)
        out_ref[:, 0, rows] = block[:, :tokens]
        out_ref[:, 1, rows] = block[:, tokens : 2 * tokens]
        parts.append(block[:, 2 * tokens :])
    padded = parts[0].shape[1]
    for number, part in enumerate(parts):
        queries_ref[:, number * padded : (number + 1) * padded] = part


def add_keys(sums, queries, keys, values):
    factor = queries.shape[1] ** (-0.5) * LOG2E
    scores = lax.dot_general(
        queries, keys, (((1,), (1,)), ((), ())), preferred_element_type=jnp.float32
    )
    weights = jnp.exp2(scores * factor).astype(jnp.bfloat16)
    beside = jnp.concatenate([values, jnp.ones_like(values)], axis=1)
    added = jnp.dot(weights, beside, preferred_element_type=jnp.float32)
    return added if sums is None else sums + added


def add_shared(sums, queries, shared, head, tokens):
    for ref in shared:
        rows = ref.shape[2]
        chunk = next(c * tokens for c in (4, 3, 2, 1) if rows % (c * tokens) == 0)
        for first in range(0, rows, chunk):
            at = slice(first, first + chunk)
            sums = add_keys(sums, queries, ref[head, 0, at], ref[head, 1, at])
    return sums


def row_blocks(ref, padded):
    rows = ref.shape[1]
    return [slice(first, min(first + 4 * padded, rows)) for first in range(0, rows, 4 * padded)]


def attend_kernel(tokens, padded, *refs):
    shared, queries_ref, sums_ref = refs[:-2], refs[-2], refs[-1]
    for head in range(queries_ref.shape[0]):
        for rows in row_blocks(queries_ref, padded):
            sums_ref[head, rows] = add_shared(None, queries_ref[head, rows], shared, head, tokens)


def complete_kernel(tokens, first, shared_ref, queries_ref, sums_ref, *outs):
    heads, padded, head_size = outs[0].shape
    for head in range(heads):
        for number in range(0, len(outs), 4):
            mine = outs[number : number + 4]
            at = (first + number) * padded
            rows = slice(at, at + len(mine) * padded)
            sums = add_shared(
                sums_ref[head, rows], queries_ref[head, rows], [shared_ref], head, tokens
            )
            result = (sums[:, :head_size] / sums[:, head_size:]).astype(jnp.bfloat16)
            for turn, out_ref in enumerate(mine):
                out_ref[head] = result[turn * padded : (turn + 1) * padded]


def finish_kernel(heads, steps, me_ref, slots_ref, cache_ref, *rest):
    returned, out_ref = rest[:-1], rest[-1]
    tokens = cache_ref.shape[0]
    head_size = returned[0].shape[2]
    groups = slots_ref.shape[0]
    outer = me_ref[0] // INNER
    one_hot = []
    owned = jnp.zeros((tokens, 1), jnp.float32)
    for low in range(groups):
        group = lax.bitwise_xor(outer % groups, low)
        mine = place(slots_ref[pl.ds(group, 1)], tokens).astype(jnp.float32)
        owned = owned + jnp.sum(mine, axis=1, keepdims=True)
        one_hot.append(mine.astype(jnp.bfloat16))
    is_fresh = owned > 0.5
    for high in range(len(steps) // groups):
        block = lax.bitwise_xor(outer // groups, high)
        for head in range(heads):
            at = (block * heads + head) * head_size
            columns = pl.ds(pl.multiple_of(at, head_size), head_size)
            placed = jnp.zeros((tokens, head_size), jnp.float32)
            for low in range(groups):
                made = returned[steps.index(high * groups + low)][head]
                placed = placed + jnp.dot(one_hot[low], made, preferred_element_type=jnp.float32)
            out_ref[:, columns] = jnp.where(
                is_fresh, placed, cache_ref[:, columns].astype(jnp.float32)
            ).astype(out_ref.dtype)


def work(micros):
    return pl.CostEstimate(
        flops=int(micros * 1e9), bytes_accessed=int(micros * 3e6), transcendentals=0
    )


def trade(block, distance):
    count = lax.axis_size("seq")
    return lax.ppermute(block, "seq", [(a, a ^ distance) for a in range(count)])


def shards(fresh_qkv, slot_rows, k_cache, v_cache, attn_cache, text_k, text_v, q_gain, k_gain):
    seq_count = lax.axis_size("seq")
    me = lax.axis_index("seq").reshape(1)
    slot_count = slot_rows.shape[0]
    tokens, row_width = k_cache.shape
    text = text_k.shape[0]
    head_size = q_gain.shape[0]
    outers = seq_count // INNER
    all_heads = row_width // head_size
    heads = max(1, all_heads // outers)
    groups = outers * heads // all_heads
    per_group = slot_count // groups
    padded = round_up(per_group, 16)
    width = heads * head_size
    qkv = jnp.transpose(fresh_qkv, (1, 0, 2))
    q_gain = q_gain.reshape(1, head_size)
    k_gain = k_gain.reshape(1, head_size)
    slots = slot_rows.reshape(1, slot_count)
    padded_slots = jnp.pad(
        slot_rows.reshape(groups, per_group),
        ((0, 0), (0, padded - per_group)),
        constant_values=tokens,
    )

    def shaped(*shape, dtype=jnp.bfloat16):
        return jax.ShapeDtypeStruct(shape, dtype)

    in_hbm = pl.BlockSpec(memory_space=pltpu.HBM)
    in_vmem = pl.BlockSpec(memory_space=pltpu.VMEM)
    in_smem = pl.BlockSpec(memory_space=pltpu.SMEM)

    def prepare(plan, with_text, name, params, *extra):
        shapes = []
        for _, apart in plan:
            if apart:
                shapes += [shaped(heads, 2 * tokens, head_size), shaped(heads, padded, head_size)]
            else:
                shapes += [shaped(heads, 2 * tokens + padded, head_size)]
        if with_text:
            shapes += [shaped(heads, text, head_size)] * 2
        made = pl.pallas_call(
            lambda *refs: prepare_kernel(plan, groups, per_group, padded, with_text, *refs),
            out_shape=shapes,
            in_specs=[in_smem] + [in_hbm] * 6 + [in_hbm] * (2 * with_text)
            + [pl.BlockSpec(memory_space=pl.ANY)] * with_text,
            out_specs=[in_vmem] * len(shapes),
            scratch_shapes=[
                pltpu.VMEM((1, slot_count), jnp.int32),
                pltpu.VMEM((1, head_size), jnp.float32),
                pltpu.VMEM((1, head_size), jnp.float32),
                pltpu.VMEM((len(plan), 3, slot_count, width), jnp.bfloat16),
                pltpu.VMEM((len(plan), tokens, width), jnp.bfloat16),
                pltpu.VMEM((len(plan), tokens, width), jnp.bfloat16),
                pltpu.VMEM((2, text, width), jnp.bfloat16),
                pltpu.VMEM((groups, padded, head_size), jnp.bfloat16),
                pltpu.SemaphoreType.DMA((3,)),
                pltpu.SemaphoreType.DMA((len(plan), 3)),
                pltpu.SemaphoreType.DMA((2,)),
            ],
            compiler_params=params,
            name=name,
        )(me, slots, q_gain, k_gain, qkv, k_cache, v_cache, *extra)
        return list(made)

    half = outers // 2
    far = list(reversed(range(half, outers)))
    near = list(range(1, half))
    small = pltpu.CompilerParams(vmem_limit_bytes=24 * MIB)
    block, own, own_queries = prepare(
        [(far[0], False), (0, True)], False, "prepare_first", pltpu.CompilerParams()
    )
    arrived = {far[0]: trade(block, far[0] * INNER)}
    other = trade(own, 1)

    late = far[1:2]
    for turn in range(half):
        late += near[turn : turn + 1] + far[turn + 2 : turn + 3]
    *made, text_keys, text_values = prepare(
        [(step, False) for step in late], True, "prepare_rest", small, text_k, text_v, other
    )
    for step, block in zip(late, made):
        arrived[step] = trade(block, step * INNER)

    steps = [far[0]] + late
    count = len(steps) + 1
    keys, queries, kept = pl.pallas_call(
        lambda *refs: gather_kernel(tokens, True, len(steps), *refs),
        out_shape=[
            shaped(heads, 2, len(steps) * tokens, head_size),
            shaped(heads, count * padded, head_size),
            shaped(heads, 2, text + 2 * tokens, head_size),
        ],
        in_specs=[in_vmem] * (len(steps) + 5),
        out_specs=[in_vmem] * 3,
        compiler_params=small,
        name="gather",
    )(*[arrived[step] for step in steps], own, other, text_keys, text_values, own_queries)
    other_keys = trade(keys, 1)
    sums = pl.pallas_call(
        lambda *refs: attend_kernel(tokens, padded, *refs),
        out_shape=shaped(heads, count * padded, 2 * head_size, dtype=jnp.float32),
        in_specs=[in_vmem] * 3,
        out_specs=in_vmem,
        compiler_params=small,
        cost_estimate=work(5),
        name="attend",
    )(kept, keys, queries)

    sources = [0] + steps

    def complete(first, last, name):
        return pl.pallas_call(
            lambda *refs: complete_kernel(tokens, first, *refs),
            out_shape=[shaped(heads, padded, head_size)] * (last - first),
            in_specs=[in_vmem] * 3,
            out_specs=[in_vmem] * (last - first),
            compiler_params=small,
            name=name,
        )(other_keys, queries, sums)

    results = dict(zip(sources, complete(0, count, "complete")))
    order = near[-1:] + far + near[:-1]
    returned = {0: results[0]}
    for step in order:
        returned[step] = trade(results[step], step * INNER)
    order = order + [0]

    return pl.pallas_call(
        lambda *refs: finish_kernel(heads, order, *refs),
        out_shape=jax.ShapeDtypeStruct((tokens, row_width), attn_cache.dtype),
        in_specs=[in_smem] + [in_vmem] * (2 + len(order)),
        out_specs=in_vmem,
        compiler_params=small,
        name="finish",
    )(me, padded_slots, attn_cache, *[returned[step] for step in order])


def solution(mesh):
    return jax.shard_map(
        shards,
        mesh=mesh,
        in_specs=(
            P(("parts", "seq"), None, None),
            P(("parts", "seq")),
            P(("parts", "seq"), None),
            P(("parts", "seq"), None),
            P(("parts", "seq"), None),
            P("parts", None),
            P("parts", None),
            P(),
            P(),
        ),
        out_specs=P(("parts", "seq"), None),
        check_vma=False,
    )
```

```python
import math

import jax
import jax.numpy as jnp
from jax import lax
from jax.experimental import pallas as pl
from jax.experimental.pallas import tpu as pltpu
from jax.sharding import PartitionSpec as P

LOG2E = math.log2(math.e)
FIRST_HEADS = [15, 14, 13, 1]


def round_up(count, step):
    return (count + step - 1) // step * step


def normalize(entries, scales):
    mean_square = jnp.mean(entries * entries, axis=-1, keepdims=True)
    return entries * lax.rsqrt(mean_square + 1e-06) * scales


def place(slots, tokens):
    owner = lax.broadcasted_iota(jnp.int32, (tokens, slots.shape[1]), 0)
    return owner == slots


def prepare_kernel(per_group, padded, highs, by_head, me_ref, slots_ref, q_gain_ref, k_gain_ref, *rest):
    tokens = 0
    if by_head:
        groups = slots_ref.shape[1] // per_group
        loads = [rest[3 * turn : 3 * turn + 3] for turn in range(len(highs))]
        outs = rest[3 * len(highs) : 3 * len(highs) + groups * len(highs)]
        queries_ref = rest[-1]
        tokens = loads[0][1].shape[0]
    else:
        groups = slots_ref.shape[1] // per_group
        qkv_ref, k_ref, v_ref, text_k_ref, text_v_ref = rest[:5]
        rest = rest[6:]
        outs = rest[: groups * len(highs)]
        text_keys_ref, text_values_ref, queries_ref = rest[groups * len(highs) :]
        tokens = k_ref.shape[0]
    head_size = q_gain_ref.shape[1]
    me = me_ref[0]
    mine = place(slots_ref[...], tokens)
    is_fresh = jnp.max(mine.astype(jnp.float32), axis=1, keepdims=True) > 0.5
    one_hot = mine.astype(jnp.bfloat16)
    q_gain = q_gain_ref[...]
    k_gain = k_gain_ref[...]

    def merged(fresh, cache):
        spread = jnp.dot(one_hot, fresh, preferred_element_type=jnp.float32)
        return jnp.where(is_fresh, spread, cache.astype(jnp.float32))

    for turn, high in enumerate(highs):
        if by_head:
            fresh_ref, cache_k_ref, cache_v_ref = loads[turn]
            fresh = [fresh_ref[part] for part in range(3)]
            cache_k, cache_v = cache_k_ref[...], cache_v_ref[...]
        else:
            head = lax.bitwise_xor(me // groups, high)
            columns = pl.ds(pl.multiple_of(head * head_size, head_size), head_size)
            fresh = [qkv_ref[part, :, columns] for part in range(3)]
            cache_k, cache_v = k_ref[:, columns], v_ref[:, columns]
        keys = normalize(merged(fresh[1], cache_k), k_gain).astype(jnp.bfloat16)
        values = merged(fresh[2], cache_v).astype(jnp.bfloat16)
        queries = normalize(fresh[0].astype(jnp.float32), q_gain)
        empty = jnp.zeros((padded - per_group, head_size), jnp.float32)
        for group in range(groups):
            share = queries[group * per_group : (group + 1) * per_group]
            if padded > per_group:
                share = jnp.concatenate([share, empty], axis=0)
            queries_ref[group] = share.astype(jnp.bfloat16)
        for low in range(groups):
            out_ref = outs[turn * groups + low]
            group = lax.bitwise_xor(me % groups, low)
            out_ref[:tokens] = keys
            out_ref[tokens : 2 * tokens] = values
            out_ref[2 * tokens :] = queries_ref[group]
    if not by_head:
        text_keys = normalize(text_k_ref[...].astype(jnp.float32), k_gain)
        text_keys_ref[...] = text_keys.astype(jnp.bfloat16)
        text_values_ref[...] = text_v_ref[...]


def attend_kernel(tokens, query_rows, key_rows, steps, me_ref, *rest):
    me = me_ref[0]
    count = len(steps)
    arrived = rest[:count]
    text_keys_ref, text_values_ref = rest[count : count + 2]
    out_ref, queries_ref, keys_ref, values_ref, result_ref = rest[count + 2 :]
    head_size = text_keys_ref.shape[1]
    padded = arrived[0].shape[0] - 2 * tokens
    factor = head_size ** (-0.5) * LOG2E
    text = text_keys_ref.shape[0]
    keys_ref[:text] = text_keys_ref[...]
    values_ref[:text] = text_values_ref[...]
    for step in range(count):
        first = text + step * tokens
        keys_ref[first : first + tokens] = arrived[step][:tokens]
        values_ref[first : first + tokens] = arrived[step][tokens : 2 * tokens]
        queries_ref[step * padded : (step + 1) * padded] = arrived[step][2 * tokens :]

    def add_queries(step, carry):
        first_row = step * query_rows
        mine = pl.ds(first_row if isinstance(step, int) else pl.multiple_of(first_row, 16), query_rows)
        queries = queries_ref[mine]
        sums = None
        for first in range(0, keys_ref.shape[0], key_rows):
            scores = lax.dot_general(
                queries,
                keys_ref[first : first + key_rows],
                (((1,), (1,)), ((), ())),
                preferred_element_type=jnp.float32,
            )
            weights = jnp.exp2(scores * factor).astype(jnp.bfloat16)
            values = values_ref[first : first + key_rows]
            beside = jnp.concatenate([values, jnp.ones_like(values)], axis=1)
            added = jnp.dot(weights, beside, preferred_element_type=jnp.float32)
            sums = added if sums is None else sums + added
        result_ref[mine] = (sums[:, :head_size] / sums[:, head_size:]).astype(jnp.bfloat16)
        return carry

    turns = queries_ref.shape[0] // query_rows
    if turns <= 4:
        for step in range(turns):
            add_queries(step, 0)
    else:
        lax.fori_loop(0, turns, add_queries, 0)
    for step in range(count):
        owner = lax.bitwise_xor(me, steps[step])
        out_ref[owner] = result_ref[step * padded : (step + 1) * padded]


def finish_kernel(per_group, slots_ref, returned_ref, cache_ref, out_ref):
    tokens = cache_ref.shape[0]
    head_size = returned_ref.shape[2]
    groups = slots_ref.shape[0]
    heads = cache_ref.shape[1] // head_size
    mine = [place(slots_ref[group : group + 1], tokens) for group in range(groups)]
    count = sum(jnp.sum(m.astype(jnp.float32), axis=1, keepdims=True) for m in mine)
    is_fresh = count > 0.5
    one_hot = [m.astype(jnp.bfloat16) for m in mine]
    for head in range(heads):
        columns = slice(head * head_size, (head + 1) * head_size)
        placed = sum(
            jnp.dot(
                one_hot[group],
                returned_ref[head * groups + group],
                preferred_element_type=jnp.float32,
            )
            for group in range(groups)
        )
        out_ref[:, columns] = jnp.where(
            is_fresh, placed, cache_ref[:, columns].astype(jnp.float32)
        ).astype(out_ref.dtype)


def whole(shape):
    return pl.BlockSpec(shape, lambda i, me: (0,) * len(shape))


def partners(count):
    half = count // 2
    far = list(reversed(range(half, count)))
    near = list(reversed(range(1, half)))
    order = far + near
    names = sorted(range(count - 1), key=lambda number: str(number) if number else "")
    return [0] + [order[names.index(number)] for number in range(count - 1)]


def trade(block, step):
    if step == 0:
        return block
    count = lax.axis_size("seq")
    return lax.ppermute(block, "seq", [(a, a ^ step) for a in range(count)])


def shards(fresh_qkv, slot_rows, k_cache, v_cache, attn_cache, text_k, text_v, q_gain, k_gain):
    seq_count = lax.axis_size("seq")
    me = lax.axis_index("seq").reshape(1)
    slot_count = slot_rows.shape[0]
    tokens, row_width = k_cache.shape
    text = text_k.shape[0]
    head_size = q_gain.shape[0]
    head_count = row_width // head_size
    groups = seq_count // head_count
    per_group = slot_count // groups
    padded = round_up(per_group, 16)
    rows = 2 * tokens + padded
    q_gain = q_gain.reshape(1, head_size)
    k_gain = k_gain.reshape(1, head_size)
    qkv = jnp.transpose(fresh_qkv, (1, 0, 2))
    slots = slot_rows.reshape(1, slot_count)
    padded_slots = jnp.pad(
        slot_rows.reshape(groups, per_group),
        ((0, 0), (0, padded - per_group)),
        constant_values=tokens,
    )

    steps = partners(seq_count)
    block = jax.ShapeDtypeStruct((rows, head_size), jnp.bfloat16)
    text_block = jax.ShapeDtypeStruct((text, head_size), jnp.bfloat16)
    scratch = [pltpu.VMEM((groups, padded, head_size), jnp.bfloat16)]
    common = [whole((1, slot_count)), whole((1, head_size)), whole((1, head_size))]
    early = FIRST_HEADS
    late = [high for high in reversed(range(head_count)) if high not in early]

    def head_specs(high):
        def column(me):
            return lax.bitwise_xor(me[0] // groups, high)

        return [
            pl.BlockSpec((3, slot_count, head_size), lambda i, me: (0, 0, column(me))),
            pl.BlockSpec((tokens, head_size), lambda i, me: (0, column(me))),
            pl.BlockSpec((tokens, head_size), lambda i, me: (0, column(me))),
        ]

    first = pl.pallas_call(
        lambda *refs: prepare_kernel(per_group, padded, early, True, *refs),
        out_shape=[block] * (groups * len(early)),
        grid_spec=pltpu.PrefetchScalarGridSpec(
            num_scalar_prefetch=1,
            grid=(1,),
            in_specs=common + [spec for high in early for spec in head_specs(high)],
            out_specs=[whole((rows, head_size))] * (groups * len(early)),
            scratch_shapes=scratch,
        ),
        name="prepare_first",
    )(me, slots, q_gain, k_gain, *([qkv, k_cache, v_cache] * len(early)))
    met = {}
    for turn, made in enumerate(first):
        step = early[turn // groups] * groups + turn % groups
        met[step] = trade(made, step)
    text_spec = pl.BlockSpec((text, head_size), lambda i, me: (0, me[0] // groups))
    *second, text_keys, text_values = pl.pallas_call(
        lambda *refs: prepare_kernel(per_group, padded, late, False, *refs),
        out_shape=[block] * (groups * len(late)) + [text_block] * 2,
        grid_spec=pltpu.PrefetchScalarGridSpec(
            num_scalar_prefetch=1,
            grid=(1,),
            in_specs=common
            + [
                whole((3, slot_count, row_width)),
                whole((tokens, row_width)),
                whole((tokens, row_width)),
                text_spec,
                text_spec,
                pl.BlockSpec(memory_space=pl.ANY),
            ],
            out_specs=[whole((rows, head_size))] * (groups * len(late))
            + [whole((text, head_size))] * 2,
            scratch_shapes=scratch,
        ),
        compiler_params=pltpu.CompilerParams(vmem_limit_bytes=24 * 2**20),
        name="prepare_rest",
    )(me, slots, q_gain, k_gain, qkv, k_cache, v_cache, text_k, text_v, met[groups])
    arrived = dict(met)
    for turn, made in enumerate(second):
        step = late[turn // groups] * groups + turn % groups
        arrived[step] = trade(made, step)
    arrived = [arrived[step] for step in steps]

    query_rows = 4 * padded
    all_keys = text + seq_count * tokens
    result = pl.pallas_call(
        lambda *refs: attend_kernel(tokens, query_rows, 768, steps, *refs),
        out_shape=jax.ShapeDtypeStruct((seq_count, padded, head_size), jnp.bfloat16),
        grid_spec=pltpu.PrefetchScalarGridSpec(
            num_scalar_prefetch=1,
            grid=(1,),
            in_specs=[whole((rows, head_size))] * seq_count
            + [whole((text, head_size))] * 2,
            out_specs=whole((seq_count, padded, head_size)),
            scratch_shapes=[
                pltpu.VMEM((seq_count * padded, head_size), jnp.bfloat16),
                pltpu.VMEM((all_keys, head_size), jnp.bfloat16),
                pltpu.VMEM((all_keys, head_size), jnp.bfloat16),
                pltpu.VMEM((seq_count * padded, head_size), jnp.bfloat16),
            ],
        ),
        compiler_params=pltpu.CompilerParams(vmem_limit_bytes=40 * 2**20),
        name="attend",
    )(me, *arrived, text_keys, text_values)

    returned = lax.all_to_all(result, "seq", split_axis=0, concat_axis=0, tiled=True)

    finish_steps = 1
    return pl.pallas_call(
        lambda *refs: finish_kernel(per_group, *refs),
        out_shape=jax.ShapeDtypeStruct((tokens, row_width), attn_cache.dtype),
        grid=(finish_steps,),
        in_specs=[
            pl.BlockSpec((groups, padded), lambda i: (0, 0)),
            pl.BlockSpec((seq_count // finish_steps, padded, head_size), lambda i: (i, 0, 0)),
            pl.BlockSpec((tokens, row_width // finish_steps), lambda i: (0, i)),
        ],
        out_specs=pl.BlockSpec((tokens, row_width // finish_steps), lambda i: (0, i)),
        compiler_params=pltpu.CompilerParams(vmem_limit_bytes=32 * 2**20),
        name="finish",
    )(padded_slots, returned, attn_cache)


def solution(mesh):
    return jax.shard_map(
        shards,
        mesh=mesh,
        in_specs=(
            P(("parts", "seq"), None, None),
            P(("parts", "seq")),
            P(("parts", "seq"), None),
            P(("parts", "seq"), None),
            P(("parts", "seq"), None),
            P("parts", None),
            P("parts", None),
            P(),
            P(),
        ),
        out_specs=P(("parts", "seq"), None),
        check_vma=False,
    )
```

```python
import math

import jax
import jax.numpy as jnp
from jax import lax
from jax.experimental import pallas as pl
from jax.experimental.pallas import tpu as pltpu
from jax.sharding import PartitionSpec as P

LOG2E = math.log2(math.e)
FIRST_HEADS = [15, 14, 13, 1]


def round_up(count, step):
    return (count + step - 1) // step * step


def normalize(entries, scales):
    mean_square = jnp.mean(entries * entries, axis=-1, keepdims=True)
    return entries * lax.rsqrt(mean_square + 1e-06) * scales


def place(slots, tokens):
    owner = lax.broadcasted_iota(jnp.int32, (tokens, slots.shape[1]), 0)
    return owner == slots


def prepare_kernel(per_group, padded, highs, by_head, me_ref, slots_ref, q_gain_ref, k_gain_ref, *rest):
    tokens = 0
    if by_head:
        groups = slots_ref.shape[1] // per_group
        loads = [rest[3 * turn : 3 * turn + 3] for turn in range(len(highs))]
        outs = rest[3 * len(highs) : 3 * len(highs) + groups * len(highs)]
        queries_ref = rest[-1]
        tokens = loads[0][1].shape[0]
    else:
        groups = slots_ref.shape[1] // per_group
        qkv_ref, k_ref, v_ref, text_k_ref, text_v_ref = rest[:5]
        rest = rest[6:]
        outs = rest[: groups * len(highs)]
        text_keys_ref, text_values_ref, queries_ref = rest[groups * len(highs) :]
        tokens = k_ref.shape[0]
    head_size = q_gain_ref.shape[1]
    me = me_ref[0]
    mine = place(slots_ref[...], tokens)
    is_fresh = jnp.max(mine.astype(jnp.float32), axis=1, keepdims=True) > 0.5
    one_hot = mine.astype(jnp.bfloat16)
    q_gain = q_gain_ref[...]
    k_gain = k_gain_ref[...]

    def merged(fresh, cache):
        spread = jnp.dot(one_hot, fresh, preferred_element_type=jnp.float32)
        return jnp.where(is_fresh, spread, cache.astype(jnp.float32))

    for turn, high in enumerate(highs):
        if by_head:
            fresh_ref, cache_k_ref, cache_v_ref = loads[turn]
            fresh = [fresh_ref[part] for part in range(3)]
            cache_k, cache_v = cache_k_ref[...], cache_v_ref[...]
        else:
            head = lax.bitwise_xor(me // groups, high)
            columns = pl.ds(pl.multiple_of(head * head_size, head_size), head_size)
            fresh = [qkv_ref[part, :, columns] for part in range(3)]
            cache_k, cache_v = k_ref[:, columns], v_ref[:, columns]
        keys = normalize(merged(fresh[1], cache_k), k_gain).astype(jnp.bfloat16)
        values = merged(fresh[2], cache_v).astype(jnp.bfloat16)
        queries = normalize(fresh[0].astype(jnp.float32), q_gain)
        empty = jnp.zeros((padded - per_group, head_size), jnp.float32)
        for group in range(groups):
            share = queries[group * per_group : (group + 1) * per_group]
            if padded > per_group:
                share = jnp.concatenate([share, empty], axis=0)
            queries_ref[group] = share.astype(jnp.bfloat16)
        for low in range(groups):
            out_ref = outs[turn * groups + low]
            group = lax.bitwise_xor(me % groups, low)
            out_ref[:tokens] = keys
            out_ref[tokens : 2 * tokens] = values
            out_ref[2 * tokens :] = queries_ref[group]
    if not by_head:
        text_keys = normalize(text_k_ref[...].astype(jnp.float32), k_gain)
        text_keys_ref[...] = text_keys.astype(jnp.bfloat16)
        text_values_ref[...] = text_v_ref[...]


def attend_kernel(tokens, query_rows, key_rows, steps, me_ref, *rest):
    me = me_ref[0]
    count = len(steps)
    arrived = rest[:count]
    text_keys_ref, text_values_ref = rest[count : count + 2]
    out_ref, queries_ref, keys_ref, values_ref, result_ref = rest[count + 2 :]
    head_size = text_keys_ref.shape[1]
    padded = arrived[0].shape[0] - 2 * tokens
    factor = head_size ** (-0.5) * LOG2E
    text = text_keys_ref.shape[0]
    keys_ref[:text] = text_keys_ref[...]
    values_ref[:text] = text_values_ref[...]
    for step in range(count):
        first = text + step * tokens
        keys_ref[first : first + tokens] = arrived[step][:tokens]
        values_ref[first : first + tokens] = arrived[step][tokens : 2 * tokens]
        queries_ref[step * padded : (step + 1) * padded] = arrived[step][2 * tokens :]

    def add_queries(step, carry):
        first_row = step * query_rows
        if not isinstance(step, int):
            first_row = pl.multiple_of(first_row, 16)
        mine = pl.ds(first_row, query_rows)
        queries = queries_ref[mine]
        sums = None
        for first in range(0, keys_ref.shape[0], key_rows):
            scores = lax.dot_general(
                queries,
                keys_ref[first : first + key_rows],
                (((1,), (1,)), ((), ())),
                preferred_element_type=jnp.float32,
            )
            weights = jnp.exp2(scores * factor).astype(jnp.bfloat16)
            values = values_ref[first : first + key_rows]
            beside = jnp.concatenate([values, jnp.ones_like(values)], axis=1)
            added = jnp.dot(weights, beside, preferred_element_type=jnp.float32)
            sums = added if sums is None else sums + added
        result_ref[mine] = (sums[:, :head_size] / sums[:, head_size:]).astype(jnp.bfloat16)
        return carry

    turns = queries_ref.shape[0] // query_rows
    if turns <= 4:
        for step in range(turns):
            add_queries(step, 0)
    else:
        lax.fori_loop(0, turns, add_queries, 0)
    for step in range(count):
        owner = lax.bitwise_xor(me, steps[step])
        out_ref[owner] = result_ref[step * padded : (step + 1) * padded]


def finish_kernel(per_group, slots_ref, returned_ref, cache_ref, out_ref):
    tokens = cache_ref.shape[0]
    head_size = returned_ref.shape[2]
    groups = slots_ref.shape[0]
    heads = cache_ref.shape[1] // head_size
    mine = [place(slots_ref[group : group + 1], tokens) for group in range(groups)]
    count = sum(jnp.sum(m.astype(jnp.float32), axis=1, keepdims=True) for m in mine)
    is_fresh = count > 0.5
    one_hot = [m.astype(jnp.bfloat16) for m in mine]
    for head in range(heads):
        columns = slice(head * head_size, (head + 1) * head_size)
        placed = sum(
            jnp.dot(
                one_hot[group],
                returned_ref[head * groups + group],
                preferred_element_type=jnp.float32,
            )
            for group in range(groups)
        )
        out_ref[:, columns] = jnp.where(
            is_fresh, placed, cache_ref[:, columns].astype(jnp.float32)
        ).astype(out_ref.dtype)


def whole(shape):
    return pl.BlockSpec(shape, lambda i, me: (0,) * len(shape))


def partners(count):
    half = count // 2
    far = list(reversed(range(half, count)))
    near = list(reversed(range(1, half)))
    order = far[:3]
    for turn in range(max(len(far) - 3, len(near))):
        order += far[turn + 3 : turn + 4] + near[turn : turn + 1]
    names = sorted(range(count - 1), key=lambda number: str(number) if number else "")
    return [0] + [order[names.index(number)] for number in range(count - 1)]


def trade(block, step):
    if step == 0:
        return block
    count = lax.axis_size("seq")
    return lax.ppermute(block, "seq", [(a, a ^ step) for a in range(count)])


def shards(fresh_qkv, slot_rows, k_cache, v_cache, attn_cache, text_k, text_v, q_gain, k_gain):
    seq_count = lax.axis_size("seq")
    me = lax.axis_index("seq").reshape(1)
    slot_count = slot_rows.shape[0]
    tokens, row_width = k_cache.shape
    text = text_k.shape[0]
    head_size = q_gain.shape[0]
    head_count = row_width // head_size
    groups = seq_count // head_count
    per_group = slot_count // groups
    padded = round_up(per_group, 16)
    rows = 2 * tokens + padded
    q_gain = q_gain.reshape(1, head_size)
    k_gain = k_gain.reshape(1, head_size)
    qkv = jnp.transpose(fresh_qkv, (1, 0, 2))
    slots = slot_rows.reshape(1, slot_count)
    padded_slots = jnp.pad(
        slot_rows.reshape(groups, per_group),
        ((0, 0), (0, padded - per_group)),
        constant_values=tokens,
    )

    steps = partners(seq_count)
    block = jax.ShapeDtypeStruct((rows, head_size), jnp.bfloat16)
    text_block = jax.ShapeDtypeStruct((text, head_size), jnp.bfloat16)
    scratch = [pltpu.VMEM((groups, padded, head_size), jnp.bfloat16)]
    common = [whole((1, slot_count)), whole((1, head_size)), whole((1, head_size))]
    early = FIRST_HEADS
    late = [high for high in reversed(range(head_count)) if high not in early]

    def head_specs(high):
        def column(me):
            return lax.bitwise_xor(me[0] // groups, high)

        return [
            pl.BlockSpec((3, slot_count, head_size), lambda i, me: (0, 0, column(me))),
            pl.BlockSpec((tokens, head_size), lambda i, me: (0, column(me))),
            pl.BlockSpec((tokens, head_size), lambda i, me: (0, column(me))),
        ]

    first = pl.pallas_call(
        lambda *refs: prepare_kernel(per_group, padded, early, True, *refs),
        out_shape=[block] * (groups * len(early)),
        grid_spec=pltpu.PrefetchScalarGridSpec(
            num_scalar_prefetch=1,
            grid=(1,),
            in_specs=common + [spec for high in early for spec in head_specs(high)],
            out_specs=[whole((rows, head_size))] * (groups * len(early)),
            scratch_shapes=scratch,
        ),
        name="prepare_first",
    )(me, slots, q_gain, k_gain, *([qkv, k_cache, v_cache] * len(early)))
    met = {}
    for turn, made in enumerate(first):
        step = early[turn // groups] * groups + turn % groups
        met[step] = trade(made, step)
    text_spec = pl.BlockSpec((text, head_size), lambda i, me: (0, me[0] // groups))
    *second, text_keys, text_values = pl.pallas_call(
        lambda *refs: prepare_kernel(per_group, padded, late, False, *refs),
        out_shape=[block] * (groups * len(late)) + [text_block] * 2,
        grid_spec=pltpu.PrefetchScalarGridSpec(
            num_scalar_prefetch=1,
            grid=(1,),
            in_specs=common
            + [
                whole((3, slot_count, row_width)),
                whole((tokens, row_width)),
                whole((tokens, row_width)),
                text_spec,
                text_spec,
                pl.BlockSpec(memory_space=pl.ANY),
            ],
            out_specs=[whole((rows, head_size))] * (groups * len(late))
            + [whole((text, head_size))] * 2,
            scratch_shapes=scratch,
        ),
        compiler_params=pltpu.CompilerParams(vmem_limit_bytes=24 * 2**20),
        name="prepare_rest",
    )(me, slots, q_gain, k_gain, qkv, k_cache, v_cache, text_k, text_v, met[groups])
    arrived = dict(met)
    for turn, made in enumerate(second):
        step = late[turn // groups] * groups + turn % groups
        arrived[step] = trade(made, step)
    arrived = [arrived[step] for step in steps]

    query_rows = 4 * padded
    all_keys = text + seq_count * tokens
    result = pl.pallas_call(
        lambda *refs: attend_kernel(tokens, query_rows, 768, steps, *refs),
        out_shape=jax.ShapeDtypeStruct((seq_count, padded, head_size), jnp.bfloat16),
        grid_spec=pltpu.PrefetchScalarGridSpec(
            num_scalar_prefetch=1,
            grid=(1,),
            in_specs=[whole((rows, head_size))] * seq_count
            + [whole((text, head_size))] * 2,
            out_specs=whole((seq_count, padded, head_size)),
            scratch_shapes=[
                pltpu.VMEM((seq_count * padded, head_size), jnp.bfloat16),
                pltpu.VMEM((all_keys, head_size), jnp.bfloat16),
                pltpu.VMEM((all_keys, head_size), jnp.bfloat16),
                pltpu.VMEM((seq_count * padded, head_size), jnp.bfloat16),
            ],
        ),
        compiler_params=pltpu.CompilerParams(vmem_limit_bytes=40 * 2**20),
        name="attend",
    )(me, *arrived, text_keys, text_values)

    returned = lax.all_to_all(result, "seq", split_axis=0, concat_axis=0, tiled=True)

    finish_steps = 1
    return pl.pallas_call(
        lambda *refs: finish_kernel(per_group, *refs),
        out_shape=jax.ShapeDtypeStruct((tokens, row_width), attn_cache.dtype),
        grid=(finish_steps,),
        in_specs=[
            pl.BlockSpec((groups, padded), lambda i: (0, 0)),
            pl.BlockSpec((seq_count // finish_steps, padded, head_size), lambda i: (i, 0, 0)),
            pl.BlockSpec((tokens, row_width // finish_steps), lambda i: (0, i)),
        ],
        out_specs=pl.BlockSpec((tokens, row_width // finish_steps), lambda i: (0, i)),
        compiler_params=pltpu.CompilerParams(vmem_limit_bytes=32 * 2**20),
        name="finish",
    )(padded_slots, returned, attn_cache)


def solution(mesh):
    return jax.shard_map(
        shards,
        mesh=mesh,
        in_specs=(
            P(("parts", "seq"), None, None),
            P(("parts", "seq")),
            P(("parts", "seq"), None),
            P(("parts", "seq"), None),
            P(("parts", "seq"), None),
            P("parts", None),
            P("parts", None),
            P(),
            P(),
        ),
        out_specs=P(("parts", "seq"), None),
        check_vma=False,
    )
```

```python
import math

import jax
import jax.numpy as jnp
from jax import lax
from jax.experimental import pallas as pl
from jax.experimental.pallas import tpu as pltpu
from jax.sharding import PartitionSpec as P

LOG2E = math.log2(math.e)
FIRST_HEADS = [15, 14, 1]


def round_up(count, step):
    return (count + step - 1) // step * step


def normalize(entries, scales):
    mean_square = jnp.mean(entries * entries, axis=-1, keepdims=True)
    return entries * lax.rsqrt(mean_square + 1e-06) * scales


def place(slots, tokens):
    owner = lax.broadcasted_iota(jnp.int32, (tokens, slots.shape[1]), 0)
    return owner == slots


def prepare_kernel(per_group, padded, highs, by_head, me_ref, slots_ref, q_gain_ref, k_gain_ref, *rest):
    tokens = 0
    if by_head:
        groups = slots_ref.shape[1] // per_group
        loads = [rest[3 * turn : 3 * turn + 3] for turn in range(len(highs))]
        outs = rest[3 * len(highs) : 3 * len(highs) + groups * len(highs)]
        queries_ref = rest[-1]
        tokens = loads[0][1].shape[0]
    else:
        groups = slots_ref.shape[1] // per_group
        qkv_ref, k_ref, v_ref, text_k_ref, text_v_ref = rest[:5]
        rest = rest[6:]
        outs = rest[: groups * len(highs)]
        text_keys_ref, text_values_ref, queries_ref = rest[groups * len(highs) :]
        tokens = k_ref.shape[0]
    head_size = q_gain_ref.shape[1]
    me = me_ref[0]
    mine = place(slots_ref[...], tokens)
    is_fresh = jnp.max(mine.astype(jnp.float32), axis=1, keepdims=True) > 0.5
    one_hot = mine.astype(jnp.bfloat16)
    q_gain = q_gain_ref[...]
    k_gain = k_gain_ref[...]

    spare = []
    for group in range(groups):
        held = slots_ref[:, group * per_group : (group + 1) * per_group] < tokens
        fresh_count = jnp.sum(held.astype(jnp.float32), axis=1, keepdims=True)
        spare.append(jnp.broadcast_to(fresh_count, (padded - per_group, head_size)))

    def merged(fresh, cache):
        spread = jnp.dot(one_hot, fresh, preferred_element_type=jnp.float32)
        return jnp.where(is_fresh, spread, cache.astype(jnp.float32))

    for turn, high in enumerate(highs):
        if by_head:
            fresh_ref, cache_k_ref, cache_v_ref = loads[turn]
            fresh = [fresh_ref[part] for part in range(3)]
            cache_k, cache_v = cache_k_ref[...], cache_v_ref[...]
        else:
            head = lax.bitwise_xor(me // groups, high)
            columns = pl.ds(pl.multiple_of(head * head_size, head_size), head_size)
            fresh = [qkv_ref[part, :, columns] for part in range(3)]
            cache_k, cache_v = k_ref[:, columns], v_ref[:, columns]
        keys = normalize(merged(fresh[1], cache_k), k_gain).astype(jnp.bfloat16)
        values = merged(fresh[2], cache_v).astype(jnp.bfloat16)
        queries = normalize(fresh[0].astype(jnp.float32), q_gain)
        for group in range(groups):
            share = queries[group * per_group : (group + 1) * per_group]
            share = jnp.concatenate([share, spare[group]], axis=0)
            queries_ref[group] = share.astype(jnp.bfloat16)
        for low in range(groups):
            out_ref = outs[turn * groups + low]
            group = lax.bitwise_xor(me % groups, low)
            out_ref[:tokens] = keys
            out_ref[tokens : 2 * tokens] = values
            out_ref[2 * tokens :] = queries_ref[group]
    if not by_head:
        text_keys = normalize(text_k_ref[...].astype(jnp.float32), k_gain)
        text_keys_ref[...] = text_keys.astype(jnp.bfloat16)
        text_values_ref[...] = text_v_ref[...]


def attend_kernel(tokens, per_group, query_rows, key_rows, turns, steps, me_ref, *rest):
    me = me_ref[0]
    count = len(steps)
    arrived = rest[:count]
    text_keys_ref, text_values_ref = rest[count : count + 2]
    out_ref, queries_ref, keys_ref, values_ref, result_ref = rest[count + 2 :]
    head_size = text_keys_ref.shape[1]
    padded = arrived[0].shape[0] - 2 * tokens
    factor = head_size ** (-0.5) * LOG2E
    text = text_keys_ref.shape[0]
    keys_ref[:text] = text_keys_ref[...]
    values_ref[:text] = text_values_ref[...]
    for step in range(count):
        first = text + step * tokens
        keys_ref[first : first + tokens] = arrived[step][:tokens]
        values_ref[first : first + tokens] = arrived[step][tokens : 2 * tokens]

    last_rows = slice(2 * tokens + padded - 16, 2 * tokens + padded)
    count_row = per_group - (padded - 16)
    firsts = [0]
    for step in range(count):
        spare = arrived[step][last_rows].astype(jnp.float32)[count_row : count_row + 1]
        firsts.append(firsts[-1] + jnp.max(spare).astype(jnp.int32))
    result_ref[...] = jnp.zeros_like(result_ref)
    for step in range(count):
        rows = arrived[step][2 * tokens :].astype(jnp.float32)
        queries_ref[pl.ds(firsts[step], padded)] = rows
    after = query_rows + padded
    queries_ref[pl.ds(firsts[count], after)] = jnp.zeros((after, head_size), jnp.float32)

    def add_queries(step, carry):
        first_row = step * query_rows
        if not isinstance(step, int):
            first_row = pl.multiple_of(first_row, 16)
        mine = pl.ds(first_row, query_rows)
        queries = queries_ref[mine].astype(jnp.bfloat16)
        sums = None
        for first in range(0, keys_ref.shape[0], key_rows):
            scores = lax.dot_general(
                queries,
                keys_ref[first : first + key_rows],
                (((1,), (1,)), ((), ())),
                preferred_element_type=jnp.float32,
            )
            weights = jnp.exp2(scores * factor).astype(jnp.bfloat16)
            values = values_ref[first : first + key_rows]
            beside = jnp.concatenate([values, jnp.ones_like(values)], axis=1)
            added = jnp.dot(weights, beside, preferred_element_type=jnp.float32)
            sums = added if sums is None else sums + added
        result_ref[mine] = sums[:, :head_size] / sums[:, head_size:]
        return carry

    if turns is not None:
        for step in range(turns):
            add_queries(step, 0)
    else:
        lax.fori_loop(0, (firsts[count] + query_rows - 1) // query_rows, add_queries, 0)
    for step in range(count):
        owner = lax.bitwise_xor(me, steps[step])
        out_ref[owner] = result_ref[pl.ds(firsts[step], padded)].astype(jnp.bfloat16)


def finish_kernel(per_group, slots_ref, returned_ref, cache_ref, out_ref):
    tokens = cache_ref.shape[0]
    head_size = returned_ref.shape[2]
    groups = slots_ref.shape[0]
    heads = cache_ref.shape[1] // head_size
    mine = [place(slots_ref[group : group + 1], tokens) for group in range(groups)]
    count = sum(jnp.sum(m.astype(jnp.float32), axis=1, keepdims=True) for m in mine)
    is_fresh = count > 0.5
    one_hot = [m.astype(jnp.bfloat16) for m in mine]
    for head in range(heads):
        columns = slice(head * head_size, (head + 1) * head_size)
        placed = sum(
            jnp.dot(
                one_hot[group],
                returned_ref[head * groups + group],
                preferred_element_type=jnp.float32,
            )
            for group in range(groups)
        )
        out_ref[:, columns] = jnp.where(
            is_fresh, placed, cache_ref[:, columns].astype(jnp.float32)
        ).astype(out_ref.dtype)


def whole(shape):
    return pl.BlockSpec(shape, lambda i, me: (0,) * len(shape))


def partners(count):
    half = count // 2
    far = list(reversed(range(half, count)))
    near = list(reversed(range(1, half)))
    order = far[:3]
    for turn in range(max(len(far) - 3, len(near))):
        order += far[turn + 3 : turn + 4] + near[turn : turn + 1]
    names = sorted(range(count - 1), key=lambda number: str(number) if number else "")
    return [0] + [order[names.index(number)] for number in range(count - 1)]


def trade(block, step):
    if step == 0:
        return block
    count = lax.axis_size("seq")
    return lax.ppermute(block, "seq", [(a, a ^ step) for a in range(count)])


def shards(fresh_qkv, slot_rows, k_cache, v_cache, attn_cache, text_k, text_v, q_gain, k_gain):
    seq_count = lax.axis_size("seq")
    me = lax.axis_index("seq").reshape(1)
    slot_count = slot_rows.shape[0]
    tokens, row_width = k_cache.shape
    text = text_k.shape[0]
    head_size = q_gain.shape[0]
    head_count = row_width // head_size
    groups = seq_count // head_count
    per_group = slot_count // groups
    padded = round_up(per_group + 1, 16)
    rows = 2 * tokens + padded
    q_gain = q_gain.reshape(1, head_size)
    k_gain = k_gain.reshape(1, head_size)
    qkv = jnp.transpose(fresh_qkv, (1, 0, 2))
    slots = slot_rows.reshape(1, slot_count)
    padded_slots = jnp.pad(
        slot_rows.reshape(groups, per_group),
        ((0, 0), (0, padded - per_group)),
        constant_values=tokens,
    )

    steps = partners(seq_count)
    block = jax.ShapeDtypeStruct((rows, head_size), jnp.bfloat16)
    text_block = jax.ShapeDtypeStruct((text, head_size), jnp.bfloat16)
    scratch = [pltpu.VMEM((groups, padded, head_size), jnp.bfloat16)]
    common = [whole((1, slot_count)), whole((1, head_size)), whole((1, head_size))]
    early = FIRST_HEADS
    late = [high for high in reversed(range(head_count)) if high not in early]

    def head_specs(high):
        def column(me):
            return lax.bitwise_xor(me[0] // groups, high)

        return [
            pl.BlockSpec((3, slot_count, head_size), lambda i, me: (0, 0, column(me))),
            pl.BlockSpec((tokens, head_size), lambda i, me: (0, column(me))),
            pl.BlockSpec((tokens, head_size), lambda i, me: (0, column(me))),
        ]

    first = pl.pallas_call(
        lambda *refs: prepare_kernel(per_group, padded, early, True, *refs),
        out_shape=[block] * (groups * len(early)),
        grid_spec=pltpu.PrefetchScalarGridSpec(
            num_scalar_prefetch=1,
            grid=(1,),
            in_specs=common + [spec for high in early for spec in head_specs(high)],
            out_specs=[whole((rows, head_size))] * (groups * len(early)),
            scratch_shapes=scratch,
        ),
        name="prepare_first",
    )(me, slots, q_gain, k_gain, *([qkv, k_cache, v_cache] * len(early)))
    met = {}
    for turn, made in enumerate(first):
        step = early[turn // groups] * groups + turn % groups
        met[step] = trade(made, step)
    text_spec = pl.BlockSpec((text, head_size), lambda i, me: (0, me[0] // groups))
    *second, text_keys, text_values = pl.pallas_call(
        lambda *refs: prepare_kernel(per_group, padded, late, False, *refs),
        out_shape=[block] * (groups * len(late)) + [text_block] * 2,
        grid_spec=pltpu.PrefetchScalarGridSpec(
            num_scalar_prefetch=1,
            grid=(1,),
            in_specs=common
            + [
                whole((3, slot_count, row_width)),
                whole((tokens, row_width)),
                whole((tokens, row_width)),
                text_spec,
                text_spec,
                pl.BlockSpec(memory_space=pl.ANY),
            ],
            out_specs=[whole((rows, head_size))] * (groups * len(late))
            + [whole((text, head_size))] * 2,
            scratch_shapes=scratch,
        ),
        compiler_params=pltpu.CompilerParams(vmem_limit_bytes=24 * 2**20),
        name="prepare_rest",
    )(me, slots, q_gain, k_gain, qkv, k_cache, v_cache, text_k, text_v, met[groups])
    arrived = dict(met)
    for turn, made in enumerate(second):
        step = late[turn // groups] * groups + turn % groups
        arrived[step] = trade(made, step)
    arrived = [arrived[step] for step in steps]

    all_fresh = seq_count * slot_count // 2
    query_rows = 4 * slot_count
    turns = -(-all_fresh // query_rows) if groups == 1 else None
    packed_rows = seq_count * padded + query_rows + padded
    all_keys = text + seq_count * tokens
    result = pl.pallas_call(
        lambda *refs: attend_kernel(
            tokens, per_group, query_rows, 768, turns, steps, *refs
        ),
        out_shape=jax.ShapeDtypeStruct((seq_count, padded, head_size), jnp.bfloat16),
        grid_spec=pltpu.PrefetchScalarGridSpec(
            num_scalar_prefetch=1,
            grid=(1,),
            in_specs=[whole((rows, head_size))] * seq_count
            + [whole((text, head_size))] * 2,
            out_specs=whole((seq_count, padded, head_size)),
            scratch_shapes=[
                pltpu.VMEM((packed_rows, head_size), jnp.float32),
                pltpu.VMEM((all_keys, head_size), jnp.bfloat16),
                pltpu.VMEM((all_keys, head_size), jnp.bfloat16),
                pltpu.VMEM((packed_rows, head_size), jnp.float32),
            ],
        ),
        compiler_params=pltpu.CompilerParams(vmem_limit_bytes=40 * 2**20),
        name="attend",
    )(me, *arrived, text_keys, text_values)

    returned = lax.all_to_all(result, "seq", split_axis=0, concat_axis=0, tiled=True)

    finish_steps = 1
    return pl.pallas_call(
        lambda *refs: finish_kernel(per_group, *refs),
        out_shape=jax.ShapeDtypeStruct((tokens, row_width), attn_cache.dtype),
        grid=(finish_steps,),
        in_specs=[
            pl.BlockSpec((groups, padded), lambda i: (0, 0)),
            pl.BlockSpec((seq_count // finish_steps, padded, head_size), lambda i: (i, 0, 0)),
            pl.BlockSpec((tokens, row_width // finish_steps), lambda i: (0, i)),
        ],
        out_specs=pl.BlockSpec((tokens, row_width // finish_steps), lambda i: (0, i)),
        compiler_params=pltpu.CompilerParams(vmem_limit_bytes=32 * 2**20),
        name="finish",
    )(padded_slots, returned, attn_cache)


def solution(mesh):
    return jax.shard_map(
        shards,
        mesh=mesh,
        in_specs=(
            P(("parts", "seq"), None, None),
            P(("parts", "seq")),
            P(("parts", "seq"), None),
            P(("parts", "seq"), None),
            P(("parts", "seq"), None),
            P("parts", None),
            P("parts", None),
            P(),
            P(),
        ),
        out_specs=P(("parts", "seq"), None),
        check_vma=False,
    )
```

```python
import math

import jax
import jax.numpy as jnp
from jax import lax
from jax.experimental import pallas as pl
from jax.experimental.pallas import tpu as pltpu
from jax.sharding import PartitionSpec as P

LOG2E = math.log2(math.e)
INNER = 4
CORE, NEXT = 1, 2
MIB = 2**20


def round_up(count, step):
    return (count + step - 1) // step * step


def normalize(entries, scales):
    mean_square = jnp.mean(entries * entries, axis=-1, keepdims=True)
    return entries * lax.rsqrt(mean_square + 1e-06) * scales


def place(slots, tokens):
    owner = lax.broadcasted_iota(jnp.int32, (tokens, slots.shape[1]), 0)
    return owner == slots


def prepare_kernel(plan, padded, me_ref, *refs):
    with_text = any(share for _, _, share in plan)
    slots_hbm, q_gain_hbm, k_gain_hbm, qkv_hbm, k_hbm, v_hbm = refs[:6]
    rest = refs[6:]
    if with_text:
        text_k_hbm, text_v_hbm = rest[:2]
        rest = rest[2:]
    outs = []
    for _, pair, share in plan:
        outs.append((rest[0] if pair else None, rest[pair] if share else None))
        rest = rest[pair + share :]
    if with_text:
        text_out_ref, rest = rest[0], rest[1:]
    slots_ref, q_gain_ref, k_gain_ref, fresh_ref, k_ref, v_ref, text_ref = rest[:7]
    small_sems, sems, text_sems = rest[7:]
    slot_count = slots_ref.shape[1]
    tokens, width = k_ref.shape[1:]
    head_size = q_gain_ref.shape[1]
    outer = me_ref[0] // INNER

    def columns(step):
        return pl.ds(pl.multiple_of(lax.bitwise_xor(outer, step) * width, width), width)

    small = [
        pltpu.make_async_copy(slots_hbm, slots_ref, small_sems.at[0]),
        pltpu.make_async_copy(q_gain_hbm, q_gain_ref, small_sems.at[1]),
        pltpu.make_async_copy(k_gain_hbm, k_gain_ref, small_sems.at[2]),
    ]
    for copy in small:
        copy.start()
    loads = []
    for turn, (step, pair, _) in enumerate(plan):
        mine = columns(step)
        copies = [
            pltpu.make_async_copy(qkv_hbm.at[:, :, mine], fresh_ref.at[turn], sems.at[turn, 0])
        ]
        if pair:
            copies += [
                pltpu.make_async_copy(k_hbm.at[:, mine], k_ref.at[turn], sems.at[turn, 1]),
                pltpu.make_async_copy(v_hbm.at[:, mine], v_ref.at[turn], sems.at[turn, 2]),
            ]
        for copy in copies:
            copy.start()
        loads.append(copies)
    if with_text:
        mine = columns(0)
        text_loads = [
            pltpu.make_async_copy(text_k_hbm.at[:, mine], text_ref.at[0], text_sems.at[0]),
            pltpu.make_async_copy(text_v_hbm.at[:, mine], text_ref.at[1], text_sems.at[1]),
        ]
        for copy in text_loads:
            copy.start()
    for copy in small:
        copy.wait()
    belongs = place(slots_ref[...], tokens)
    is_fresh = jnp.max(belongs.astype(jnp.float32), axis=1, keepdims=True) > 0.5
    one_hot = belongs.astype(jnp.bfloat16)
    q_gain = q_gain_ref[...]
    k_gain = k_gain_ref[...]
    empty = jnp.zeros((padded - slot_count, head_size), jnp.float32)

    def merged(fresh, cache):
        spread = jnp.dot(one_hot, fresh, preferred_element_type=jnp.float32)
        return jnp.where(is_fresh, spread, cache.astype(jnp.float32))

    for turn, (pair_ref, share_ref) in enumerate(outs):
        for copy in loads[turn]:
            copy.wait()
        for head in range(width // head_size):
            lanes = slice(head * head_size, (head + 1) * head_size)
            if pair_ref is not None:
                keys = merged(fresh_ref[turn, 1, :, lanes], k_ref[turn, :, lanes])
                values = merged(fresh_ref[turn, 2, :, lanes], v_ref[turn, :, lanes])
                pair_ref[0, head] = normalize(keys, k_gain).astype(jnp.bfloat16)
                pair_ref[1, head] = values.astype(jnp.bfloat16)
            if share_ref is not None:
                queries = normalize(fresh_ref[turn, 0, :, lanes].astype(jnp.float32), q_gain)
                if padded > slot_count:
                    queries = jnp.concatenate([queries, empty], axis=0)
                share_ref[head] = queries.astype(jnp.bfloat16)
    if with_text:
        for copy in text_loads:
            copy.wait()
        for head in range(width // head_size):
            lanes = slice(head * head_size, (head + 1) * head_size)
            text_keys = normalize(text_ref[0, :, lanes].astype(jnp.float32), k_gain)
            text_out_ref[0, head] = text_keys.astype(jnp.bfloat16)
            text_out_ref[1, head] = text_ref[1, :, lanes]


def stack_kernel(*refs):
    out_ref = refs[-1]
    for number, ref in enumerate(refs[:-1]):
        out_ref[number] = ref[...]


def add_keys(sums, queries, keys, values):
    factor = queries.shape[1] ** (-0.5) * LOG2E
    scores = lax.dot_general(
        queries, keys, (((1,), (1,)), ((), ())), preferred_element_type=jnp.float32
    )
    weights = jnp.exp2(scores * factor).astype(jnp.bfloat16)
    beside = jnp.concatenate([values, jnp.ones_like(values)], axis=1)
    added = jnp.dot(weights, beside, preferred_element_type=jnp.float32)
    return added if sums is None else sums + added


def add_pairs(sums, queries, refs, head):
    pairs = []
    for ref in refs:
        if len(ref.shape) == 4:
            pairs.append(lambda part, ref=ref: ref[part, head])
        else:
            for number in range(ref.shape[0]):
                pairs.append(lambda part, ref=ref, number=number: ref[number, part, head])
    for first in range(0, len(pairs), 6):
        some = pairs[first : first + 6]
        keys = jnp.concatenate([pair(0) for pair in some], axis=0)
        values = jnp.concatenate([pair(1) for pair in some], axis=0)
        sums = add_keys(sums, queries, keys, values)
    return sums


def query_blocks(queries, head):
    for first in range(0, len(queries), 4):
        yield first, jnp.concatenate([ref[head] for ref in queries[first : first + 4]], axis=0)


def attend_kernel(count, *refs):
    queries, pairs, sums_ref = refs[:count], refs[count:-1], refs[-1]
    for head in range(queries[0].shape[0]):
        for first, block in query_blocks(queries, head):
            sums_ref[head, first // 4] = add_pairs(None, block, pairs, head)


def complete_kernel(count, *refs):
    queries, rest = refs[:count], refs[count:]
    pairs, sums_ref, outs = rest[:2], rest[2], rest[3:]
    heads, padded, head_size = queries[0].shape
    for head in range(heads):
        for first, block in query_blocks(queries, head):
            sums = add_pairs(sums_ref[head, first // 4], block, pairs, head)
            result = (sums[:, :head_size] / sums[:, head_size:]).astype(jnp.bfloat16)
            for turn in range(block.shape[0] // padded):
                outs[first + turn][head] = result[turn * padded : (turn + 1) * padded]


def finish_kernel(heads, steps, me_ref, slots_ref, cache_ref, *rest):
    returned, out_ref = rest[:-1], rest[-1]
    tokens = cache_ref.shape[0]
    head_size = returned[0].shape[2]
    groups = slots_ref.shape[0]
    outer = me_ref[0] // INNER
    one_hot = []
    owned = jnp.zeros((tokens, 1), jnp.float32)
    for low in range(groups):
        group = lax.bitwise_xor(outer % groups, low)
        mine = place(slots_ref[pl.ds(group, 1)], tokens).astype(jnp.float32)
        owned = owned + jnp.sum(mine, axis=1, keepdims=True)
        one_hot.append(mine.astype(jnp.bfloat16))
    is_fresh = owned > 0.5
    for high in range(len(steps) // groups):
        block = lax.bitwise_xor(outer // groups, high)
        for head in range(heads):
            at = (block * heads + head) * head_size
            columns = pl.ds(pl.multiple_of(at, head_size), head_size)
            placed = jnp.zeros((tokens, head_size), jnp.float32)
            for low in range(groups):
                made = returned[steps.index(high * groups + low)][head]
                placed = placed + jnp.dot(one_hot[low], made, preferred_element_type=jnp.float32)
            out_ref[:, columns] = jnp.where(
                is_fresh, placed, cache_ref[:, columns].astype(jnp.float32)
            ).astype(out_ref.dtype)


def trade(block, distance):
    count = lax.axis_size("seq")
    return lax.ppermute(block, "seq", [(a, a ^ distance) for a in range(count)])


def shards(fresh_qkv, slot_rows, k_cache, v_cache, attn_cache, text_k, text_v, q_gain, k_gain):
    seq_count = lax.axis_size("seq")
    me = lax.axis_index("seq").reshape(1)
    slot_count = slot_rows.shape[0]
    tokens, row_width = k_cache.shape
    text = text_k.shape[0]
    head_size = q_gain.shape[0]
    outers = seq_count // INNER
    width = row_width // outers
    heads = width // head_size
    padded = round_up(slot_count, 16)
    qkv = jnp.transpose(fresh_qkv, (1, 0, 2))
    q_gain = q_gain.reshape(1, head_size)
    k_gain = k_gain.reshape(1, head_size)
    slots = slot_rows.reshape(1, slot_count)
    padded_slots = jnp.pad(
        slots, ((0, 0), (0, padded - slot_count)), constant_values=tokens
    )

    def shaped(*shape, dtype=jnp.bfloat16):
        return jax.ShapeDtypeStruct(shape, dtype)

    in_hbm = pl.BlockSpec(memory_space=pltpu.HBM)
    in_vmem = pl.BlockSpec(memory_space=pltpu.VMEM)
    in_smem = pl.BlockSpec(memory_space=pltpu.SMEM)
    small = pltpu.CompilerParams(vmem_limit_bytes=24 * MIB)

    def prepare(plan, name, params, *extra):
        with_text = len(extra) > 0
        shapes = []
        for _, pair, share in plan:
            shapes += [shaped(2, heads, tokens, head_size)] * pair
            shapes += [shaped(heads, padded, head_size)] * share
        if with_text:
            shapes.append(shaped(2, heads, text, head_size))
        made = pl.pallas_call(
            lambda *refs: prepare_kernel(plan, padded, *refs),
            out_shape=shapes,
            in_specs=[in_smem] + [in_hbm] * 6 + [in_hbm] * (2 * with_text),
            out_specs=[in_vmem] * len(shapes),
            scratch_shapes=[
                pltpu.VMEM((1, slot_count), jnp.int32),
                pltpu.VMEM((1, head_size), jnp.float32),
                pltpu.VMEM((1, head_size), jnp.float32),
                pltpu.VMEM((len(plan), 3, slot_count, width), jnp.bfloat16),
                pltpu.VMEM((len(plan), tokens, width), jnp.bfloat16),
                pltpu.VMEM((len(plan), tokens, width), jnp.bfloat16),
                pltpu.VMEM((2, text, width), jnp.bfloat16),
                pltpu.SemaphoreType.DMA((3,)),
                pltpu.SemaphoreType.DMA((len(plan), 3)),
                pltpu.SemaphoreType.DMA((2,)),
            ],
            compiler_params=params,
            name=name,
        )(me, slots, q_gain, k_gain, qkv, k_cache, v_cache, *extra)
        return list(made)

    def stack(blocks, after, name):
        return pl.pallas_call(
            lambda *refs: stack_kernel(*refs[len(after) :]),
            out_shape=shaped(len(blocks), *blocks[0].shape),
            in_specs=[pl.BlockSpec(memory_space=pl.ANY)] * len(after) + [in_vmem] * len(blocks),
            out_specs=in_vmem,
            compiler_params=small,
            name=name,
        )(*after, *blocks)

    half = outers // 2
    near = list(range(1, half))
    far = list(reversed(range(half + 1, outers)))
    order = far[:1] + near + [half] + far[1:] + [0]
    made = prepare(
        [(step, True, True) for step in order], "prepare", pltpu.CompilerParams(), text_k, text_v
    )
    text_pair = made.pop()
    own = made[-2]
    own_other = trade(own, CORE)
    pairs, shares = {}, {0: made[-1]}
    for number, step in enumerate(order[:-1]):
        pairs[step] = trade(made[2 * number], step * INNER)
        shares[step] = trade(made[2 * number + 1], step * INNER)

    own_next = trade(own, NEXT)
    early = [own_next]
    for step in near:
        early += [pairs[step], trade(pairs[step], NEXT)]
    early = stack(early, [shares[step] for step in near], "stack_near")
    middle = []
    for step in far:
        middle += [pairs[step], trade(pairs[step], NEXT)]
    middle = stack(middle, [shares[step] for step in far], "stack_far")
    late = stack([pairs[half], trade(pairs[half], NEXT)], [shares[half]], "stack_last")

    sources = far + [half] + near + [0]
    queries = [shares[step] for step in sources]
    known = [own, own_other, early, trade(early, CORE), middle, trade(middle, CORE)]
    blocks = -(-outers // 4)
    sums = pl.pallas_call(
        lambda *refs: attend_kernel(outers, *refs),
        out_shape=shaped(heads, blocks, 4 * padded, 2 * head_size, dtype=jnp.float32),
        in_specs=[in_vmem] * (outers + 1 + len(known)),
        out_specs=in_vmem,
        compiler_params=small,
        name="attend",
    )(*queries, text_pair, *known)
    results = pl.pallas_call(
        lambda *refs: complete_kernel(outers, *refs),
        out_shape=[shaped(heads, padded, head_size)] * outers,
        in_specs=[in_vmem] * (outers + 3),
        out_specs=[in_vmem] * outers,
        compiler_params=small,
        name="complete",
    )(*queries, late, trade(late, CORE), sums)

    returned = [
        trade(result, step * INNER) if step else result
        for step, result in zip(sources, results)
    ]
    return pl.pallas_call(
        lambda *refs: finish_kernel(heads, sources, *refs),
        out_shape=jax.ShapeDtypeStruct((tokens, row_width), attn_cache.dtype),
        in_specs=[in_smem] + [in_vmem] * (2 + outers),
        out_specs=in_vmem,
        compiler_params=small,
        name="finish",
    )(me, padded_slots, attn_cache, *returned)


def solution(mesh):
    return jax.shard_map(
        shards,
        mesh=mesh,
        in_specs=(
            P(("parts", "seq"), None, None),
            P(("parts", "seq")),
            P(("parts", "seq"), None),
            P(("parts", "seq"), None),
            P(("parts", "seq"), None),
            P("parts", None),
            P("parts", None),
            P(),
            P(),
        ),
        out_specs=P(("parts", "seq"), None),
        check_vma=False,
    )
```

```python
import math

import jax
import jax.numpy as jnp
from jax import lax
from jax.experimental import pallas as pl
from jax.experimental.pallas import tpu as pltpu
from jax.sharding import PartitionSpec as P

LOG2E = math.log2(math.e)
INNER = 4
CORE, NEXT = 1, 2
MIB = 2**20


def round_up(count, step):
    return (count + step - 1) // step * step


def normalize(entries, scales):
    mean_square = jnp.mean(entries * entries, axis=-1, keepdims=True)
    return entries * lax.rsqrt(mean_square + 1e-06) * scales


def place(slots, tokens):
    owner = lax.broadcasted_iota(jnp.int32, (tokens, slots.shape[1]), 0)
    return owner == slots


def prepare_kernel(plan, padded, me_ref, *refs):
    slots_hbm, q_gain_hbm, k_gain_hbm, qkv_hbm, k_hbm, v_hbm = refs[:6]
    rest = refs[6:]
    outs = []
    for _, pair, share in plan:
        outs.append((rest[0] if pair else None, rest[pair] if share else None))
        rest = rest[pair + share :]
    slots_ref, q_gain_ref, k_gain_ref, fresh_ref, k_ref, v_ref = rest[:6]
    small_sems, sems = rest[6:]
    slot_count = slots_ref.shape[1]
    tokens, width = k_ref.shape[1:]
    head_size = q_gain_ref.shape[1]
    outer = me_ref[0] // INNER

    def columns(step):
        return pl.ds(pl.multiple_of(lax.bitwise_xor(outer, step) * width, width), width)

    small = [
        pltpu.make_async_copy(slots_hbm, slots_ref, small_sems.at[0]),
        pltpu.make_async_copy(q_gain_hbm, q_gain_ref, small_sems.at[1]),
        pltpu.make_async_copy(k_gain_hbm, k_gain_ref, small_sems.at[2]),
    ]
    for copy in small:
        copy.start()
    loads = []
    for turn, (step, pair, _) in enumerate(plan):
        mine = columns(step)
        copies = [
            pltpu.make_async_copy(qkv_hbm.at[:, :, mine], fresh_ref.at[turn], sems.at[turn, 0])
        ]
        if pair:
            copies += [
                pltpu.make_async_copy(k_hbm.at[:, mine], k_ref.at[turn], sems.at[turn, 1]),
                pltpu.make_async_copy(v_hbm.at[:, mine], v_ref.at[turn], sems.at[turn, 2]),
            ]
        for copy in copies:
            copy.start()
        loads.append(copies)
    for copy in small:
        copy.wait()
    belongs = place(slots_ref[...], tokens)
    is_fresh = jnp.max(belongs.astype(jnp.float32), axis=1, keepdims=True) > 0.5
    one_hot = belongs.astype(jnp.bfloat16)
    q_gain = q_gain_ref[...]
    k_gain = k_gain_ref[...]
    empty = jnp.zeros((padded - slot_count, head_size), jnp.float32)

    def merged(fresh, cache):
        spread = jnp.dot(one_hot, fresh, preferred_element_type=jnp.float32)
        return jnp.where(is_fresh, spread, cache.astype(jnp.float32))

    for turn, (pair_ref, share_ref) in enumerate(outs):
        for copy in loads[turn]:
            copy.wait()
        for head in range(width // head_size):
            lanes = slice(head * head_size, (head + 1) * head_size)
            if pair_ref is not None:
                keys = merged(fresh_ref[turn, 1, :, lanes], k_ref[turn, :, lanes])
                values = merged(fresh_ref[turn, 2, :, lanes], v_ref[turn, :, lanes])
                pair_ref[0, head] = normalize(keys, k_gain).astype(jnp.bfloat16)
                pair_ref[1, head] = values.astype(jnp.bfloat16)
            if share_ref is not None:
                queries = normalize(fresh_ref[turn, 0, :, lanes].astype(jnp.float32), q_gain)
                if padded > slot_count:
                    queries = jnp.concatenate([queries, empty], axis=0)
                share_ref[head] = queries.astype(jnp.bfloat16)


def text_kernel(me_ref, text_k_hbm, text_v_hbm, k_gain_ref, *refs):
    blocks, out_ref, pair_ref, text_ref, sems = refs[:-4], *refs[-4:]
    heads, text, head_size = pair_ref.shape[1:]
    width = heads * head_size
    mine = pl.ds(pl.multiple_of(me_ref[0] // INNER * width, width), width)
    loads = [
        pltpu.make_async_copy(text_k_hbm.at[:, mine], text_ref.at[0], sems.at[0]),
        pltpu.make_async_copy(text_v_hbm.at[:, mine], text_ref.at[1], sems.at[1]),
    ]
    for copy in loads:
        copy.start()
    for number, ref in enumerate(blocks):
        out_ref[number] = ref[...]
    for copy in loads:
        copy.wait()
    for head in range(heads):
        lanes = slice(head * head_size, (head + 1) * head_size)
        keys = normalize(text_ref[0, :, lanes].astype(jnp.float32), k_gain_ref[...])
        pair_ref[0, head] = keys.astype(jnp.bfloat16)
        pair_ref[1, head] = text_ref[1, :, lanes]


def stack_kernel(*refs):
    out_ref = refs[-1]
    for number, ref in enumerate(refs[:-1]):
        out_ref[number] = ref[...]


def add_keys(sums, queries, keys, values):
    factor = queries.shape[1] ** (-0.5) * LOG2E
    scores = lax.dot_general(
        queries, keys, (((1,), (1,)), ((), ())), preferred_element_type=jnp.float32
    )
    weights = jnp.exp2(scores * factor).astype(jnp.bfloat16)
    beside = jnp.concatenate([values, jnp.ones_like(values)], axis=1)
    added = jnp.dot(weights, beside, preferred_element_type=jnp.float32)
    return added if sums is None else sums + added


def add_pairs(sums, queries, refs, head):
    pairs = []
    for ref in refs:
        if len(ref.shape) == 4:
            pairs.append(lambda part, ref=ref: ref[part, head])
        else:
            for number in range(ref.shape[0]):
                pairs.append(lambda part, ref=ref, number=number: ref[number, part, head])
    for first in range(0, len(pairs), 6):
        some = pairs[first : first + 6]
        keys = jnp.concatenate([pair(0) for pair in some], axis=0)
        values = jnp.concatenate([pair(1) for pair in some], axis=0)
        sums = add_keys(sums, queries, keys, values)
    return sums


def query_blocks(queries, head):
    for first in range(0, len(queries), 4):
        yield first, jnp.concatenate([ref[head] for ref in queries[first : first + 4]], axis=0)


def attend_kernel(count, *refs):
    queries, pairs, sums_ref = refs[:count], refs[count:-1], refs[-1]
    for head in range(queries[0].shape[0]):
        for first, block in query_blocks(queries, head):
            sums_ref[head, first // 4] = add_pairs(None, block, pairs, head)


def complete_kernel(count, *refs):
    queries, rest = refs[:count], refs[count:]
    pairs, sums_ref, outs = rest[:2], rest[2], rest[3:]
    heads, padded, head_size = queries[0].shape
    for head in range(heads):
        for first, block in query_blocks(queries, head):
            sums = add_pairs(sums_ref[head, first // 4], block, pairs, head)
            result = (sums[:, :head_size] / sums[:, head_size:]).astype(jnp.bfloat16)
            for turn in range(block.shape[0] // padded):
                outs[first + turn][head] = result[turn * padded : (turn + 1) * padded]


def finish_kernel(heads, steps, me_ref, slots_ref, cache_ref, *rest):
    returned, out_ref = rest[:-1], rest[-1]
    tokens = cache_ref.shape[0]
    head_size = returned[0].shape[2]
    groups = slots_ref.shape[0]
    outer = me_ref[0] // INNER
    one_hot = []
    owned = jnp.zeros((tokens, 1), jnp.float32)
    for low in range(groups):
        group = lax.bitwise_xor(outer % groups, low)
        mine = place(slots_ref[pl.ds(group, 1)], tokens).astype(jnp.float32)
        owned = owned + jnp.sum(mine, axis=1, keepdims=True)
        one_hot.append(mine.astype(jnp.bfloat16))
    is_fresh = owned > 0.5
    for high in range(len(steps) // groups):
        block = lax.bitwise_xor(outer // groups, high)
        for head in range(heads):
            at = (block * heads + head) * head_size
            columns = pl.ds(pl.multiple_of(at, head_size), head_size)
            placed = jnp.zeros((tokens, head_size), jnp.float32)
            for low in range(groups):
                made = returned[steps.index(high * groups + low)][head]
                placed = placed + jnp.dot(one_hot[low], made, preferred_element_type=jnp.float32)
            out_ref[:, columns] = jnp.where(
                is_fresh, placed, cache_ref[:, columns].astype(jnp.float32)
            ).astype(out_ref.dtype)


def trade(block, distance):
    count = lax.axis_size("seq")
    return lax.ppermute(block, "seq", [(a, a ^ distance) for a in range(count)])


def shards(fresh_qkv, slot_rows, k_cache, v_cache, attn_cache, text_k, text_v, q_gain, k_gain):
    seq_count = lax.axis_size("seq")
    me = lax.axis_index("seq").reshape(1)
    slot_count = slot_rows.shape[0]
    tokens, row_width = k_cache.shape
    text = text_k.shape[0]
    head_size = q_gain.shape[0]
    outers = seq_count // INNER
    width = row_width // outers
    heads = width // head_size
    padded = round_up(slot_count, 16)
    qkv = jnp.transpose(fresh_qkv, (1, 0, 2))
    q_gain = q_gain.reshape(1, head_size)
    k_gain = k_gain.reshape(1, head_size)
    slots = slot_rows.reshape(1, slot_count)
    padded_slots = jnp.pad(
        slots, ((0, 0), (0, padded - slot_count)), constant_values=tokens
    )

    def shaped(*shape, dtype=jnp.bfloat16):
        return jax.ShapeDtypeStruct(shape, dtype)

    in_hbm = pl.BlockSpec(memory_space=pltpu.HBM)
    in_vmem = pl.BlockSpec(memory_space=pltpu.VMEM)
    in_smem = pl.BlockSpec(memory_space=pltpu.SMEM)
    small = pltpu.CompilerParams(vmem_limit_bytes=24 * MIB)

    def prepare(plan, name, params):
        shapes = []
        for _, pair, share in plan:
            shapes += [shaped(2, heads, tokens, head_size)] * pair
            shapes += [shaped(heads, padded, head_size)] * share
        made = pl.pallas_call(
            lambda *refs: prepare_kernel(plan, padded, *refs),
            out_shape=shapes,
            in_specs=[in_smem] + [in_hbm] * 6,
            out_specs=[in_vmem] * len(shapes),
            scratch_shapes=[
                pltpu.VMEM((1, slot_count), jnp.int32),
                pltpu.VMEM((1, head_size), jnp.float32),
                pltpu.VMEM((1, head_size), jnp.float32),
                pltpu.VMEM((len(plan), 3, slot_count, width), jnp.bfloat16),
                pltpu.VMEM((len(plan), tokens, width), jnp.bfloat16),
                pltpu.VMEM((len(plan), tokens, width), jnp.bfloat16),
                pltpu.SemaphoreType.DMA((3,)),
                pltpu.SemaphoreType.DMA((len(plan), 3)),
            ],
            compiler_params=params,
            name=name,
        )(me, slots, q_gain, k_gain, qkv, k_cache, v_cache)
        return list(made)

    def stack(blocks, after, name):
        return pl.pallas_call(
            lambda *refs: stack_kernel(*refs[len(after) :]),
            out_shape=shaped(len(blocks), *blocks[0].shape),
            in_specs=[pl.BlockSpec(memory_space=pl.ANY)] * len(after) + [in_vmem] * len(blocks),
            out_specs=in_vmem,
            compiler_params=small,
            name=name,
        )(*after, *blocks)

    half = outers // 2
    near = list(range(1, half))
    far = list(reversed(range(half + 1, outers)))
    order = far[:1] + near + [half] + far[1:] + [0]
    made = prepare([(step, True, True) for step in order], "prepare", pltpu.CompilerParams())
    own = made[-2]
    own_other = trade(own, CORE)
    pairs, shares = {}, {0: made[-1]}
    for number, step in enumerate(order[:-1]):
        pairs[step] = trade(made[2 * number], step * INNER)
        shares[step] = trade(made[2 * number + 1], step * INNER)

    own_next = trade(own, NEXT)
    early = [own_next]
    for step in near:
        early += [pairs[step], trade(pairs[step], NEXT)]
    after = [shares[step] for step in near + far] + [own_other]
    early, text_pair = pl.pallas_call(
        lambda *refs: text_kernel(*refs[len(after) :]),
        out_shape=[
            shaped(len(early), 2, heads, tokens, head_size),
            shaped(2, heads, text, head_size),
        ],
        in_specs=[pl.BlockSpec(memory_space=pl.ANY)] * len(after)
        + [in_smem, in_hbm, in_hbm, in_vmem]
        + [in_vmem] * len(early),
        out_specs=[in_vmem] * 2,
        scratch_shapes=[
            pltpu.VMEM((2, text, width), jnp.bfloat16),
            pltpu.SemaphoreType.DMA((2,)),
        ],
        compiler_params=small,
        name="stack_near",
    )(*after, me, text_k, text_v, k_gain, *early)
    middle = []
    for step in far:
        middle += [pairs[step], trade(pairs[step], NEXT)]
    middle = stack(middle, [], "stack_far")
    late = stack([pairs[half], trade(pairs[half], NEXT)], [shares[half]], "stack_last")

    sources = far + [half] + near + [0]
    queries = [shares[step] for step in sources]
    known = [own, own_other, early, trade(early, CORE), middle, trade(middle, CORE)]
    blocks = -(-outers // 4)
    sums = pl.pallas_call(
        lambda *refs: attend_kernel(outers, *refs),
        out_shape=shaped(heads, blocks, 4 * padded, 2 * head_size, dtype=jnp.float32),
        in_specs=[in_vmem] * (outers + 1 + len(known)),
        out_specs=in_vmem,
        compiler_params=small,
        name="attend",
    )(*queries, text_pair, *known)
    results = pl.pallas_call(
        lambda *refs: complete_kernel(outers, *refs),
        out_shape=[shaped(heads, padded, head_size)] * outers,
        in_specs=[in_vmem] * (outers + 3),
        out_specs=[in_vmem] * outers,
        compiler_params=small,
        name="complete",
    )(*queries, late, trade(late, CORE), sums)

    returned = [
        trade(result, step * INNER) if step else result
        for step, result in zip(sources, results)
    ]
    return pl.pallas_call(
        lambda *refs: finish_kernel(heads, sources, *refs),
        out_shape=jax.ShapeDtypeStruct((tokens, row_width), attn_cache.dtype),
        in_specs=[in_smem] + [in_vmem] * (2 + outers),
        out_specs=in_vmem,
        compiler_params=small,
        name="finish",
    )(me, padded_slots, attn_cache, *returned)


def solution(mesh):
    return jax.shard_map(
        shards,
        mesh=mesh,
        in_specs=(
            P(("parts", "seq"), None, None),
            P(("parts", "seq")),
            P(("parts", "seq"), None),
            P(("parts", "seq"), None),
            P(("parts", "seq"), None),
            P("parts", None),
            P("parts", None),
            P(),
            P(),
        ),
        out_specs=P(("parts", "seq"), None),
        check_vma=False,
    )
```

```python
import math

import jax
import jax.numpy as jnp
from jax import lax
from jax.experimental import pallas as pl
from jax.experimental.pallas import tpu as pltpu
from jax.sharding import PartitionSpec as P

LOG2E = math.log2(math.e)
INNER = 4
CORE, NEXT = 1, 2
MIB = 2**20


def round_up(count, step):
    return (count + step - 1) // step * step


def normalize(entries, scales):
    mean_square = jnp.mean(entries * entries, axis=-1, keepdims=True)
    return entries * lax.rsqrt(mean_square + 1e-06) * scales


def place(slots, tokens):
    owner = lax.broadcasted_iota(jnp.int32, (tokens, slots.shape[1]), 0)
    return owner == slots


def prepare_kernel(plan, padded, me_ref, *refs):
    slots_hbm, q_gain_hbm, k_gain_hbm, qkv_hbm, k_hbm, v_hbm = refs[:6]
    rest = refs[6:]
    outs = []
    for _, pair, share in plan:
        outs.append((rest[0] if pair else None, rest[pair] if share else None))
        rest = rest[pair + share :]
    slots_ref, q_gain_ref, k_gain_ref, fresh_ref, k_ref, v_ref = rest[:6]
    small_sems, sems = rest[6:]
    slot_count = slots_ref.shape[1]
    tokens, width = k_ref.shape[1:]
    head_size = q_gain_ref.shape[1]
    outer = me_ref[0] // INNER

    def columns(step):
        return pl.ds(pl.multiple_of(lax.bitwise_xor(outer, step) * width, width), width)

    small = [
        pltpu.make_async_copy(slots_hbm, slots_ref, small_sems.at[0]),
        pltpu.make_async_copy(q_gain_hbm, q_gain_ref, small_sems.at[1]),
        pltpu.make_async_copy(k_gain_hbm, k_gain_ref, small_sems.at[2]),
    ]
    for copy in small:
        copy.start()
    loads = []
    for turn, (step, pair, _) in enumerate(plan):
        mine = columns(step)
        copies = [
            pltpu.make_async_copy(qkv_hbm.at[:, :, mine], fresh_ref.at[turn], sems.at[turn, 0])
        ]
        if pair:
            copies += [
                pltpu.make_async_copy(k_hbm.at[:, mine], k_ref.at[turn], sems.at[turn, 1]),
                pltpu.make_async_copy(v_hbm.at[:, mine], v_ref.at[turn], sems.at[turn, 2]),
            ]
        for copy in copies:
            copy.start()
        loads.append(copies)
    for copy in small:
        copy.wait()
    belongs = place(slots_ref[...], tokens)
    is_fresh = jnp.max(belongs.astype(jnp.float32), axis=1, keepdims=True) > 0.5
    one_hot = belongs.astype(jnp.bfloat16)
    q_gain = q_gain_ref[...]
    k_gain = k_gain_ref[...]
    empty = jnp.zeros((padded - slot_count, head_size), jnp.float32)

    def merged(fresh, cache):
        spread = jnp.dot(one_hot, fresh, preferred_element_type=jnp.float32)
        return jnp.where(is_fresh, spread, cache.astype(jnp.float32))

    for turn, (pair_ref, share_ref) in enumerate(outs):
        for copy in loads[turn]:
            copy.wait()
        for head in range(width // head_size):
            lanes = slice(head * head_size, (head + 1) * head_size)
            if pair_ref is not None:
                keys = merged(fresh_ref[turn, 1, :, lanes], k_ref[turn, :, lanes])
                values = merged(fresh_ref[turn, 2, :, lanes], v_ref[turn, :, lanes])
                pair_ref[0, head] = normalize(keys, k_gain).astype(jnp.bfloat16)
                pair_ref[1, head] = values.astype(jnp.bfloat16)
            if share_ref is not None:
                queries = normalize(fresh_ref[turn, 0, :, lanes].astype(jnp.float32), q_gain)
                if padded > slot_count:
                    queries = jnp.concatenate([queries, empty], axis=0)
                share_ref[head] = queries.astype(jnp.bfloat16)


def text_kernel(me_ref, text_k_hbm, text_v_hbm, k_gain_ref, *refs):
    blocks, out_ref, pair_ref, text_ref, sems = refs[:-4], *refs[-4:]
    heads, text, head_size = pair_ref.shape[1:]
    width = heads * head_size
    mine = pl.ds(pl.multiple_of(me_ref[0] // INNER * width, width), width)
    loads = [
        pltpu.make_async_copy(text_k_hbm.at[:, mine], text_ref.at[0], sems.at[0]),
        pltpu.make_async_copy(text_v_hbm.at[:, mine], text_ref.at[1], sems.at[1]),
    ]
    for copy in loads:
        copy.start()
    for number, ref in enumerate(blocks):
        out_ref[number] = ref[...]
    for copy in loads:
        copy.wait()
    for head in range(heads):
        lanes = slice(head * head_size, (head + 1) * head_size)
        keys = normalize(text_ref[0, :, lanes].astype(jnp.float32), k_gain_ref[...])
        pair_ref[0, head] = keys.astype(jnp.bfloat16)
        pair_ref[1, head] = text_ref[1, :, lanes]


def stack_kernel(*refs):
    out_ref = refs[-1]
    for number, ref in enumerate(refs[:-1]):
        out_ref[number] = ref[...]


def add_keys(sums, queries, keys, values):
    factor = queries.shape[1] ** (-0.5) * LOG2E
    scores = lax.dot_general(
        queries, keys, (((1,), (1,)), ((), ())), preferred_element_type=jnp.float32
    )
    weights = jnp.exp2(scores * factor).astype(jnp.bfloat16)
    beside = jnp.concatenate([values, jnp.ones_like(values)], axis=1)
    added = jnp.dot(weights, beside, preferred_element_type=jnp.float32)
    return added if sums is None else sums + added


def add_pairs(sums, queries, refs, head):
    pairs = []
    for ref in refs:
        if len(ref.shape) == 4:
            pairs.append(lambda part, ref=ref: ref[part, head])
        else:
            for number in range(ref.shape[0]):
                pairs.append(lambda part, ref=ref, number=number: ref[number, part, head])
    for first in range(0, len(pairs), 6):
        some = pairs[first : first + 6]
        keys = jnp.concatenate([pair(0) for pair in some], axis=0)
        values = jnp.concatenate([pair(1) for pair in some], axis=0)
        sums = add_keys(sums, queries, keys, values)
    return sums


def query_blocks(queries, head):
    for first in range(0, len(queries), 4):
        yield first, jnp.concatenate([ref[head] for ref in queries[first : first + 4]], axis=0)


def attend_kernel(count, *refs):
    queries, pairs, sums_ref = refs[:count], refs[count:-1], refs[-1]
    for head in range(queries[0].shape[0]):
        for first, block in query_blocks(queries, head):
            sums_ref[head, first // 4] = add_pairs(None, block, pairs, head)


def complete_kernel(count, *refs):
    queries, rest = refs[:count], refs[count:]
    pairs, sums_ref, outs = rest[:2], rest[2], rest[3:]
    heads, padded, head_size = queries[0].shape
    for head in range(heads):
        for first, block in query_blocks(queries, head):
            sums = add_pairs(sums_ref[head, first // 4], block, pairs, head)
            result = (sums[:, :head_size] / sums[:, head_size:]).astype(jnp.bfloat16)
            for turn in range(block.shape[0] // padded):
                outs[first + turn][head] = result[turn * padded : (turn + 1) * padded]


def finish_kernel(heads, steps, me_ref, slots_ref, cache_ref, *rest):
    returned, out_ref = rest[:-1], rest[-1]
    tokens = cache_ref.shape[0]
    head_size = returned[0].shape[2]
    groups = slots_ref.shape[0]
    outer = me_ref[0] // INNER
    one_hot = []
    owned = jnp.zeros((tokens, 1), jnp.float32)
    for low in range(groups):
        group = lax.bitwise_xor(outer % groups, low)
        mine = place(slots_ref[pl.ds(group, 1)], tokens).astype(jnp.float32)
        owned = owned + jnp.sum(mine, axis=1, keepdims=True)
        one_hot.append(mine.astype(jnp.bfloat16))
    is_fresh = owned > 0.5
    for high in range(len(steps) // groups):
        block = lax.bitwise_xor(outer // groups, high)
        for head in range(heads):
            at = (block * heads + head) * head_size
            columns = pl.ds(pl.multiple_of(at, head_size), head_size)
            placed = jnp.zeros((tokens, head_size), jnp.float32)
            for low in range(groups):
                made = returned[steps.index(high * groups + low)][head]
                placed = placed + jnp.dot(one_hot[low], made, preferred_element_type=jnp.float32)
            out_ref[:, columns] = jnp.where(
                is_fresh, placed, cache_ref[:, columns].astype(jnp.float32)
            ).astype(out_ref.dtype)


def trade(block, distance):
    count = lax.axis_size("seq")
    return lax.ppermute(block, "seq", [(a, a ^ distance) for a in range(count)])


def shards(fresh_qkv, slot_rows, k_cache, v_cache, attn_cache, text_k, text_v, q_gain, k_gain):
    seq_count = lax.axis_size("seq")
    me = lax.axis_index("seq").reshape(1)
    slot_count = slot_rows.shape[0]
    tokens, row_width = k_cache.shape
    text = text_k.shape[0]
    head_size = q_gain.shape[0]
    outers = seq_count // INNER
    width = row_width // outers
    heads = width // head_size
    padded = round_up(slot_count, 16)
    qkv = jnp.transpose(fresh_qkv, (1, 0, 2))
    q_gain = q_gain.reshape(1, head_size)
    k_gain = k_gain.reshape(1, head_size)
    slots = slot_rows.reshape(1, slot_count)
    padded_slots = jnp.pad(
        slots, ((0, 0), (0, padded - slot_count)), constant_values=tokens
    )

    def shaped(*shape, dtype=jnp.bfloat16):
        return jax.ShapeDtypeStruct(shape, dtype)

    in_hbm = pl.BlockSpec(memory_space=pltpu.HBM)
    in_vmem = pl.BlockSpec(memory_space=pltpu.VMEM)
    in_smem = pl.BlockSpec(memory_space=pltpu.SMEM)
    small = pltpu.CompilerParams(vmem_limit_bytes=24 * MIB)

    def prepare(plan, name, params):
        shapes = []
        for _, pair, share in plan:
            shapes += [shaped(2, heads, tokens, head_size)] * pair
            shapes += [shaped(heads, padded, head_size)] * share
        made = pl.pallas_call(
            lambda *refs: prepare_kernel(plan, padded, *refs),
            out_shape=shapes,
            in_specs=[in_smem] + [in_hbm] * 6,
            out_specs=[in_vmem] * len(shapes),
            scratch_shapes=[
                pltpu.VMEM((1, slot_count), jnp.int32),
                pltpu.VMEM((1, head_size), jnp.float32),
                pltpu.VMEM((1, head_size), jnp.float32),
                pltpu.VMEM((len(plan), 3, slot_count, width), jnp.bfloat16),
                pltpu.VMEM((len(plan), tokens, width), jnp.bfloat16),
                pltpu.VMEM((len(plan), tokens, width), jnp.bfloat16),
                pltpu.SemaphoreType.DMA((3,)),
                pltpu.SemaphoreType.DMA((len(plan), 3)),
            ],
            compiler_params=params,
            name=name,
        )(me, slots, q_gain, k_gain, qkv, k_cache, v_cache)
        return list(made)

    def stack(blocks, after, name):
        return pl.pallas_call(
            lambda *refs: stack_kernel(*refs[len(after) :]),
            out_shape=shaped(len(blocks), *blocks[0].shape),
            in_specs=[pl.BlockSpec(memory_space=pl.ANY)] * len(after) + [in_vmem] * len(blocks),
            out_specs=in_vmem,
            compiler_params=small,
            name=name,
        )(*after, *blocks)

    half = outers // 2
    near = list(range(1, half))
    far = list(reversed(range(half + 1, outers)))
    order = far[:1] + near + [half] + far[1:] + [0]
    made = prepare([(step, True, True) for step in order], "prepare", pltpu.CompilerParams())
    own = made[-2]
    own_other = trade(own, CORE)
    pairs, shares = {}, {0: made[-1]}
    for number, step in enumerate(order[:-1]):
        pairs[step] = trade(made[2 * number], step * INNER)
        shares[step] = trade(made[2 * number + 1], step * INNER)

    own_next = trade(own, NEXT)
    early = [own_next]
    for step in near:
        early += [pairs[step], trade(pairs[step], NEXT)]
    middle = []
    for step in far:
        middle += [pairs[step], trade(pairs[step], NEXT)]
    middle = stack(middle, [shares[step] for step in far], "stack_far")
    after = [shares[step] for step in near] + [own_other, middle]
    early, text_pair = pl.pallas_call(
        lambda *refs: text_kernel(*refs[len(after) :]),
        out_shape=[
            shaped(len(early), 2, heads, tokens, head_size),
            shaped(2, heads, text, head_size),
        ],
        in_specs=[pl.BlockSpec(memory_space=pl.ANY)] * len(after)
        + [in_smem, in_hbm, in_hbm, in_vmem]
        + [in_vmem] * len(early),
        out_specs=[in_vmem] * 2,
        scratch_shapes=[
            pltpu.VMEM((2, text, width), jnp.bfloat16),
            pltpu.SemaphoreType.DMA((2,)),
        ],
        compiler_params=small,
        name="stack_near",
    )(*after, me, text_k, text_v, k_gain, *early)
    late = stack([pairs[half], trade(pairs[half], NEXT)], [shares[half]], "stack_last")

    sources = far + [half] + near + [0]
    queries = [shares[step] for step in sources]
    known = [own, own_other, early, trade(early, CORE), middle, trade(middle, CORE)]
    blocks = -(-outers // 4)
    sums = pl.pallas_call(
        lambda *refs: attend_kernel(outers, *refs),
        out_shape=shaped(heads, blocks, 4 * padded, 2 * head_size, dtype=jnp.float32),
        in_specs=[in_vmem] * (outers + 1 + len(known)),
        out_specs=in_vmem,
        compiler_params=small,
        name="attend",
    )(*queries, text_pair, *known)
    results = pl.pallas_call(
        lambda *refs: complete_kernel(outers, *refs),
        out_shape=[shaped(heads, padded, head_size)] * outers,
        in_specs=[in_vmem] * (outers + 3),
        out_specs=[in_vmem] * outers,
        compiler_params=small,
        name="complete",
    )(*queries, late, trade(late, CORE), sums)

    returned = [
        trade(result, step * INNER) if step else result
        for step, result in zip(sources, results)
    ]
    return pl.pallas_call(
        lambda *refs: finish_kernel(heads, sources, *refs),
        out_shape=jax.ShapeDtypeStruct((tokens, row_width), attn_cache.dtype),
        in_specs=[in_smem] + [in_vmem] * (2 + outers),
        out_specs=in_vmem,
        compiler_params=small,
        name="finish",
    )(me, padded_slots, attn_cache, *returned)


def solution(mesh):
    return jax.shard_map(
        shards,
        mesh=mesh,
        in_specs=(
            P(("parts", "seq"), None, None),
            P(("parts", "seq")),
            P(("parts", "seq"), None),
            P(("parts", "seq"), None),
            P(("parts", "seq"), None),
            P("parts", None),
            P("parts", None),
            P(),
            P(),
        ),
        out_specs=P(("parts", "seq"), None),
        check_vma=False,
    )
```

```python
import math

import jax
import jax.numpy as jnp
from jax import lax
from jax.experimental import pallas as pl
from jax.experimental.pallas import tpu as pltpu
from jax.sharding import PartitionSpec as P

LOG2E = math.log2(math.e)
INNER = 2
MIB = 2**20


def round_up(count, step):
    return (count + step - 1) // step * step


def normalize(entries, scales):
    mean_square = jnp.mean(entries * entries, axis=-1, keepdims=True)
    return entries * lax.rsqrt(mean_square + 1e-06) * scales


def place(slots, tokens):
    owner = lax.broadcasted_iota(jnp.int32, (tokens, slots.shape[1]), 0)
    return owner == slots


def prepare_kernel(plan, groups, per_group, padded, with_text, me_ref, *refs):
    slots_hbm, q_gain_hbm, k_gain_hbm, qkv_hbm, k_hbm, v_hbm = refs[:6]
    rest = refs[6:]
    if with_text:
        text_k_hbm, text_v_hbm = rest[:2]
        rest = rest[3:]
    outs = []
    for _, apart in plan:
        taken = 2 if apart else 1
        outs.append(rest[:taken])
        rest = rest[taken:]
    if with_text:
        text_keys_ref, text_values_ref = rest[:2]
        rest = rest[2:]
    slots_ref, q_gain_ref, k_gain_ref, fresh_ref, k_ref, v_ref, text_ref, share_ref = rest[:8]
    small_sems, sems, text_sems = rest[8:]
    tokens, width = k_ref.shape[1:]
    head_size = q_gain_ref.shape[1]
    outer = me_ref[0] // INNER

    def columns(step):
        block = lax.bitwise_xor(outer // groups, step // groups)
        return pl.ds(pl.multiple_of(block * width, width), width)

    small = [
        pltpu.make_async_copy(slots_hbm, slots_ref, small_sems.at[0]),
        pltpu.make_async_copy(q_gain_hbm, q_gain_ref, small_sems.at[1]),
        pltpu.make_async_copy(k_gain_hbm, k_gain_ref, small_sems.at[2]),
    ]
    for copy in small:
        copy.start()
    loads = []
    for turn, (step, _) in enumerate(plan):
        mine = columns(step)
        loads.append(
            [
                pltpu.make_async_copy(
                    qkv_hbm.at[:, :, mine], fresh_ref.at[turn], sems.at[turn, 0]
                ),
                pltpu.make_async_copy(k_hbm.at[:, mine], k_ref.at[turn], sems.at[turn, 1]),
                pltpu.make_async_copy(v_hbm.at[:, mine], v_ref.at[turn], sems.at[turn, 2]),
            ]
        )
        for copy in loads[-1]:
            copy.start()
    if with_text:
        mine = columns(0)
        text_loads = [
            pltpu.make_async_copy(text_k_hbm.at[:, mine], text_ref.at[0], text_sems.at[0]),
            pltpu.make_async_copy(text_v_hbm.at[:, mine], text_ref.at[1], text_sems.at[1]),
        ]
        for copy in text_loads:
            copy.start()
    for copy in small:
        copy.wait()
    belongs = place(slots_ref[...], tokens)
    is_fresh = jnp.max(belongs.astype(jnp.float32), axis=1, keepdims=True) > 0.5
    one_hot = belongs.astype(jnp.bfloat16)
    q_gain = q_gain_ref[...]
    k_gain = k_gain_ref[...]

    def merged(fresh, cache):
        spread = jnp.dot(one_hot, fresh, preferred_element_type=jnp.float32)
        return jnp.where(is_fresh, spread, cache.astype(jnp.float32))

    for turn, (step, apart) in enumerate(plan):
        for copy in loads[turn]:
            copy.wait()
        group = lax.bitwise_xor(outer % groups, step % groups)
        for head in range(width // head_size):
            lanes = slice(head * head_size, (head + 1) * head_size)
            keys = normalize(merged(fresh_ref[turn, 1, :, lanes], k_ref[turn, :, lanes]), k_gain)
            values = merged(fresh_ref[turn, 2, :, lanes], v_ref[turn, :, lanes])
            queries = normalize(fresh_ref[turn, 0, :, lanes].astype(jnp.float32), q_gain)
            for part in range(groups):
                share = queries[part * per_group : (part + 1) * per_group]
                if padded > per_group:
                    empty = jnp.zeros((padded - per_group, head_size), jnp.float32)
                    share = jnp.concatenate([share, empty], axis=0)
                share_ref[part] = share.astype(jnp.bfloat16)
            outs[turn][0][head, :tokens] = keys.astype(jnp.bfloat16)
            outs[turn][0][head, tokens : 2 * tokens] = values.astype(jnp.bfloat16)
            if apart:
                outs[turn][1][head] = share_ref[group]
            else:
                outs[turn][0][head, 2 * tokens :] = share_ref[group]
    if with_text:
        for copy in text_loads:
            copy.wait()
        for head in range(width // head_size):
            lanes = slice(head * head_size, (head + 1) * head_size)
            text_keys = normalize(text_ref[0, :, lanes].astype(jnp.float32), k_gain)
            text_keys_ref[head] = text_keys.astype(jnp.bfloat16)
            text_values_ref[head] = text_ref[1, :, lanes]


def gather_kernel(tokens, extra, count, *refs):
    blocks, refs = refs[:count], refs[count:]
    if extra:
        own, other, text_keys, text_values, own_queries = refs[:5]
        refs = refs[5:]
        kept_ref = refs[2]
        text = text_keys.shape[1]
        for number, block in enumerate([own, other]):
            rows = slice(text + number * tokens, text + (number + 1) * tokens)
            kept_ref[:, 0, rows] = block[:, :tokens]
            kept_ref[:, 1, rows] = block[:, tokens:]
        kept_ref[:, 0, :text] = text_keys[...]
        kept_ref[:, 1, :text] = text_values[...]
        parts = [own_queries[...]]
    else:
        parts = []
    out_ref, queries_ref = refs[:2]
    for number, block in enumerate(blocks):
        rows = slice(number * tokens, (number + 1) * tokens)
        out_ref[:, 0, rows] = block[:, :tokens]
        out_ref[:, 1, rows] = block[:, tokens : 2 * tokens]
        parts.append(block[:, 2 * tokens :])
    padded = parts[0].shape[1]
    for number, part in enumerate(parts):
        queries_ref[:, number * padded : (number + 1) * padded] = part


def add_keys(sums, queries, keys, values):
    factor = queries.shape[1] ** (-0.5) * LOG2E
    scores = lax.dot_general(
        queries, keys, (((1,), (1,)), ((), ())), preferred_element_type=jnp.float32
    )
    weights = jnp.exp2(scores * factor).astype(jnp.bfloat16)
    beside = jnp.concatenate([values, jnp.ones_like(values)], axis=1)
    added = jnp.dot(weights, beside, preferred_element_type=jnp.float32)
    return added if sums is None else sums + added


def add_shared(sums, queries, shared, head, tokens):
    for ref in shared:
        rows = ref.shape[2]
        chunk = next(c * tokens for c in (7, 6, 5, 4, 3, 2, 1) if rows % (c * tokens) == 0)
        for first in range(0, rows, chunk):
            at = slice(first, first + chunk)
            sums = add_keys(sums, queries, ref[head, 0, at], ref[head, 1, at])
    return sums


def row_blocks(ref, padded):
    rows = ref.shape[1]
    return [slice(first, min(first + 4 * padded, rows)) for first in range(0, rows, 4 * padded)]


def attend_kernel(tokens, padded, *refs):
    shared, queries_ref, sums_ref = refs[:-2], refs[-2], refs[-1]
    for head in range(queries_ref.shape[0]):
        for rows in row_blocks(queries_ref, padded):
            sums_ref[head, rows] = add_shared(None, queries_ref[head, rows], shared, head, tokens)


def complete_kernel(tokens, first, shared_ref, queries_ref, sums_ref, *outs):
    heads, padded, head_size = outs[0].shape
    for head in range(heads):
        for number in range(0, len(outs), 4):
            mine = outs[number : number + 4]
            at = (first + number) * padded
            rows = slice(at, at + len(mine) * padded)
            sums = add_shared(
                sums_ref[head, rows], queries_ref[head, rows], [shared_ref], head, tokens
            )
            result = (sums[:, :head_size] / sums[:, head_size:]).astype(jnp.bfloat16)
            for turn, out_ref in enumerate(mine):
                out_ref[head] = result[turn * padded : (turn + 1) * padded]


def finish_kernel(heads, steps, me_ref, slots_ref, cache_ref, *rest):
    returned, out_ref = rest[:-1], rest[-1]
    tokens = cache_ref.shape[0]
    head_size = returned[0].shape[2]
    groups = slots_ref.shape[0]
    outer = me_ref[0] // INNER
    one_hot = []
    owned = jnp.zeros((tokens, 1), jnp.float32)
    for low in range(groups):
        group = lax.bitwise_xor(outer % groups, low)
        mine = place(slots_ref[pl.ds(group, 1)], tokens).astype(jnp.float32)
        owned = owned + jnp.sum(mine, axis=1, keepdims=True)
        one_hot.append(mine.astype(jnp.bfloat16))
    is_fresh = owned > 0.5
    for high in range(len(steps) // groups):
        block = lax.bitwise_xor(outer // groups, high)
        for head in range(heads):
            at = (block * heads + head) * head_size
            columns = pl.ds(pl.multiple_of(at, head_size), head_size)
            placed = jnp.zeros((tokens, head_size), jnp.float32)
            for low in range(groups):
                made = returned[steps.index(high * groups + low)][head]
                placed = placed + jnp.dot(one_hot[low], made, preferred_element_type=jnp.float32)
            out_ref[:, columns] = jnp.where(
                is_fresh, placed, cache_ref[:, columns].astype(jnp.float32)
            ).astype(out_ref.dtype)


def work(micros):
    return pl.CostEstimate(
        flops=int(micros * 1e9), bytes_accessed=int(micros * 3e6), transcendentals=0
    )


def trade(block, distance):
    count = lax.axis_size("seq")
    return lax.ppermute(block, "seq", [(a, a ^ distance) for a in range(count)])


def shards(fresh_qkv, slot_rows, k_cache, v_cache, attn_cache, text_k, text_v, q_gain, k_gain):
    seq_count = lax.axis_size("seq")
    me = lax.axis_index("seq").reshape(1)
    slot_count = slot_rows.shape[0]
    tokens, row_width = k_cache.shape
    text = text_k.shape[0]
    head_size = q_gain.shape[0]
    outers = seq_count // INNER
    all_heads = row_width // head_size
    heads = max(1, all_heads // outers)
    groups = outers * heads // all_heads
    per_group = slot_count // groups
    padded = round_up(per_group, 16)
    width = heads * head_size
    qkv = jnp.transpose(fresh_qkv, (1, 0, 2))
    q_gain = q_gain.reshape(1, head_size)
    k_gain = k_gain.reshape(1, head_size)
    slots = slot_rows.reshape(1, slot_count)
    padded_slots = jnp.pad(
        slot_rows.reshape(groups, per_group),
        ((0, 0), (0, padded - per_group)),
        constant_values=tokens,
    )

    def shaped(*shape, dtype=jnp.bfloat16):
        return jax.ShapeDtypeStruct(shape, dtype)

    in_hbm = pl.BlockSpec(memory_space=pltpu.HBM)
    in_vmem = pl.BlockSpec(memory_space=pltpu.VMEM)
    in_smem = pl.BlockSpec(memory_space=pltpu.SMEM)

    def prepare(plan, with_text, name, params, *extra):
        shapes = []
        for _, apart in plan:
            if apart:
                shapes += [shaped(heads, 2 * tokens, head_size), shaped(heads, padded, head_size)]
            else:
                shapes += [shaped(heads, 2 * tokens + padded, head_size)]
        if with_text:
            shapes += [shaped(heads, text, head_size)] * 2
        made = pl.pallas_call(
            lambda *refs: prepare_kernel(plan, groups, per_group, padded, with_text, *refs),
            out_shape=shapes,
            in_specs=[in_smem] + [in_hbm] * 6 + [in_hbm] * (2 * with_text)
            + [pl.BlockSpec(memory_space=pl.ANY)] * with_text,
            out_specs=[in_vmem] * len(shapes),
            scratch_shapes=[
                pltpu.VMEM((1, slot_count), jnp.int32),
                pltpu.VMEM((1, head_size), jnp.float32),
                pltpu.VMEM((1, head_size), jnp.float32),
                pltpu.VMEM((len(plan), 3, slot_count, width), jnp.bfloat16),
                pltpu.VMEM((len(plan), tokens, width), jnp.bfloat16),
                pltpu.VMEM((len(plan), tokens, width), jnp.bfloat16),
                pltpu.VMEM((2, text, width), jnp.bfloat16),
                pltpu.VMEM((groups, padded, head_size), jnp.bfloat16),
                pltpu.SemaphoreType.DMA((3,)),
                pltpu.SemaphoreType.DMA((len(plan), 3)),
                pltpu.SemaphoreType.DMA((2,)),
            ],
            compiler_params=params,
            name=name,
        )(me, slots, q_gain, k_gain, qkv, k_cache, v_cache, *extra)
        return list(made)

    half = outers // 2
    far = list(reversed(range(half, outers)))
    near = list(range(1, half))
    small = pltpu.CompilerParams(vmem_limit_bytes=24 * MIB)
    block, own, own_queries = prepare(
        [(far[0], False), (0, True)], False, "prepare_first", pltpu.CompilerParams()
    )
    arrived = {far[0]: trade(block, far[0] * INNER)}
    other = trade(own, 1)

    late = far[1:2]
    for turn in range(half):
        late += near[turn : turn + 1] + far[turn + 2 : turn + 3]
    *made, text_keys, text_values = prepare(
        [(step, False) for step in late], True, "prepare_rest", small, text_k, text_v, other
    )
    for step, block in zip(late, made):
        arrived[step] = trade(block, step * INNER)

    steps = [far[0]] + late
    count = len(steps) + 1
    keys, queries, kept = pl.pallas_call(
        lambda *refs: gather_kernel(tokens, True, len(steps), *refs),
        out_shape=[
            shaped(heads, 2, len(steps) * tokens, head_size),
            shaped(heads, count * padded, head_size),
            shaped(heads, 2, text + 2 * tokens, head_size),
        ],
        in_specs=[in_vmem] * (len(steps) + 5),
        out_specs=[in_vmem] * 3,
        compiler_params=small,
        name="gather",
    )(*[arrived[step] for step in steps], own, other, text_keys, text_values, own_queries)
    other_keys = trade(keys, 1)
    sums = pl.pallas_call(
        lambda *refs: attend_kernel(tokens, padded, *refs),
        out_shape=shaped(heads, count * padded, 2 * head_size, dtype=jnp.float32),
        in_specs=[in_vmem] * 3,
        out_specs=in_vmem,
        compiler_params=small,
        cost_estimate=work(5),
        name="attend",
    )(kept, keys, queries)

    sources = [0] + steps

    def complete(first, last, name):
        return pl.pallas_call(
            lambda *refs: complete_kernel(tokens, first, *refs),
            out_shape=[shaped(heads, padded, head_size)] * (last - first),
            in_specs=[in_vmem] * 3,
            out_specs=[in_vmem] * (last - first),
            compiler_params=small,
            name=name,
        )(other_keys, queries, sums)

    results = dict(zip(sources, complete(0, count, "complete")))
    order = near[-1:] + far + near[:-1]
    returned = {0: results[0]}
    for step in order:
        returned[step] = trade(results[step], step * INNER)
    order = order + [0]

    return pl.pallas_call(
        lambda *refs: finish_kernel(heads, order, *refs),
        out_shape=jax.ShapeDtypeStruct((tokens, row_width), attn_cache.dtype),
        in_specs=[in_smem] + [in_vmem] * (2 + len(order)),
        out_specs=in_vmem,
        compiler_params=small,
        name="finish",
    )(me, padded_slots, attn_cache, *[returned[step] for step in order])


def solution(mesh):
    return jax.shard_map(
        shards,
        mesh=mesh,
        in_specs=(
            P(("parts", "seq"), None, None),
            P(("parts", "seq")),
            P(("parts", "seq"), None),
            P(("parts", "seq"), None),
            P(("parts", "seq"), None),
            P("parts", None),
            P("parts", None),
            P(),
            P(),
        ),
        out_specs=P(("parts", "seq"), None),
        check_vma=False,
    )
```

```python
import math

import jax
import jax.numpy as jnp
from jax import lax
from jax.experimental import pallas as pl
from jax.experimental.pallas import tpu as pltpu
from jax.sharding import PartitionSpec as P

LOG2E = math.log2(math.e)
FIRST_HEADS = [15, 14, 13, 1]


def round_up(count, step):
    return (count + step - 1) // step * step


def normalize(entries, scales):
    mean_square = jnp.mean(entries * entries, axis=-1, keepdims=True)
    return entries * lax.rsqrt(mean_square + 1e-06) * scales


def place(slots, tokens):
    owner = lax.broadcasted_iota(jnp.int32, (tokens, slots.shape[1]), 0)
    return owner == slots


def prepare_kernel(per_group, padded, highs, by_head, me_ref, slots_ref, q_gain_ref, k_gain_ref, *rest):
    tokens = 0
    if by_head:
        groups = slots_ref.shape[1] // per_group
        loads = [rest[3 * turn : 3 * turn + 3] for turn in range(len(highs))]
        outs = rest[3 * len(highs) : 3 * len(highs) + groups * len(highs)]
        queries_ref = rest[-1]
        tokens = loads[0][1].shape[0]
    else:
        groups = slots_ref.shape[1] // per_group
        qkv_ref, k_ref, v_ref, text_k_ref, text_v_ref = rest[:5]
        rest = rest[6:]
        outs = rest[: groups * len(highs)]
        text_keys_ref, text_values_ref, queries_ref = rest[groups * len(highs) :]
        tokens = k_ref.shape[0]
    head_size = q_gain_ref.shape[1]
    me = me_ref[0]
    mine = place(slots_ref[...], tokens)
    is_fresh = jnp.max(mine.astype(jnp.float32), axis=1, keepdims=True) > 0.5
    one_hot = mine.astype(jnp.bfloat16)
    q_gain = q_gain_ref[...]
    k_gain = k_gain_ref[...]

    spare = []
    for group in range(groups):
        held = slots_ref[:, group * per_group : (group + 1) * per_group] < tokens
        fresh_count = jnp.sum(held.astype(jnp.float32), axis=1, keepdims=True)
        spare.append(jnp.broadcast_to(fresh_count, (padded - per_group, head_size)))

    def merged(fresh, cache):
        spread = jnp.dot(one_hot, fresh, preferred_element_type=jnp.float32)
        return jnp.where(is_fresh, spread, cache.astype(jnp.float32))

    for turn, high in enumerate(highs):
        if by_head:
            fresh_ref, cache_k_ref, cache_v_ref = loads[turn]
            fresh = [fresh_ref[part] for part in range(3)]
            cache_k, cache_v = cache_k_ref[...], cache_v_ref[...]
        else:
            head = lax.bitwise_xor(me // groups, high)
            columns = pl.ds(pl.multiple_of(head * head_size, head_size), head_size)
            fresh = [qkv_ref[part, :, columns] for part in range(3)]
            cache_k, cache_v = k_ref[:, columns], v_ref[:, columns]
        keys = normalize(merged(fresh[1], cache_k), k_gain).astype(jnp.bfloat16)
        values = merged(fresh[2], cache_v).astype(jnp.bfloat16)
        queries = normalize(fresh[0].astype(jnp.float32), q_gain)
        for group in range(groups):
            share = queries[group * per_group : (group + 1) * per_group]
            share = jnp.concatenate([share, spare[group]], axis=0)
            queries_ref[group] = share.astype(jnp.bfloat16)
        for low in range(groups):
            out_ref = outs[turn * groups + low]
            group = lax.bitwise_xor(me % groups, low)
            out_ref[:tokens] = keys
            out_ref[tokens : 2 * tokens] = values
            out_ref[2 * tokens :] = queries_ref[group]
    if not by_head:
        text_keys = normalize(text_k_ref[...].astype(jnp.float32), k_gain)
        text_keys_ref[...] = text_keys.astype(jnp.bfloat16)
        text_values_ref[...] = text_v_ref[...]


def attend_kernel(tokens, per_group, query_rows, key_rows, turns, steps, me_ref, *rest):
    me = me_ref[0]
    count = len(steps)
    arrived = rest[:count]
    text_keys_ref, text_values_ref = rest[count : count + 2]
    out_ref, queries_ref, keys_ref, values_ref, result_ref = rest[count + 2 :]
    head_size = text_keys_ref.shape[1]
    padded = arrived[0].shape[0] - 2 * tokens
    factor = head_size ** (-0.5) * LOG2E
    text = text_keys_ref.shape[0]
    keys_ref[:text] = text_keys_ref[...]
    values_ref[:text] = text_values_ref[...]
    for step in range(count):
        first = text + step * tokens
        keys_ref[first : first + tokens] = arrived[step][:tokens]
        values_ref[first : first + tokens] = arrived[step][tokens : 2 * tokens]

    last_rows = slice(2 * tokens + padded - 16, 2 * tokens + padded)
    count_row = per_group - (padded - 16)
    firsts = [0]
    for step in range(count):
        spare = arrived[step][last_rows].astype(jnp.float32)[count_row : count_row + 1]
        firsts.append(firsts[-1] + jnp.max(spare).astype(jnp.int32))
    result_ref[...] = jnp.zeros_like(result_ref)
    for step in range(count):
        rows = arrived[step][2 * tokens :].astype(jnp.float32)
        queries_ref[pl.ds(firsts[step], padded)] = rows
    after = query_rows + padded
    queries_ref[pl.ds(firsts[count], after)] = jnp.zeros((after, head_size), jnp.float32)

    def add_queries(step, carry):
        first_row = step * query_rows
        if not isinstance(step, int):
            first_row = pl.multiple_of(first_row, 16)
        mine = pl.ds(first_row, query_rows)
        queries = queries_ref[mine].astype(jnp.bfloat16)
        sums = None
        for first in range(0, keys_ref.shape[0], key_rows):
            scores = lax.dot_general(
                queries,
                keys_ref[first : first + key_rows],
                (((1,), (1,)), ((), ())),
                preferred_element_type=jnp.float32,
            )
            weights = jnp.exp2(scores * factor).astype(jnp.bfloat16)
            values = values_ref[first : first + key_rows]
            beside = jnp.concatenate([values, jnp.ones_like(values)], axis=1)
            added = jnp.dot(weights, beside, preferred_element_type=jnp.float32)
            sums = added if sums is None else sums + added
        result_ref[mine] = sums[:, :head_size] / sums[:, head_size:]
        return carry

    if turns is not None:
        for step in range(turns):
            add_queries(step, 0)
    else:
        lax.fori_loop(0, (firsts[count] + query_rows - 1) // query_rows, add_queries, 0)
    for step in range(count):
        owner = lax.bitwise_xor(me, steps[step])
        out_ref[owner] = result_ref[pl.ds(firsts[step], padded)].astype(jnp.bfloat16)


def finish_kernel(per_group, slots_ref, returned_ref, cache_ref, out_ref):
    tokens = cache_ref.shape[0]
    head_size = returned_ref.shape[2]
    groups = slots_ref.shape[0]
    heads = cache_ref.shape[1] // head_size
    mine = [place(slots_ref[group : group + 1], tokens) for group in range(groups)]
    count = sum(jnp.sum(m.astype(jnp.float32), axis=1, keepdims=True) for m in mine)
    is_fresh = count > 0.5
    one_hot = [m.astype(jnp.bfloat16) for m in mine]
    for head in range(heads):
        columns = slice(head * head_size, (head + 1) * head_size)
        placed = sum(
            jnp.dot(
                one_hot[group],
                returned_ref[head * groups + group],
                preferred_element_type=jnp.float32,
            )
            for group in range(groups)
        )
        out_ref[:, columns] = jnp.where(
            is_fresh, placed, cache_ref[:, columns].astype(jnp.float32)
        ).astype(out_ref.dtype)


def whole(shape):
    return pl.BlockSpec(shape, lambda i, me: (0,) * len(shape))


def partners(count):
    half = count // 2
    far = list(reversed(range(half, count)))
    near = list(reversed(range(1, half)))
    order = far[:3]
    for turn in range(max(len(far) - 3, len(near))):
        order += near[turn : turn + 1] + far[turn + 3 : turn + 4]
    names = sorted(range(count - 1), key=lambda number: str(number) if number else "")
    return [0] + [order[names.index(number)] for number in range(count - 1)]


def trade(block, step):
    if step == 0:
        return block
    count = lax.axis_size("seq")
    return lax.ppermute(block, "seq", [(a, a ^ step) for a in range(count)])


def shards(fresh_qkv, slot_rows, k_cache, v_cache, attn_cache, text_k, text_v, q_gain, k_gain):
    seq_count = lax.axis_size("seq")
    me = lax.axis_index("seq").reshape(1)
    slot_count = slot_rows.shape[0]
    tokens, row_width = k_cache.shape
    text = text_k.shape[0]
    head_size = q_gain.shape[0]
    head_count = row_width // head_size
    groups = seq_count // head_count
    per_group = slot_count // groups
    padded = round_up(per_group + 1, 16)
    rows = 2 * tokens + padded
    q_gain = q_gain.reshape(1, head_size)
    k_gain = k_gain.reshape(1, head_size)
    qkv = jnp.transpose(fresh_qkv, (1, 0, 2))
    slots = slot_rows.reshape(1, slot_count)
    padded_slots = jnp.pad(
        slot_rows.reshape(groups, per_group),
        ((0, 0), (0, padded - per_group)),
        constant_values=tokens,
    )

    steps = partners(seq_count)
    block = jax.ShapeDtypeStruct((rows, head_size), jnp.bfloat16)
    text_block = jax.ShapeDtypeStruct((text, head_size), jnp.bfloat16)
    scratch = [pltpu.VMEM((groups, padded, head_size), jnp.bfloat16)]
    common = [whole((1, slot_count)), whole((1, head_size)), whole((1, head_size))]
    early = FIRST_HEADS
    late = [high for high in reversed(range(head_count)) if high not in early]

    def head_specs(high):
        def column(me):
            return lax.bitwise_xor(me[0] // groups, high)

        return [
            pl.BlockSpec((3, slot_count, head_size), lambda i, me: (0, 0, column(me))),
            pl.BlockSpec((tokens, head_size), lambda i, me: (0, column(me))),
            pl.BlockSpec((tokens, head_size), lambda i, me: (0, column(me))),
        ]

    first = pl.pallas_call(
        lambda *refs: prepare_kernel(per_group, padded, early, True, *refs),
        out_shape=[block] * (groups * len(early)),
        grid_spec=pltpu.PrefetchScalarGridSpec(
            num_scalar_prefetch=1,
            grid=(1,),
            in_specs=common + [spec for high in early for spec in head_specs(high)],
            out_specs=[whole((rows, head_size))] * (groups * len(early)),
            scratch_shapes=scratch,
        ),
        name="prepare_first",
    )(me, slots, q_gain, k_gain, *([qkv, k_cache, v_cache] * len(early)))
    met = {}
    for turn, made in enumerate(first):
        step = early[turn // groups] * groups + turn % groups
        met[step] = trade(made, step)
    text_spec = pl.BlockSpec((text, head_size), lambda i, me: (0, me[0] // groups))
    *second, text_keys, text_values = pl.pallas_call(
        lambda *refs: prepare_kernel(per_group, padded, late, False, *refs),
        out_shape=[block] * (groups * len(late)) + [text_block] * 2,
        grid_spec=pltpu.PrefetchScalarGridSpec(
            num_scalar_prefetch=1,
            grid=(1,),
            in_specs=common
            + [
                whole((3, slot_count, row_width)),
                whole((tokens, row_width)),
                whole((tokens, row_width)),
                text_spec,
                text_spec,
                pl.BlockSpec(memory_space=pl.ANY),
            ],
            out_specs=[whole((rows, head_size))] * (groups * len(late))
            + [whole((text, head_size))] * 2,
            scratch_shapes=scratch,
        ),
        compiler_params=pltpu.CompilerParams(vmem_limit_bytes=24 * 2**20),
        name="prepare_rest",
    )(me, slots, q_gain, k_gain, qkv, k_cache, v_cache, text_k, text_v, met[groups])
    arrived = dict(met)
    for turn, made in enumerate(second):
        step = late[turn // groups] * groups + turn % groups
        arrived[step] = trade(made, step)
    arrived = [arrived[step] for step in steps]

    all_fresh = seq_count * slot_count // 2
    query_rows = 4 * slot_count
    turns = -(-all_fresh // query_rows) if groups == 1 else None
    packed_rows = seq_count * padded + query_rows + padded
    all_keys = text + seq_count * tokens
    result = pl.pallas_call(
        lambda *refs: attend_kernel(
            tokens, per_group, query_rows, 768, turns, steps, *refs
        ),
        out_shape=jax.ShapeDtypeStruct((seq_count, padded, head_size), jnp.bfloat16),
        grid_spec=pltpu.PrefetchScalarGridSpec(
            num_scalar_prefetch=1,
            grid=(1,),
            in_specs=[whole((rows, head_size))] * seq_count
            + [whole((text, head_size))] * 2,
            out_specs=whole((seq_count, padded, head_size)),
            scratch_shapes=[
                pltpu.VMEM((packed_rows, head_size), jnp.float32),
                pltpu.VMEM((all_keys, head_size), jnp.bfloat16),
                pltpu.VMEM((all_keys, head_size), jnp.bfloat16),
                pltpu.VMEM((packed_rows, head_size), jnp.float32),
            ],
        ),
        compiler_params=pltpu.CompilerParams(vmem_limit_bytes=40 * 2**20),
        name="attend",
    )(me, *arrived, text_keys, text_values)

    returned = lax.all_to_all(result, "seq", split_axis=0, concat_axis=0, tiled=True)

    finish_steps = 1
    return pl.pallas_call(
        lambda *refs: finish_kernel(per_group, *refs),
        out_shape=jax.ShapeDtypeStruct((tokens, row_width), attn_cache.dtype),
        grid=(finish_steps,),
        in_specs=[
            pl.BlockSpec((groups, padded), lambda i: (0, 0)),
            pl.BlockSpec((seq_count // finish_steps, padded, head_size), lambda i: (i, 0, 0)),
            pl.BlockSpec((tokens, row_width // finish_steps), lambda i: (0, i)),
        ],
        out_specs=pl.BlockSpec((tokens, row_width // finish_steps), lambda i: (0, i)),
        compiler_params=pltpu.CompilerParams(vmem_limit_bytes=32 * 2**20),
        name="finish",
    )(padded_slots, returned, attn_cache)


def solution(mesh):
    return jax.shard_map(
        shards,
        mesh=mesh,
        in_specs=(
            P(("parts", "seq"), None, None),
            P(("parts", "seq")),
            P(("parts", "seq"), None),
            P(("parts", "seq"), None),
            P(("parts", "seq"), None),
            P("parts", None),
            P("parts", None),
            P(),
            P(),
        ),
        out_specs=P(("parts", "seq"), None),
        check_vma=False,
    )
```

```python
import math

import jax
import jax.numpy as jnp
from jax import lax
from jax.experimental import pallas as pl
from jax.experimental.pallas import tpu as pltpu
from jax.sharding import PartitionSpec as P

LOG2E = math.log2(math.e)
FIRST_HEADS = [15, 14, 13, 1]


def round_up(count, step):
    return (count + step - 1) // step * step


def normalize(entries, scales):
    mean_square = jnp.mean(entries * entries, axis=-1, keepdims=True)
    return entries * lax.rsqrt(mean_square + 1e-06) * scales


def place(slots, tokens):
    owner = lax.broadcasted_iota(jnp.int32, (tokens, slots.shape[1]), 0)
    return owner == slots


def prepare_kernel(per_group, padded, highs, by_head, me_ref, slots_ref, q_gain_ref, k_gain_ref, *rest):
    tokens = 0
    if by_head:
        groups = slots_ref.shape[1] // per_group
        loads = [rest[3 * turn : 3 * turn + 3] for turn in range(len(highs))]
        outs = rest[3 * len(highs) : 3 * len(highs) + groups * len(highs)]
        queries_ref = rest[-1]
        tokens = loads[0][1].shape[0]
    else:
        groups = slots_ref.shape[1] // per_group
        qkv_ref, k_ref, v_ref, text_k_ref, text_v_ref = rest[:5]
        rest = rest[6:]
        outs = rest[: groups * len(highs)]
        text_keys_ref, text_values_ref, queries_ref = rest[groups * len(highs) :]
        tokens = k_ref.shape[0]
    head_size = q_gain_ref.shape[1]
    me = me_ref[0]
    mine = place(slots_ref[...], tokens)
    is_fresh = jnp.max(mine.astype(jnp.float32), axis=1, keepdims=True) > 0.5
    one_hot = mine.astype(jnp.bfloat16)
    q_gain = q_gain_ref[...]
    k_gain = k_gain_ref[...]

    spare = []
    for group in range(groups):
        held = slots_ref[:, group * per_group : (group + 1) * per_group] < tokens
        fresh_count = jnp.sum(held.astype(jnp.float32), axis=1, keepdims=True)
        spare.append(jnp.broadcast_to(fresh_count, (padded - per_group, head_size)))

    def merged(fresh, cache):
        spread = jnp.dot(one_hot, fresh, preferred_element_type=jnp.float32)
        return jnp.where(is_fresh, spread, cache.astype(jnp.float32))

    for turn, high in enumerate(highs):
        if by_head:
            fresh_ref, cache_k_ref, cache_v_ref = loads[turn]
            fresh = [fresh_ref[part] for part in range(3)]
            cache_k, cache_v = cache_k_ref[...], cache_v_ref[...]
        else:
            head = lax.bitwise_xor(me // groups, high)
            columns = pl.ds(pl.multiple_of(head * head_size, head_size), head_size)
            fresh = [qkv_ref[part, :, columns] for part in range(3)]
            cache_k, cache_v = k_ref[:, columns], v_ref[:, columns]
        keys = normalize(merged(fresh[1], cache_k), k_gain).astype(jnp.bfloat16)
        values = merged(fresh[2], cache_v).astype(jnp.bfloat16)
        queries = normalize(fresh[0].astype(jnp.float32), q_gain)
        for group in range(groups):
            share = queries[group * per_group : (group + 1) * per_group]
            share = jnp.concatenate([share, spare[group]], axis=0)
            queries_ref[group] = share.astype(jnp.bfloat16)
        for low in range(groups):
            out_ref = outs[turn * groups + low]
            group = lax.bitwise_xor(me % groups, low)
            out_ref[:tokens] = keys
            out_ref[tokens : 2 * tokens] = values
            out_ref[2 * tokens :] = queries_ref[group]
    if not by_head:
        text_keys = normalize(text_k_ref[...].astype(jnp.float32), k_gain)
        text_keys_ref[...] = text_keys.astype(jnp.bfloat16)
        text_values_ref[...] = text_v_ref[...]


def attend_kernel(tokens, per_group, query_rows, key_rows, turns, steps, me_ref, *rest):
    me = me_ref[0]
    count = len(steps)
    arrived = rest[:count]
    text_keys_ref, text_values_ref = rest[count : count + 2]
    out_ref, queries_ref, keys_ref, values_ref, result_ref = rest[count + 2 :]
    head_size = text_keys_ref.shape[1]
    padded = arrived[0].shape[0] - 2 * tokens
    factor = head_size ** (-0.5) * LOG2E
    text = text_keys_ref.shape[0]
    keys_ref[:text] = text_keys_ref[...]
    values_ref[:text] = text_values_ref[...]
    for step in range(count):
        first = text + step * tokens
        keys_ref[first : first + tokens] = arrived[step][:tokens]
        values_ref[first : first + tokens] = arrived[step][tokens : 2 * tokens]

    last_rows = slice(2 * tokens + padded - 16, 2 * tokens + padded)
    count_row = per_group - (padded - 16)
    firsts = [0]
    for step in range(count):
        spare = arrived[step][last_rows].astype(jnp.float32)[count_row : count_row + 1]
        firsts.append(firsts[-1] + jnp.max(spare).astype(jnp.int32))
    result_ref[...] = jnp.zeros_like(result_ref)
    for step in range(count):
        rows = arrived[step][2 * tokens :].astype(jnp.float32)
        queries_ref[pl.ds(firsts[step], padded)] = rows
    after = query_rows + padded
    queries_ref[pl.ds(firsts[count], after)] = jnp.zeros((after, head_size), jnp.float32)

    def add_queries(step, carry):
        first_row = step * query_rows
        if not isinstance(step, int):
            first_row = pl.multiple_of(first_row, 16)
        mine = pl.ds(first_row, query_rows)
        queries = queries_ref[mine].astype(jnp.bfloat16)
        sums = None
        for first in range(0, keys_ref.shape[0], key_rows):
            scores = lax.dot_general(
                queries,
                keys_ref[first : first + key_rows],
                (((1,), (1,)), ((), ())),
                preferred_element_type=jnp.float32,
            )
            weights = jnp.exp2(scores * factor).astype(jnp.bfloat16)
            values = values_ref[first : first + key_rows]
            beside = jnp.concatenate([values, jnp.ones_like(values)], axis=1)
            added = jnp.dot(weights, beside, preferred_element_type=jnp.float32)
            sums = added if sums is None else sums + added
        result_ref[mine] = sums[:, :head_size] / sums[:, head_size:]
        return carry

    if turns is not None:
        for step in range(turns):
            add_queries(step, 0)
    else:
        lax.fori_loop(0, (firsts[count] + query_rows - 1) // query_rows, add_queries, 0)
    for step in range(count):
        owner = lax.bitwise_xor(me, steps[step])
        out_ref[owner] = result_ref[pl.ds(firsts[step], padded)].astype(jnp.bfloat16)


def finish_kernel(per_group, slots_ref, returned_ref, cache_ref, out_ref):
    tokens = cache_ref.shape[0]
    head_size = returned_ref.shape[2]
    groups = slots_ref.shape[0]
    heads = cache_ref.shape[1] // head_size
    mine = [place(slots_ref[group : group + 1], tokens) for group in range(groups)]
    count = sum(jnp.sum(m.astype(jnp.float32), axis=1, keepdims=True) for m in mine)
    is_fresh = count > 0.5
    one_hot = [m.astype(jnp.bfloat16) for m in mine]
    for head in range(heads):
        columns = slice(head * head_size, (head + 1) * head_size)
        placed = sum(
            jnp.dot(
                one_hot[group],
                returned_ref[head * groups + group],
                preferred_element_type=jnp.float32,
            )
            for group in range(groups)
        )
        out_ref[:, columns] = jnp.where(
            is_fresh, placed, cache_ref[:, columns].astype(jnp.float32)
        ).astype(out_ref.dtype)


def whole(shape):
    return pl.BlockSpec(shape, lambda i, me: (0,) * len(shape))


def partners(count):
    half = count // 2
    far = list(reversed(range(half, count)))
    near = list(reversed(range(1, half)))
    order = far[:3] + near[:1] + far[3:4] + near[1:2] + far[4:6] + near[2:3] + far[6:] + near[3:]
    names = sorted(range(count - 1), key=lambda number: str(number) if number else "")
    return [0] + [order[names.index(number)] for number in range(count - 1)]


def trade(block, step):
    if step == 0:
        return block
    count = lax.axis_size("seq")
    return lax.ppermute(block, "seq", [(a, a ^ step) for a in range(count)])


def shards(fresh_qkv, slot_rows, k_cache, v_cache, attn_cache, text_k, text_v, q_gain, k_gain):
    seq_count = lax.axis_size("seq")
    me = lax.axis_index("seq").reshape(1)
    slot_count = slot_rows.shape[0]
    tokens, row_width = k_cache.shape
    text = text_k.shape[0]
    head_size = q_gain.shape[0]
    head_count = row_width // head_size
    groups = seq_count // head_count
    per_group = slot_count // groups
    padded = round_up(per_group + 1, 16)
    rows = 2 * tokens + padded
    q_gain = q_gain.reshape(1, head_size)
    k_gain = k_gain.reshape(1, head_size)
    qkv = jnp.transpose(fresh_qkv, (1, 0, 2))
    slots = slot_rows.reshape(1, slot_count)
    padded_slots = jnp.pad(
        slot_rows.reshape(groups, per_group),
        ((0, 0), (0, padded - per_group)),
        constant_values=tokens,
    )

    steps = partners(seq_count)
    block = jax.ShapeDtypeStruct((rows, head_size), jnp.bfloat16)
    text_block = jax.ShapeDtypeStruct((text, head_size), jnp.bfloat16)
    scratch = [pltpu.VMEM((groups, padded, head_size), jnp.bfloat16)]
    common = [whole((1, slot_count)), whole((1, head_size)), whole((1, head_size))]
    early = FIRST_HEADS
    late = [high for high in reversed(range(head_count)) if high not in early]

    def head_specs(high):
        def column(me):
            return lax.bitwise_xor(me[0] // groups, high)

        return [
            pl.BlockSpec((3, slot_count, head_size), lambda i, me: (0, 0, column(me))),
            pl.BlockSpec((tokens, head_size), lambda i, me: (0, column(me))),
            pl.BlockSpec((tokens, head_size), lambda i, me: (0, column(me))),
        ]

    first = pl.pallas_call(
        lambda *refs: prepare_kernel(per_group, padded, early, True, *refs),
        out_shape=[block] * (groups * len(early)),
        grid_spec=pltpu.PrefetchScalarGridSpec(
            num_scalar_prefetch=1,
            grid=(1,),
            in_specs=common + [spec for high in early for spec in head_specs(high)],
            out_specs=[whole((rows, head_size))] * (groups * len(early)),
            scratch_shapes=scratch,
        ),
        name="prepare_first",
    )(me, slots, q_gain, k_gain, *([qkv, k_cache, v_cache] * len(early)))
    met = {}
    for turn, made in enumerate(first):
        step = early[turn // groups] * groups + turn % groups
        met[step] = trade(made, step)
    text_spec = pl.BlockSpec((text, head_size), lambda i, me: (0, me[0] // groups))
    *second, text_keys, text_values = pl.pallas_call(
        lambda *refs: prepare_kernel(per_group, padded, late, False, *refs),
        out_shape=[block] * (groups * len(late)) + [text_block] * 2,
        grid_spec=pltpu.PrefetchScalarGridSpec(
            num_scalar_prefetch=1,
            grid=(1,),
            in_specs=common
            + [
                whole((3, slot_count, row_width)),
                whole((tokens, row_width)),
                whole((tokens, row_width)),
                text_spec,
                text_spec,
                pl.BlockSpec(memory_space=pl.ANY),
            ],
            out_specs=[whole((rows, head_size))] * (groups * len(late))
            + [whole((text, head_size))] * 2,
            scratch_shapes=scratch,
        ),
        compiler_params=pltpu.CompilerParams(vmem_limit_bytes=24 * 2**20),
        name="prepare_rest",
    )(me, slots, q_gain, k_gain, qkv, k_cache, v_cache, text_k, text_v, met[groups])
    arrived = dict(met)
    for turn, made in enumerate(second):
        step = late[turn // groups] * groups + turn % groups
        arrived[step] = trade(made, step)
    arrived = [arrived[step] for step in steps]

    all_fresh = seq_count * slot_count // 2
    query_rows = 4 * slot_count
    turns = -(-all_fresh // query_rows) if groups == 1 else None
    packed_rows = seq_count * padded + query_rows + padded
    all_keys = text + seq_count * tokens
    result = pl.pallas_call(
        lambda *refs: attend_kernel(
            tokens, per_group, query_rows, 768, turns, steps, *refs
        ),
        out_shape=jax.ShapeDtypeStruct((seq_count, padded, head_size), jnp.bfloat16),
        grid_spec=pltpu.PrefetchScalarGridSpec(
            num_scalar_prefetch=1,
            grid=(1,),
            in_specs=[whole((rows, head_size))] * seq_count
            + [whole((text, head_size))] * 2,
            out_specs=whole((seq_count, padded, head_size)),
            scratch_shapes=[
                pltpu.VMEM((packed_rows, head_size), jnp.float32),
                pltpu.VMEM((all_keys, head_size), jnp.bfloat16),
                pltpu.VMEM((all_keys, head_size), jnp.bfloat16),
                pltpu.VMEM((packed_rows, head_size), jnp.float32),
            ],
        ),
        compiler_params=pltpu.CompilerParams(vmem_limit_bytes=40 * 2**20),
        name="attend",
    )(me, *arrived, text_keys, text_values)

    returned = lax.all_to_all(result, "seq", split_axis=0, concat_axis=0, tiled=True)

    finish_steps = 1
    return pl.pallas_call(
        lambda *refs: finish_kernel(per_group, *refs),
        out_shape=jax.ShapeDtypeStruct((tokens, row_width), attn_cache.dtype),
        grid=(finish_steps,),
        in_specs=[
            pl.BlockSpec((groups, padded), lambda i: (0, 0)),
            pl.BlockSpec((seq_count // finish_steps, padded, head_size), lambda i: (i, 0, 0)),
            pl.BlockSpec((tokens, row_width // finish_steps), lambda i: (0, i)),
        ],
        out_specs=pl.BlockSpec((tokens, row_width // finish_steps), lambda i: (0, i)),
        compiler_params=pltpu.CompilerParams(vmem_limit_bytes=32 * 2**20),
        name="finish",
    )(padded_slots, returned, attn_cache)


def solution(mesh):
    return jax.shard_map(
        shards,
        mesh=mesh,
        in_specs=(
            P(("parts", "seq"), None, None),
            P(("parts", "seq")),
            P(("parts", "seq"), None),
            P(("parts", "seq"), None),
            P(("parts", "seq"), None),
            P("parts", None),
            P("parts", None),
            P(),
            P(),
        ),
        out_specs=P(("parts", "seq"), None),
        check_vma=False,
    )
```

```python
import math

import jax
import jax.numpy as jnp
from jax import lax
from jax.experimental import pallas as pl
from jax.experimental.pallas import tpu as pltpu
from jax.sharding import PartitionSpec as P

LOG2E = math.log2(math.e)
FIRST_HEADS = [15, 14, 13, 1]


def round_up(count, step):
    return (count + step - 1) // step * step


def normalize(entries, scales):
    mean_square = jnp.mean(entries * entries, axis=-1, keepdims=True)
    return entries * lax.rsqrt(mean_square + 1e-06) * scales


def place(slots, tokens):
    owner = lax.broadcasted_iota(jnp.int32, (tokens, slots.shape[1]), 0)
    return owner == slots


def prepare_kernel(per_group, padded, highs, by_head, me_ref, slots_ref, q_gain_ref, k_gain_ref, *rest):
    tokens = 0
    if by_head:
        groups = slots_ref.shape[1] // per_group
        loads = [rest[3 * turn : 3 * turn + 3] for turn in range(len(highs))]
        outs = rest[3 * len(highs) : 3 * len(highs) + groups * len(highs)]
        queries_ref = rest[-1]
        tokens = loads[0][1].shape[0]
    else:
        groups = slots_ref.shape[1] // per_group
        qkv_ref, k_ref, v_ref, text_k_ref, text_v_ref = rest[:5]
        rest = rest[6:]
        outs = rest[: groups * len(highs)]
        text_keys_ref, text_values_ref, queries_ref = rest[groups * len(highs) :]
        tokens = k_ref.shape[0]
    head_size = q_gain_ref.shape[1]
    me = me_ref[0]
    mine = place(slots_ref[...], tokens)
    is_fresh = jnp.max(mine.astype(jnp.float32), axis=1, keepdims=True) > 0.5
    one_hot = mine.astype(jnp.bfloat16)
    q_gain = q_gain_ref[...]
    k_gain = k_gain_ref[...]

    spare = []
    for group in range(groups):
        held = slots_ref[:, group * per_group : (group + 1) * per_group] < tokens
        fresh_count = jnp.sum(held.astype(jnp.float32), axis=1, keepdims=True)
        spare.append(jnp.broadcast_to(fresh_count, (padded - per_group, head_size)))

    def merged(fresh, cache):
        spread = jnp.dot(one_hot, fresh, preferred_element_type=jnp.float32)
        return jnp.where(is_fresh, spread, cache.astype(jnp.float32))

    for turn, high in enumerate(highs):
        if by_head:
            fresh_ref, cache_k_ref, cache_v_ref = loads[turn]
            fresh = [fresh_ref[part] for part in range(3)]
            cache_k, cache_v = cache_k_ref[...], cache_v_ref[...]
        else:
            head = lax.bitwise_xor(me // groups, high)
            columns = pl.ds(pl.multiple_of(head * head_size, head_size), head_size)
            fresh = [qkv_ref[part, :, columns] for part in range(3)]
            cache_k, cache_v = k_ref[:, columns], v_ref[:, columns]
        keys = normalize(merged(fresh[1], cache_k), k_gain).astype(jnp.bfloat16)
        values = merged(fresh[2], cache_v).astype(jnp.bfloat16)
        queries = normalize(fresh[0].astype(jnp.float32), q_gain)
        for group in range(groups):
            share = queries[group * per_group : (group + 1) * per_group]
            share = jnp.concatenate([share, spare[group]], axis=0)
            queries_ref[group] = share.astype(jnp.bfloat16)
        for low in range(groups):
            out_ref = outs[turn * groups + low]
            group = lax.bitwise_xor(me % groups, low)
            out_ref[:tokens] = keys
            out_ref[tokens : 2 * tokens] = values
            out_ref[2 * tokens :] = queries_ref[group]
    if not by_head:
        text_keys = normalize(text_k_ref[...].astype(jnp.float32), k_gain)
        text_keys_ref[...] = text_keys.astype(jnp.bfloat16)
        text_values_ref[...] = text_v_ref[...]


def attend_kernel(tokens, per_group, query_rows, key_rows, turns, steps, me_ref, *rest):
    me = me_ref[0]
    count = len(steps)
    arrived = rest[:count]
    text_keys_ref, text_values_ref = rest[count : count + 2]
    out_ref, queries_ref, keys_ref, values_ref, result_ref = rest[count + 2 :]
    head_size = text_keys_ref.shape[1]
    padded = arrived[0].shape[0] - 2 * tokens
    factor = head_size ** (-0.5) * LOG2E
    text = text_keys_ref.shape[0]
    keys_ref[:text] = text_keys_ref[...]
    values_ref[:text] = text_values_ref[...]
    for step in range(count):
        first = text + step * tokens
        keys_ref[first : first + tokens] = arrived[step][:tokens]
        values_ref[first : first + tokens] = arrived[step][tokens : 2 * tokens]

    last_rows = slice(2 * tokens + padded - 16, 2 * tokens + padded)
    count_row = per_group - (padded - 16)
    firsts = [0]
    for step in range(count):
        spare = arrived[step][last_rows].astype(jnp.float32)[count_row : count_row + 1]
        firsts.append(firsts[-1] + jnp.max(spare).astype(jnp.int32))
    result_ref[...] = jnp.zeros_like(result_ref)
    for step in range(count):
        rows = arrived[step][2 * tokens :].astype(jnp.float32)
        queries_ref[pl.ds(firsts[step], padded)] = rows
    after = query_rows + padded
    queries_ref[pl.ds(firsts[count], after)] = jnp.zeros((after, head_size), jnp.float32)

    def add_queries(step, carry):
        first_row = step * query_rows
        if not isinstance(step, int):
            first_row = pl.multiple_of(first_row, 16)
        mine = pl.ds(first_row, query_rows)
        queries = queries_ref[mine].astype(jnp.bfloat16)
        sums = None
        for first in range(0, keys_ref.shape[0], key_rows):
            scores = lax.dot_general(
                queries,
                keys_ref[first : first + key_rows],
                (((1,), (1,)), ((), ())),
                preferred_element_type=jnp.float32,
            )
            weights = jnp.exp2(scores * factor).astype(jnp.bfloat16)
            values = values_ref[first : first + key_rows]
            beside = jnp.concatenate([values, jnp.ones_like(values)], axis=1)
            added = jnp.dot(weights, beside, preferred_element_type=jnp.float32)
            sums = added if sums is None else sums + added
        result_ref[mine] = sums[:, :head_size] / sums[:, head_size:]
        return carry

    if turns is not None:
        for step in range(turns):
            add_queries(step, 0)
    else:
        lax.fori_loop(0, (firsts[count] + query_rows - 1) // query_rows, add_queries, 0)
    for step in range(count):
        owner = lax.bitwise_xor(me, steps[step])
        out_ref[owner] = result_ref[pl.ds(firsts[step], padded)].astype(jnp.bfloat16)


def finish_kernel(per_group, slots_ref, returned_ref, cache_ref, out_ref):
    tokens = cache_ref.shape[0]
    head_size = returned_ref.shape[2]
    groups = slots_ref.shape[0]
    heads = cache_ref.shape[1] // head_size
    mine = [place(slots_ref[group : group + 1], tokens) for group in range(groups)]
    count = sum(jnp.sum(m.astype(jnp.float32), axis=1, keepdims=True) for m in mine)
    is_fresh = count > 0.5
    one_hot = [m.astype(jnp.bfloat16) for m in mine]
    for head in range(heads):
        columns = slice(head * head_size, (head + 1) * head_size)
        placed = sum(
            jnp.dot(
                one_hot[group],
                returned_ref[head * groups + group],
                preferred_element_type=jnp.float32,
            )
            for group in range(groups)
        )
        out_ref[:, columns] = jnp.where(
            is_fresh, placed, cache_ref[:, columns].astype(jnp.float32)
        ).astype(out_ref.dtype)


def whole(shape):
    return pl.BlockSpec(shape, lambda i, me: (0,) * len(shape))


def partners(count):
    half = count // 2
    far = list(reversed(range(half, count)))
    near = list(reversed(range(1, half)))
    order = far[:3]
    for turn in range(max(len(far) - 3, len(near))):
        order += near[turn : turn + 1] + far[turn + 3 : turn + 4]
    names = sorted(range(count - 1), key=lambda number: str(number) if number else "")
    return [0] + [order[names.index(number)] for number in range(count - 1)]


def trade(block, step):
    if step == 0:
        return block
    count = lax.axis_size("seq")
    return lax.ppermute(block, "seq", [(a, a ^ step) for a in range(count)])


def shards(fresh_qkv, slot_rows, k_cache, v_cache, attn_cache, text_k, text_v, q_gain, k_gain):
    seq_count = lax.axis_size("seq")
    me = lax.axis_index("seq").reshape(1)
    slot_count = slot_rows.shape[0]
    tokens, row_width = k_cache.shape
    text = text_k.shape[0]
    head_size = q_gain.shape[0]
    head_count = row_width // head_size
    groups = seq_count // head_count
    per_group = slot_count // groups
    padded = round_up(per_group + 1, 16)
    rows = 2 * tokens + padded
    q_gain = q_gain.reshape(1, head_size)
    k_gain = k_gain.reshape(1, head_size)
    qkv = jnp.transpose(fresh_qkv, (1, 0, 2))
    slots = slot_rows.reshape(1, slot_count)
    padded_slots = jnp.pad(
        slot_rows.reshape(groups, per_group),
        ((0, 0), (0, padded - per_group)),
        constant_values=tokens,
    )

    steps = partners(seq_count)
    block = jax.ShapeDtypeStruct((rows, head_size), jnp.bfloat16)
    text_block = jax.ShapeDtypeStruct((text, head_size), jnp.bfloat16)
    scratch = [pltpu.VMEM((groups, padded, head_size), jnp.bfloat16)]
    common = [whole((1, slot_count)), whole((1, head_size)), whole((1, head_size))]
    early = FIRST_HEADS
    late = [high for high in reversed(range(head_count)) if high not in early]

    def head_specs(high):
        def column(me):
            return lax.bitwise_xor(me[0] // groups, high)

        return [
            pl.BlockSpec((3, slot_count, head_size), lambda i, me: (0, 0, column(me))),
            pl.BlockSpec((tokens, head_size), lambda i, me: (0, column(me))),
            pl.BlockSpec((tokens, head_size), lambda i, me: (0, column(me))),
        ]

    first = pl.pallas_call(
        lambda *refs: prepare_kernel(per_group, padded, early, True, *refs),
        out_shape=[block] * (groups * len(early)),
        grid_spec=pltpu.PrefetchScalarGridSpec(
            num_scalar_prefetch=1,
            grid=(1,),
            in_specs=common + [spec for high in early for spec in head_specs(high)],
            out_specs=[whole((rows, head_size))] * (groups * len(early)),
            scratch_shapes=scratch,
        ),
        name="prepare_first",
    )(me, slots, q_gain, k_gain, *([qkv, k_cache, v_cache] * len(early)))
    met = {}
    for turn, made in enumerate(first):
        step = early[turn // groups] * groups + turn % groups
        met[step] = trade(made, step)
    text_spec = pl.BlockSpec((text, head_size), lambda i, me: (0, me[0] // groups))
    *second, text_keys, text_values = pl.pallas_call(
        lambda *refs: prepare_kernel(per_group, padded, late, False, *refs),
        out_shape=[block] * (groups * len(late)) + [text_block] * 2,
        grid_spec=pltpu.PrefetchScalarGridSpec(
            num_scalar_prefetch=1,
            grid=(1,),
            in_specs=common
            + [
                whole((3, slot_count, row_width)),
                whole((tokens, row_width)),
                whole((tokens, row_width)),
                text_spec,
                text_spec,
                pl.BlockSpec(memory_space=pl.ANY),
            ],
            out_specs=[whole((rows, head_size))] * (groups * len(late))
            + [whole((text, head_size))] * 2,
            scratch_shapes=scratch,
        ),
        compiler_params=pltpu.CompilerParams(vmem_limit_bytes=24 * 2**20),
        name="prepare_rest",
    )(me, slots, q_gain, k_gain, qkv, k_cache, v_cache, text_k, text_v, met[groups])
    arrived = dict(met)
    for turn, made in enumerate(second):
        step = late[turn // groups] * groups + turn % groups
        arrived[step] = trade(made, step)
    arrived = [arrived[step] for step in steps]

    all_fresh = seq_count * slot_count // 2
    query_rows = 8 * slot_count
    turns = -(-all_fresh // query_rows) if groups == 1 else None
    packed_rows = seq_count * padded + query_rows + padded
    all_keys = text + seq_count * tokens
    result = pl.pallas_call(
        lambda *refs: attend_kernel(
            tokens, per_group, query_rows, 768, turns, steps, *refs
        ),
        out_shape=jax.ShapeDtypeStruct((seq_count, padded, head_size), jnp.bfloat16),
        grid_spec=pltpu.PrefetchScalarGridSpec(
            num_scalar_prefetch=1,
            grid=(1,),
            in_specs=[whole((rows, head_size))] * seq_count
            + [whole((text, head_size))] * 2,
            out_specs=whole((seq_count, padded, head_size)),
            scratch_shapes=[
                pltpu.VMEM((packed_rows, head_size), jnp.float32),
                pltpu.VMEM((all_keys, head_size), jnp.bfloat16),
                pltpu.VMEM((all_keys, head_size), jnp.bfloat16),
                pltpu.VMEM((packed_rows, head_size), jnp.float32),
            ],
        ),
        compiler_params=pltpu.CompilerParams(vmem_limit_bytes=40 * 2**20),
        name="attend",
    )(me, *arrived, text_keys, text_values)

    returned = lax.all_to_all(result, "seq", split_axis=0, concat_axis=0, tiled=True)

    finish_steps = 1
    return pl.pallas_call(
        lambda *refs: finish_kernel(per_group, *refs),
        out_shape=jax.ShapeDtypeStruct((tokens, row_width), attn_cache.dtype),
        grid=(finish_steps,),
        in_specs=[
            pl.BlockSpec((groups, padded), lambda i: (0, 0)),
            pl.BlockSpec((seq_count // finish_steps, padded, head_size), lambda i: (i, 0, 0)),
            pl.BlockSpec((tokens, row_width // finish_steps), lambda i: (0, i)),
        ],
        out_specs=pl.BlockSpec((tokens, row_width // finish_steps), lambda i: (0, i)),
        compiler_params=pltpu.CompilerParams(vmem_limit_bytes=32 * 2**20),
        name="finish",
    )(padded_slots, returned, attn_cache)


def solution(mesh):
    return jax.shard_map(
        shards,
        mesh=mesh,
        in_specs=(
            P(("parts", "seq"), None, None),
            P(("parts", "seq")),
            P(("parts", "seq"), None),
            P(("parts", "seq"), None),
            P(("parts", "seq"), None),
            P("parts", None),
            P("parts", None),
            P(),
            P(),
        ),
        out_specs=P(("parts", "seq"), None),
        check_vma=False,
    )
```
